256 devices in a mesh: group: 8 (over z), dev: 32 (over y, x, core).
Axes of the slice: x: 4, y: 4, z: 8, core: 2. Of those that a mesh axis runs over, the one named last changes fastest.
Arguments:
- features: bfloat16 [524288, 256], P(('group', 'dev')), may hold values from -6 to 6
- weight_self: bfloat16 [256, 256], replicated, may hold values from -0.375 to 0.375
- weight_neigh: bfloat16 [256, 256], replicated, may hold values from -0.375 to 0.375
- bias: float32 [256], replicated, may hold values from -3 to 3
- cotangent: bfloat16 [524288, 256], P(('group', 'dev')), may hold values from -6 to 6
- hub_rows: int32 [2048], P(('group', 'dev')), may hold values from 0 to 2047, as said below
- halo_send: int32 [8, 32, 32, 128], P('group', 'dev'), may hold values from 0 to 2048, as said below
- block_src: int32 [8, 32, 128], P('group', 'dev'), may hold values from 0 to 63
- block_tgt: int32 [8, 32, 128], P('group', 'dev'), may hold values from 0 to 15
- block_count: int32 [8, 32], P('group', 'dev'), may hold values from 32 to 128, as said below
- block_vals: bfloat16 [8, 32, 128, 128, 128], P('group', 'dev'), may hold values from 0 to 0.071777344
Outputs:
- output: bfloat16 [524288, 256], P(('group', 'dev'))
- grad_features: bfloat16 [524288, 256], P(('group', 'dev'))
- grad_self: float32 [256, 256], replicated
- grad_neigh: float32 [256, 256], replicated
- grad_bias: float32 [256], replicated
The draws below stay inside these ranges and needn't reach their ends.
Inputs may be any that keep to these rules, and one draw needn't show every extreme that they name: `hub_rows`: the 8 hub rows of one device are distinct. `halo_send`: 2048 marks an empty slot; the rows in one list are distinct and fill its first slots; a device's list to itself is empty. `block_count`: some device has all 128 slots live.
All inputs are finite; a program needn't handle non-finite values.
Results may differ from the reference program's by a relative error of at most 0.0075.
Values may be sent and summed in bfloat16 or wider, within the bound.
A program may use at most 128 MiB of HBM per device.

```python
import math
import jax
import jax.numpy as jnp
from jax import lax

FEAT = 256
ROWS = 2048
BLK = 128
HUB_DEV = 8
TGT_BLOCKS = 16
CAPACITY = 128
HUBS = 2048
SRC_BLOCKS = 64
NODES = 524288
N_GROUP = 8
N_DEV = 32


def first_hubs(single_key):
    return jax.random.permutation(single_key, ROWS)[:HUB_DEV]


def first_rows(single_key):
    return jax.random.permutation(single_key, ROWS)[:BLK]


def draw_hub_rows(key, part):
    key = jax.random.fold_in(key, 11)
    keys = jax.random.split(key, N_GROUP * N_DEV)
    picks = jax.vmap(first_hubs)(keys)
    return picks.reshape(-1).astype(jnp.int32)


def draw_halo_send(key, part):
    key = jax.random.fold_in(key, 12)
    lists = N_GROUP * N_DEV * N_DEV
    perm_key, fill_key, forced_key = jax.random.split(key, 3)
    rows = jax.vmap(first_rows)(jax.random.split(perm_key, lists)).astype(jnp.int32)
    filled = jax.random.randint(fill_key, (lists,), BLK // 4, BLK + 1)
    forced = jax.random.randint(forced_key, (), 0, lists)
    flat = jnp.arange(lists)
    filled = jnp.where(flat == forced, BLK // 4, filled)
    sender = flat // N_DEV % N_DEV
    receiver = flat % N_DEV
    filled = jnp.where(sender == receiver, 0, filled)
    slots = jnp.arange(BLK)
    rows = jnp.where(slots[None, :] < filled[:, None], rows, ROWS)
    return rows.reshape(N_GROUP, N_DEV, N_DEV, BLK).astype(jnp.int32)


def draw_block_count(key, part):
    key = jax.random.fold_in(key, 13)
    base_key, heavy_key, high_key, forced_key = jax.random.split(key, 4)
    total = N_GROUP * N_DEV
    base = jax.random.randint(base_key, (total,), 2 * TGT_BLOCKS, 4 * TGT_BLOCKS)
    heavy = jax.random.randint(heavy_key, (total,), 0, 8) == 0
    high = jax.random.randint(high_key, (total,), 4 * TGT_BLOCKS, CAPACITY + 1)
    counts = jnp.where(heavy, high, base)
    forced = jax.random.randint(forced_key, (), 0, total)
    counts = jnp.where(jnp.arange(total) == forced, CAPACITY, counts)
    return counts.reshape(N_GROUP, N_DEV).astype(jnp.int32)


def with_ends(array, stream_key, smallest, top_value):
    longest = array.shape.index(max(array.shape))
    spots = []
    for shift in (0, 1):
        where = [jax.random.randint(jax.random.fold_in(stream_key, axis), (), 0, length) for axis, length in enumerate(array.shape)]
        where[longest] = (where[longest] + shift) % array.shape[longest]
        spots.append(tuple(where))
    return array.at[spots[0]].set(smallest).at[spots[1]].set(top_value)


def steps_of(rng, extent, cuts, least, top_value):
    loudness, own = 1.0, jax.random.fold_in(rng, 6)
    for axis_at, parts in cuts:
        draws = jnp.exp(jax.random.uniform(jax.random.fold_in(own, axis_at), (parts,), jnp.float32, least / len(cuts), top_value / len(cuts)))
        loudness = loudness * jnp.repeat(draws, extent[axis_at] // parts).reshape([-1 if axis == axis_at else 1 for axis in range(len(extent))])
    return loudness


def scatter_about(own_key, shape, width, limit, shards=(), kind=jnp.bfloat16):
    values = jax.random.normal(own_key, shape, jnp.float32) * width
    if len(shards) > 0:
        values = steps_of(own_key, shape, shards, -0.22, 0.18) * values
    return jnp.clip(values, min=-limit, max=limit).astype(kind)


def setup_inputs(seed: int = 0) -> dict:
    streams_of = jax.random.split(jax.random.key(seed), 12)
    return {
        "features": scatter_about(streams_of[0], (NODES, FEAT), 1.0, 6.0, ((0, 256),)),
        "weight_self": scatter_about(streams_of[1], (FEAT, FEAT), FEAT ** -0.5, 0.375),
        "weight_neigh": scatter_about(streams_of[2], (FEAT, FEAT), FEAT ** -0.5, 0.375),
        "bias": scatter_about(streams_of[3], (FEAT,), 0.5, 3.0, (), jnp.float32),
        "cotangent": scatter_about(streams_of[4], (NODES, FEAT), 1.0, 6.0, ((0, 256),)),
        "hub_rows": draw_hub_rows(jax.random.fold_in(streams_of[11], 71), 0),
        "halo_send": draw_halo_send(jax.random.fold_in(streams_of[11], 71), 0),
        "block_src": with_ends(jax.random.randint(streams_of[7], (N_GROUP, N_DEV, CAPACITY), 0, SRC_BLOCKS), jax.random.fold_in(streams_of[7], 1), 0, SRC_BLOCKS - 1).astype(jnp.int32),
        "block_tgt": with_ends(jax.random.randint(streams_of[8], (N_GROUP, N_DEV, CAPACITY), 0, TGT_BLOCKS), jax.random.fold_in(streams_of[8], 1), 0, TGT_BLOCKS - 1).astype(jnp.int32),
        "block_count": draw_block_count(jax.random.fold_in(streams_of[11], 71), 0),
        "block_vals": jnp.clip(0.071777344 * jax.random.uniform(streams_of[10], (N_GROUP, N_DEV, CAPACITY, BLK, BLK), jnp.float32) ** steps_of(streams_of[10], (N_GROUP, N_DEV, CAPACITY, BLK, BLK), ((0, 8), (1, 32)), -0.2, 0.2), 0.0, 0.071777344).astype(jnp.bfloat16),
    }


def silu_parts(pre):
    sigmoid = jax.nn.sigmoid(pre)
    return (pre * sigmoid, sigmoid * (1.0 + pre * (1.0 - sigmoid)))

def reference(features, weight_self, weight_neigh, bias, cotangent, hub_rows, halo_send, block_src, block_tgt, block_count, block_vals):
    devices_all = N_GROUP * N_DEV
    feat_dev = features.reshape(devices_all, ROWS, FEAT)
    padded = jnp.concatenate([feat_dev, jnp.zeros((devices_all, 1, FEAT), jnp.bfloat16)], axis=1)
    hub_owner = (jnp.arange(HUBS) // HUB_DEV).astype(jnp.int32)
    hub_table = padded[hub_owner, hub_rows]
    send_lists = halo_send.reshape(devices_all, N_DEV, BLK)
    counts = block_count.reshape(devices_all)
    sources = block_src.reshape(devices_all, CAPACITY)
    targets = block_tgt.reshape(devices_all, CAPACITY)
    values = block_vals.reshape(devices_all, CAPACITY, BLK, BLK)
    cot_dev = cotangent.reshape(devices_all, ROWS, FEAT)
    scale = 1.0 / math.sqrt(NODES)
    slots = jnp.arange(CAPACITY).astype(jnp.int32)
    peer_ids = jnp.arange(N_DEV).astype(jnp.int32)
    contract = (((0,), (0,)), ((), ()))
    contract_last = (((1,), (1,)), ((), ()))

    def one_device(carry, index):
        group_idx = index // N_DEV
        dev_idx = index % N_DEV
        peers = group_idx * N_DEV + peer_ids
        rows = send_lists[peers, dev_idx]
        halo = padded[peers[:, None], rows]
        own = feat_dev[index]
        table = jnp.concatenate([own, halo.reshape(N_DEV * BLK, FEAT), hub_table], axis=0)
        tiles = table.reshape(SRC_BLOCKS, BLK, FEAT)
        live = slots < counts[index]
        masked = jnp.where(live[:, None, None], values[index], jnp.zeros((), jnp.bfloat16)).astype(jnp.float32)
        picked = tiles[sources[index]].astype(jnp.float32)
        products = jnp.einsum('kij,kjf->kif', masked, picked)
        aggregated = jax.ops.segment_sum(products, targets[index], TGT_BLOCKS).reshape(ROWS, FEAT).astype(jnp.bfloat16)
        pre = jnp.dot(own, weight_self, preferred_element_type=jnp.float32) + jnp.dot(aggregated, weight_neigh, preferred_element_type=jnp.float32) + bias
        output, slope = silu_parts(pre)
        dpre = (cot_dev[index].astype(jnp.float32) * slope).astype(jnp.bfloat16)
        grad_self = lax.dot_general(own, dpre, contract, preferred_element_type=jnp.float32)
        grad_neigh = lax.dot_general(aggregated, dpre, contract, preferred_element_type=jnp.float32)
        grad_bias = lax.optimization_barrier(jnp.sum(dpre.astype(jnp.float32), axis=0))
        dagg = lax.dot_general(dpre, weight_neigh, contract_last, preferred_element_type=jnp.float32).astype(jnp.bfloat16)
        dagg_tiles = dagg.reshape(TGT_BLOCKS, BLK, FEAT)[targets[index]].astype(jnp.float32)
        back = jnp.einsum('kji,kjf->kif', masked, dagg_tiles)
        dtable = jax.ops.segment_sum(back, sources[index], SRC_BLOCKS).reshape(SRC_BLOCKS * BLK, FEAT)
        local = lax.dot_general(dpre, weight_self, contract_last, preferred_element_type=jnp.float32) + dtable[:ROWS]
        halo_back = dtable[ROWS:ROWS + N_DEV * BLK].astype(jnp.bfloat16).reshape(N_DEV, BLK, FEAT)
        hub_back = dtable[ROWS + N_DEV * BLK:]
        carry = (carry[0] + grad_self, carry[1] + grad_neigh, carry[2] + grad_bias, carry[3] + hub_back)
        return (carry, (output.astype(jnp.bfloat16), local, halo_back))
    start = (jnp.zeros((FEAT, FEAT), jnp.float32), jnp.zeros((FEAT, FEAT), jnp.float32), jnp.zeros((FEAT,), jnp.float32), jnp.zeros((HUBS, FEAT), jnp.float32))
    device_ids = jnp.arange(devices_all).astype(jnp.int32)
    carry, (outputs, local_grads, halo_backs) = lax.scan(one_device, start, device_ids)
    owner_idx = (device_ids // N_DEV)[:, None] * N_DEV + peer_ids[None, :]
    rows_back = send_lists[owner_idx, (device_ids % N_DEV)[:, None]]
    grads = jnp.concatenate([local_grads, jnp.zeros((devices_all, 1, FEAT), jnp.float32)], axis=1)
    grads = grads.at[owner_idx[:, :, None], rows_back].add(halo_backs.astype(jnp.float32))
    grads = grads.at[hub_owner, hub_rows].add(carry[3])
    grad_features = grads[:, :ROWS].reshape(NODES, FEAT).astype(jnp.bfloat16)
    return (outputs.reshape(NODES, FEAT), grad_features, carry[0] * scale, carry[1] * scale, carry[2] * scale)
```

```python
import functools
import math

import jax
import jax.numpy as jnp
from jax import lax
from jax.experimental import pallas as pl
from jax.experimental.pallas import tpu as pltpu
from jax.sharding import PartitionSpec as P

MESH = pl.DeviceIdType.MESH
LANES = 128
BF16 = jnp.bfloat16
F32 = jnp.float32
FIRST = (((0,), (0,)), ((), ()))
LAST = (((1,), (1,)), ((), ()))
MIB = 1 << 20


def partner(me, step):
    core = lax.rem(lax.rem(me, 2) + lax.rem(step, 2), 2)
    x = lax.rem(lax.div(me, 2) + lax.div(step, 2), 4)
    y = lax.div(me, 8) + lax.div(step, 8)
    return x * 2 + core, y


def peer_of(me, step, count):
    low, y = partner(me, step)
    return lax.rem(y, count // 8) * 8 + low


def greet(me, group, devs, groups):
    barrier = pltpu.get_barrier_semaphore()

    def plane(step, _):
        pl.semaphore_signal(
            barrier, inc=1, device_id={"dev": peer_of(me, step, devs)}, device_id_type=MESH
        )
        return _

    def column(step, _):
        pl.semaphore_signal(
            barrier, inc=1, device_id={"group": lax.rem(group + step, groups)}, device_id_type=MESH
        )
        return _

    lax.fori_loop(1, devs, plane, 0)
    lax.fori_loop(1, groups, column, 0)
    return barrier


def to_plane(src, dst, send, recv, peer):
    return pltpu.make_async_remote_copy(
        src_ref=src, dst_ref=dst, send_sem=send, recv_sem=recv,
        device_id={"dev": peer}, device_id_type=MESH,
    )


def to_column(src, dst, send, recv, peer):
    return pltpu.make_async_remote_copy(
        src_ref=src, dst_ref=dst, send_sem=send, recv_sem=recv,
        device_id={"group": peer}, device_id_type=MESH,
    )


def gather_kernel(
    groups, devs,
    feat, lists, hub_idx,
    halo, hubs,
    out_buf, hub_out, hub_in, hub_own,
    sends, recvs, hub_sends, hub_recvs, z_sends, z_recvs, c_sends, c_recvs, local_sem,
):
    group = lax.axis_index("group")
    me = lax.axis_index("dev")
    rows, width = feat.shape
    slots = lists.shape[1]
    share = hub_out.shape[0]
    plane_hubs = share * devs
    half = plane_hubs // 2
    core = lax.rem(me, 2)
    mate = me + 1 - 2 * core
    barrier = greet(me, group, devs, groups)

    lane = lax.broadcasted_iota(jnp.int32, (slots, LANES), 1)

    def onehot(column, ids):
        return jnp.concatenate(
            [
                jnp.where(column == ids + LANES * r, 1.0, 0.0).astype(BF16)
                for r in range(rows // LANES)
            ],
            axis=1,
        )

    picked = jnp.dot(
        onehot(hub_idx[...], lane[: hub_idx.shape[0]]), feat[...], preferred_element_type=F32
    )[:share]
    hub_out[...] = picked
    hub_in[pl.ds(pl.multiple_of(me * share, share), share), :] = picked

    def fill(chunk):
        parts = []
        for j in range(4):
            row = lists[pl.ds(peer_of(me, chunk * 4 + j, devs), 1), :]
            column = jnp.broadcast_to(row, (slots, slots)).T
            parts.append(onehot(column, lane))
        got = jnp.dot(jnp.concatenate(parts, axis=0), feat[...], preferred_element_type=F32)
        out_buf[pl.ds(chunk * 4, 4)] = got.astype(BF16).reshape(4, slots, width)

    fill(0)
    pl.semaphore_wait(barrier, devs + groups - 2)

    def hub_copy(step):
        peer = peer_of(me, step, devs)
        place = pl.ds(pl.multiple_of(me * share, share), share)
        return to_plane(hub_out, hub_in.at[place], hub_sends.at[step], hub_recvs.at[me], peer)

    def halo_copy(step):
        peer = peer_of(me, step, devs)
        return to_plane(out_buf.at[step], halo.at[me], sends.at[step], recvs.at[me], peer)

    def each(low, high, action):
        def body(step, _):
            action(step)
            return _
        lax.fori_loop(low, high, body, 0)

    each(1, devs, lambda step: hub_copy(step).start())
    own = pltpu.make_async_copy(out_buf.at[0], halo.at[me], local_sem.at[0])
    own.start()
    each(1, 4, lambda step: halo_copy(step).start())

    def later(chunk):
        fill(chunk)
        each(chunk * 4, chunk * 4 + 4, lambda step: halo_copy(step).start())

    each(1, devs // 4, later)

    def hub_arrived(step):
        peer = peer_of(me, step, devs)
        place = pl.ds(pl.multiple_of(peer * share, share), share)
        to_plane(hub_out, hub_in.at[place], hub_sends.at[step], hub_recvs.at[peer], peer).wait_recv()

    each(1, devs, hub_arrived)
    hub_own[...] = hub_in[...].astype(BF16)
    mine = pltpu.make_async_copy(
        hub_own, hubs.at[pl.ds(pl.multiple_of(group * plane_hubs, plane_hubs), plane_hubs)], local_sem.at[1]
    )
    mine.start()

    def half_of(which, side):
        return pl.ds(pl.multiple_of(which * plane_hubs + side * half, half), half)

    def z_copy(step):
        part = hub_own.at[pl.ds(pl.multiple_of(core * half, half), half)]
        return to_column(
            part, hubs.at[half_of(group, core)], z_sends.at[step], z_recvs.at[group],
            lax.rem(group + step, groups),
        )

    each(1, groups, lambda step: z_copy(step).start())

    def z_arrived(step):
        source = lax.rem(group + groups - step, groups)
        part = hubs.at[half_of(source, core)]
        to_column(part, part, z_sends.at[step], z_recvs.at[source], source).wait_recv()
        to_plane(part, part, c_sends.at[source], c_recvs.at[source], mate).start()

    each(1, groups, z_arrived)

    def c_done(step):
        source = lax.rem(group + groups - step, groups)
        out = hubs.at[half_of(source, core)]
        into = hubs.at[half_of(source, 1 - core)]
        to_plane(out, out, c_sends.at[source], c_recvs.at[source], mate).wait_send()
        to_plane(into, into, c_sends.at[source], c_recvs.at[source], mate).wait_recv()

    each(1, groups, c_done)
    each(1, groups, lambda step: z_copy(step).wait_send())
    each(1, devs, lambda step: hub_copy(step).wait_send())

    def halo_done(step):
        peer = peer_of(me, step, devs)
        to_plane(out_buf.at[step], halo.at[peer], sends.at[step], recvs.at[peer], peer).wait()

    each(1, devs, halo_done)
    own.wait()
    mine.wait()


def gather_call(features, lists, hub_idx, groups, devs, share):
    rows, width = features.shape
    slots = lists.shape[1]
    hubs = groups * devs * share
    dma = pltpu.SemaphoreType.DMA
    return pl.pallas_call(
        functools.partial(gather_kernel, groups, devs),
        out_shape=(
            jax.ShapeDtypeStruct((devs, slots, width), BF16),
            jax.ShapeDtypeStruct((hubs, width), BF16),
        ),
        in_specs=[pl.BlockSpec(memory_space=pltpu.VMEM)] * 3,
        out_specs=[pl.BlockSpec(memory_space=pl.ANY)] * 2,
        scratch_shapes=[
            pltpu.VMEM((devs, slots, width), BF16),
            pltpu.VMEM((share, width), F32),
            pltpu.VMEM((devs * share, width), F32),
            pltpu.VMEM((devs * share, width), BF16),
            dma((devs,)), dma((devs,)), dma((devs,)), dma((devs,)),
            dma((groups,)), dma((groups,)), dma((groups,)), dma((groups,)), dma((2,)),
        ],
        compiler_params=pltpu.CompilerParams(
            collective_id=0, has_side_effects=True, vmem_limit_bytes=24 * MIB
        ),
        name="halo_gather",
    )(features, lists, hub_idx)


UNROLL = 4


def layer_kernel(
    src, tgt, count,
    feat, halo, hubs, vals, ws, wn, bias, cot,
    output, halo_back, hub_back, own_back, dpre_ref, wsend,
    table, agg, aggb, dagg, dtab, gself, gneigh, gbias, sems,
):
    blocks, block, width = table.shape
    capacity = vals.shape[0]
    own_blocks = feat.shape[0] // block
    halo_blocks = halo.shape[0]
    copies = [
        pltpu.make_async_copy(halo, table.at[pl.ds(own_blocks, halo_blocks)], sems.at[0]),
        pltpu.make_async_copy(
            hubs, table.at[pl.ds(own_blocks + halo_blocks, blocks - own_blocks - halo_blocks)], sems.at[1]
        ),
    ]
    for copy in copies:
        copy.start()
    agg[...] = jnp.zeros_like(agg)
    dtab[...] = jnp.zeros_like(dtab)
    gself[...] = jnp.zeros_like(gself)
    gneigh[...] = jnp.zeros_like(gneigh)
    gbias[...] = jnp.zeros_like(gbias)
    table[pl.ds(0, own_blocks)] = feat[...].reshape(own_blocks, block, width)
    for copy in copies:
        copy.wait()
    live = count[0]
    steps = lax.div(live + UNROLL - 1, UNROLL)

    def value(k):
        return jnp.where(k < live, vals[k], jnp.zeros((), BF16))

    def forward(step, _):
        for u in range(UNROLL):
            k = step * UNROLL + u
            agg[tgt[k]] += jnp.dot(value(k), table[src[k]], preferred_element_type=F32)
        return _

    lax.fori_loop(0, steps, forward, 0)

    def dense(t, _):
        at = pl.ds(pl.multiple_of(t * 2 * block, 2 * block), 2 * block)
        own = feat[at, :]
        two = pl.ds(t * 2, 2)
        near = agg[two].reshape(2 * block, width).astype(BF16)
        aggb[at, :] = near
        pre = (
            jnp.dot(own, ws[...], preferred_element_type=F32)
            + jnp.dot(near, wn[...], preferred_element_type=F32)
            + bias[...]
        )
        sigmoid = jax.nn.sigmoid(pre)
        output[at, :] = (pre * sigmoid).astype(BF16)
        slope = sigmoid * (1.0 + pre * (1.0 - sigmoid))
        dpre = (cot[at, :].astype(F32) * slope).astype(BF16)
        dpre_ref[at, :] = dpre
        dagg[two] = (
            lax.dot_general(dpre, wn[...], LAST, preferred_element_type=F32)
            .astype(BF16)
            .reshape(2, block, width)
        )
        gself[...] += lax.dot_general(own, dpre, FIRST, preferred_element_type=F32)
        gneigh[...] += lax.dot_general(near, dpre, FIRST, preferred_element_type=F32)
        gbias[...] += jnp.sum(dpre.astype(F32), axis=0, keepdims=True)
        return _

    lax.fori_loop(0, own_blocks // 2, dense, 0)

    def backward(step, _):
        for u in range(UNROLL):
            k = step * UNROLL + u
            dtab[src[k]] += lax.dot_general(
                value(k), dagg[tgt[k]], FIRST, preferred_element_type=F32
            )
        return _

    lax.fori_loop(0, steps, backward, 0)

    own_back[...] = dtab[pl.ds(0, own_blocks)].reshape(own_blocks * block, width)

    def rounded(p, _):
        halo_back[p] = dtab[own_blocks + p].astype(BF16)
        return _

    lax.fori_loop(0, halo_blocks, rounded, 0)

    hub_blocks = blocks - own_blocks - halo_blocks
    hub_back[...] = (
        dtab[pl.ds(own_blocks + halo_blocks, hub_blocks)].astype(BF16).reshape(hub_back.shape)
    )
    parts = wsend.shape[0]
    rows = 2 * width // parts
    wsend[pl.ds(0, parts // 2), :, pl.ds(0, width)] = gself[...].astype(BF16).reshape(
        parts // 2, rows, width
    )
    wsend[pl.ds(parts // 2, parts // 2), :, pl.ds(0, width)] = gneigh[...].astype(BF16).reshape(
        parts // 2, rows, width
    )
    line = lax.broadcasted_iota(jnp.int32, (rows, LANES), 0)
    low, high = gbias[:, :LANES], gbias[:, LANES:]
    both = jnp.where(line == 0, low, jnp.where(line == 1, high, 0.0))
    wsend[:, :, pl.ds(width, LANES)] = jnp.broadcast_to(
        both.astype(BF16)[None], (parts, rows, LANES)
    )


def layer_call(src, tgt, count, features, halo, hubs, values, ws, wn, bias, cot, groups, devs):
    rows, width = features.shape
    block = values.shape[1]
    own_blocks = rows // block
    blocks = own_blocks + devs + hubs.shape[0] // block
    half = hubs.shape[0] // groups // 2
    vmem = pl.BlockSpec(memory_space=pltpu.VMEM)
    smem = pl.BlockSpec(memory_space=pltpu.SMEM)
    anywhere = pl.BlockSpec(memory_space=pl.ANY)
    return pl.pallas_call(
        layer_kernel,
        out_shape=(
            jax.ShapeDtypeStruct((rows, width), BF16),
            jax.ShapeDtypeStruct((devs, block, width), BF16),
            jax.ShapeDtypeStruct((groups, 2, half, width), BF16),
            jax.ShapeDtypeStruct((rows, width), F32),
            jax.ShapeDtypeStruct((rows, width), BF16),
            jax.ShapeDtypeStruct((devs, 2 * width // devs, width + LANES), BF16),
        ),
        in_specs=[smem] * 3 + [vmem, anywhere, anywhere] + [vmem] * 5,
        out_specs=[vmem] * 6,
        scratch_shapes=[
            pltpu.VMEM((blocks, block, width), BF16),
            pltpu.VMEM((own_blocks, block, width), F32),
            pltpu.VMEM((rows, width), BF16),
            pltpu.VMEM((own_blocks, block, width), BF16),
            pltpu.VMEM((blocks, block, width), F32),
            pltpu.VMEM((width, width), F32),
            pltpu.VMEM((width, width), F32),
            pltpu.VMEM((1, width), F32),
            pltpu.SemaphoreType.DMA((2,)),
        ],
        compiler_params=pltpu.CompilerParams(vmem_limit_bytes=48 * MIB),
        name="layer",
    )(src, tgt, count, features, halo, hubs.reshape(-1, block, width), values, ws, wn, bias, cot)


def return_kernel(
    groups, devs,
    lists, hub_idx, halo_back, hub_back, own_back, dpre, ws, wsend,
    grad, wout, bias_out,
    acc, halo_in, pair_in, z_out, z_in, row_out, row_in, w_in, wz_in, wfin,
    h_send, h_recv, p_sem, z_send, z_recv, r_send, r_recv,
    w_send, w_recv, y_send, y_recv, f_send, f_recv,
):
    group = lax.axis_index("group")
    me = lax.axis_index("dev")
    rows, width = grad.shape
    slots = lists.shape[1]
    core = lax.rem(me, 2)
    mate = me + 1 - 2 * core
    share = row_out.shape[1]
    owners = row_out.shape[0]
    barrier = greet(me, group, devs, groups)

    def each(low, high, action):
        def body(step, _):
            action(step)
            return _
        lax.fori_loop(low, high, body, 0)

    def w_copy(step):
        peer = peer_of(me, step, devs)
        return to_plane(wsend.at[peer], w_in.at[me], w_send.at[step], w_recv.at[me], peer)

    def halo_copy(step):
        peer = peer_of(me, step, devs)
        return to_plane(halo_back.at[peer], halo_in.at[me], h_send.at[step], h_recv.at[me], peer)

    pair = to_plane(hub_back.at[:, 1 - core], pair_in, p_sem.at[0], p_sem.at[1], mate)

    pl.semaphore_wait(barrier, devs + groups - 2)
    pair.start()
    each(1, devs, lambda step: w_copy(step).start())
    each(1, devs, lambda step: halo_copy(step).start())

    w_in[me] = wsend[me]
    halo_in[me] = jnp.zeros((slots, width), BF16)

    def begin(t):
        at = pl.ds(pl.multiple_of(t * 256, 256), 256)
        acc[at, :] = (
            lax.dot_general(dpre[at, :], ws[...], LAST, preferred_element_type=F32) + own_back[at, :]
        )

    each(0, rows // 256, begin)

    pair.wait_recv()
    z_out[...] = (hub_back[:, core].astype(F32) + pair_in[...].astype(F32)).astype(BF16)

    def z_copy(step):
        peer = lax.rem(group + step, groups)
        return to_column(z_out.at[peer], z_in.at[group], z_send.at[step], z_recv.at[group], peer)

    each(1, groups, lambda step: z_copy(step).start())
    z_in[group] = z_out[group]

    def w_arrived(step):
        peer = peer_of(me, step, devs)
        to_plane(wsend.at[peer], w_in.at[peer], w_send.at[step], w_recv.at[peer], peer).wait_recv()

    each(1, devs, w_arrived)
    wz_in[group] = jnp.sum(w_in[...].astype(F32), axis=0).astype(BF16)

    def y_copy(step):
        peer = lax.rem(group + step, groups)
        return to_column(wz_in.at[group], wz_in.at[group], y_send.at[step], y_recv.at[group], peer)

    each(1, groups, lambda step: y_copy(step).start())

    def scatter(chunk):
        wide = 4 * slots
        ids = []
        got = []
        for j in range(4):
            step = chunk * 4 + j
            peer = peer_of(me, step, devs)

            @pl.when(step > 0)
            def _():
                to_plane(
                    halo_back.at[peer], halo_in.at[peer], h_send.at[step], h_recv.at[peer], peer
                ).wait_recv()

            ids.append(lists[pl.ds(peer, 1), :])
            got.append(halo_in[peer])
        ids = jnp.concatenate(ids, axis=1)
        got = jnp.concatenate(got, axis=0)
        for t in range(rows // 256):
            node = lax.broadcasted_iota(jnp.int32, (256, wide), 0) + t * 256
            pick = jnp.where(node == ids, 1.0, 0.0).astype(BF16)
            acc[pl.ds(t * 256, 256), :] += jnp.dot(pick, got, preferred_element_type=F32)

    def y_arrived(step):
        peer = lax.rem(group + step, groups)
        to_column(
            wz_in.at[peer], wz_in.at[peer], y_send.at[step], y_recv.at[peer], peer
        ).wait_recv()

    each(1, groups, y_arrived)
    total = jnp.sum(wz_in[...].astype(F32), axis=0)
    wfin[me] = total[:, :width].astype(BF16)
    bias_out[...] = total[:8, width:]

    def f_copy(step):
        peer = peer_of(me, step, devs)
        return to_plane(wfin.at[me], wfin.at[me], f_send.at[step], f_recv.at[me], peer)

    each(1, devs, lambda step: f_copy(step).start())

    def z_arrived(step):
        peer = lax.rem(group + step, groups)
        to_column(z_out.at[peer], z_in.at[peer], z_send.at[step], z_recv.at[peer], peer).wait_recv()

    each(1, groups, z_arrived)
    row_out[...] = jnp.sum(z_in[...].astype(F32), axis=0).reshape(owners, share, width)

    chip = lax.div(me, 2)

    def row_copy(k):
        owner = core * owners + k
        return to_plane(row_out.at[k], row_in.at[chip], r_send.at[k], r_recv.at[chip], owner)

    def row_start(k):
        owner = core * owners + k

        @pl.when(owner != me)
        def _():
            row_copy(k).start()

        @pl.when(owner == me)
        def _():
            row_in[chip] = row_out[k]

    each(0, owners, row_start)

    each(0, devs // 4, scatter)

    side = lax.div(me, owners)

    def row_arrived(k):
        sender = k * 2 + side

        @pl.when(sender != me)
        def _():
            to_plane(row_out.at[k], row_in.at[k], r_send.at[k], r_recv.at[k], sender).wait_recv()

    each(0, owners, row_arrived)
    total = jnp.sum(row_in[...], axis=0)
    top = total.astype(BF16)
    rest = (total - top.astype(F32)).astype(BF16)
    both = jnp.concatenate([top.astype(F32), rest.astype(F32)], axis=0).astype(BF16)
    for t in range(rows // 256):
        node = lax.broadcasted_iota(jnp.int32, (256, 2 * share), 0) + t * 256
        pick = jnp.where(node == hub_idx[...], 1.0, 0.0).astype(BF16)
        at = pl.ds(t * 256, 256)
        grad[at, :] = (
            acc[at, :] + jnp.dot(pick, both, preferred_element_type=F32)
        ).astype(BF16)

    def f_arrived(step):
        peer = peer_of(me, step, devs)
        to_plane(wfin.at[peer], wfin.at[peer], f_send.at[step], f_recv.at[peer], peer).wait_recv()

    each(1, devs, f_arrived)
    wout[...] = wfin[...]

    def sent(step):
        w_copy(step).wait_send()
        halo_copy(step).wait_send()
        f_copy(step).wait_send()

    each(1, devs, sent)

    def column_sent(step):
        z_copy(step).wait_send()
        y_copy(step).wait_send()

    each(1, groups, column_sent)

    def row_sent(k):
        @pl.when(core * owners + k != me)
        def _():
            row_copy(k).wait_send()

    each(0, owners, row_sent)
    pair.wait_send()


def return_call(lists, hub_idx, halo_back, hub_back, own_back, dpre, ws, wsend, groups, devs, share):
    rows, width = dpre.shape
    slots = lists.shape[1]
    half = hub_back.shape[2]
    owners = half // share
    wrows = wsend.shape[1]
    dma = pltpu.SemaphoreType.DMA
    vmem = pl.BlockSpec(memory_space=pltpu.VMEM)
    anywhere = pl.BlockSpec(memory_space=pl.ANY)
    return pl.pallas_call(
        functools.partial(return_kernel, groups, devs),
        out_shape=(
            jax.ShapeDtypeStruct((rows, width), BF16),
            jax.ShapeDtypeStruct((devs, wrows, width), BF16),
            jax.ShapeDtypeStruct((8, LANES), F32),
        ),
        in_specs=[vmem, vmem, anywhere, vmem, vmem, vmem, vmem, vmem],
        out_specs=[vmem] * 3,
        scratch_shapes=[
            pltpu.VMEM((rows, width), F32),
            pltpu.VMEM((devs, slots, width), BF16),
            pltpu.VMEM((groups, half, width), BF16),
            pltpu.VMEM((groups, half, width), BF16),
            pltpu.VMEM((groups, half, width), BF16),
            pltpu.VMEM((owners, share, width), F32),
            pltpu.VMEM((devs // 2, share, width), F32),
            pltpu.VMEM((devs, wrows, width + LANES), BF16),
            pltpu.VMEM((groups, wrows, width + LANES), BF16),
            pltpu.VMEM((devs, wrows, width), BF16),
            dma((devs,)), dma((devs,)), dma((2,)), dma((groups,)), dma((groups,)),
            dma((owners,)), dma((devs // 2,)),
            dma((devs,)), dma((devs,)), dma((groups,)), dma((groups,)), dma((devs,)), dma((devs,)),
        ],
        compiler_params=pltpu.CompilerParams(
            collective_id=1, has_side_effects=True, vmem_limit_bytes=40 * MIB
        ),
        name="halo_return",
    )(lists, hub_idx, halo_back, hub_back, own_back, dpre, ws, wsend)


def shards(groups, devs, features, weight_self, weight_neigh, bias, cotangent, hub_rows,
           halo_send, block_src, block_tgt, block_count, block_vals):
    rows, width = features.shape
    scale = 1.0 / math.sqrt(rows * groups * devs)
    share = hub_rows.shape[0]
    lists = halo_send[0, 0]
    doubled = jnp.concatenate([hub_rows, hub_rows])
    columns = jnp.broadcast_to(doubled[:, None], (2 * share, LANES))
    halo, hubs = gather_call(features, lists, columns, groups, devs, share)
    output, halo_back, hub_back, own_back, dpre, wsend = layer_call(
        block_src[0, 0], block_tgt[0, 0], block_count[0], features, halo, hubs, block_vals[0, 0],
        weight_self, weight_neigh, bias[None], cotangent, groups, devs,
    )
    grad, wout, bias_out = return_call(
        lists, doubled[None], halo_back, hub_back, own_back, dpre, weight_self, wsend,
        groups, devs, share,
    )
    wgrad = wout.reshape(2, width, width).astype(F32) * scale
    return output, grad, wgrad[0], wgrad[1], bias_out[:2].reshape(width) * scale


def solution(mesh):
    groups, devs = mesh.shape["group"], mesh.shape["dev"]
    return jax.shard_map(
        functools.partial(shards, groups, devs),
        mesh=mesh,
        in_specs=(
            P(("group", "dev"), None),
            P(),
            P(),
            P(),
            P(("group", "dev"), None),
            P(("group", "dev")),
            P("group", "dev", None, None),
            P("group", "dev", None),
            P("group", "dev", None),
            P("group", "dev"),
            P("group", "dev", None, None, None),
        ),
        out_specs=(P(("group", "dev"), None), P(("group", "dev"), None), P(), P(), P()),
        check_vma=False,
    )
```

```python
import functools
import math
import random

import jax
import jax.numpy as jnp
from jax import lax
from jax.experimental import pallas as pl
from jax.experimental.pallas import tpu as pltpu
from jax.sharding import PartitionSpec as P

MESH = pl.DeviceIdType.MESH
LANES = 128
BF16 = jnp.bfloat16
F32 = jnp.float32
I32 = jnp.int32
FIRST = (((0,), (0,)), ((), ()))
LAST = (((1,), (1,)), ((), ()))
MIB = 1 << 20
PART = 4
UNROLL = 8
ROWS_OF_PLAN = 8


def send_order(devs):
    ys = devs // 8
    every = [(y, x, c) for y in range(ys) for x in range(4) for c in range(2)][1:]
    draw = random.Random(5)
    draw.shuffle(every)
    other = [(-y % ys, -x % 4, c) for y, x, c in every]
    return every, other


class Place:
    def __init__(self, me, devs):
        self.me = me
        self.ys = devs // 8
        self.y = lax.div(me, 8)
        self.x = lax.rem(lax.div(me, 2), 4)
        self.core = lax.rem(me, 2)
        self.mate = me + 1 - 2 * self.core
        self.chip = lax.div(me, 2)
        self.plans = send_order(devs)

    def at(self, offset, sign):
        y, x, c = offset
        y, x = (y, x) if sign > 0 else (self.ys - y, 4 - x)
        return (
            lax.rem(self.y + y, self.ys) * 8
            + lax.rem(self.x + x, 4) * 2
            + lax.rem(self.core + c, 2)
        )

    def target(self, n):
        first, second = self.plans
        return jnp.where(self.core == 0, self.at(first[n], 1), self.at(second[n], 1))

    def source(self, n):
        first, second = self.plans
        sender = lax.rem(self.core + first[n][2], 2)
        return jnp.where(sender == 0, self.at(first[n], -1), self.at(second[n], -1))

    def across(self, n):
        chips = 4 * self.ys
        return lax.rem(self.chip + n, chips) * 2 + self.core


def column_of(row, size):
    return jnp.broadcast_to(row, (size, size)).T


def slot_plan(key, other, count, limit):
    size = key.shape[1]
    down = lax.broadcasted_iota(I32, (size, size), 0)
    along = lax.broadcasted_iota(I32, (size, size), 1)
    live = down < count
    keys = column_of(key, size)
    others = column_of(other, size)

    def total(mask, value=1):
        return jnp.sum(jnp.where(mask, value, 0), axis=0, keepdims=True)

    earlier = (keys == key) & (down < along)
    rank = total(earlier & live)
    odd = rank & 1
    ranks = column_of(rank, size)
    odds = ranks & 1
    heads = live & (odds == 0)
    pair = total(heads & ((keys < key) | earlier)) - odd
    pairs = column_of(pair, size)
    match = live & (pairs == along)
    left = match & (odds == 0)
    right = match & (odds == 1)
    has_right = total(right)
    place = along[:1]
    return [
        total(left, down),
        total(right, down) + (1 - has_right) * size,
        total(left, others),
        total(right, others),
        place * (1 - total(match & (ranks == 0))),
        total(heads & (keys <= along)) * jnp.minimum(total(live & (keys == along)), 1),
    ]


def layer_kernel(
    groups, devs,
    meta_hbm, lists_hbm, feat_hbm, vals_hbm, ws_hbm, wn_hbm, bias_hbm, cot_hbm,
    output, grad, wout, bias_out,
    meta, lists, vals, turned, ws, wn, bias, cot,
    table, runs, own_pre, aggb, dpre_ref, dagg, acc,
    halo_out, halo_in, hub_row, hub_pair, hub_send, hub_plane,
    pair_out, pair_in, z_out, z_in, row_out, row_in, wsend, w_in, wz_in, wfin,
    plan_v, plan_s,
    local, h_send, h_recv, m_sem, a_send, a_recv, z_send, z_recv, c_send, c_recv,
    g_send, g_recv, p_sem, s_send, s_recv, r_send, r_recv,
    w_send, w_recv, y_send, y_recv, f_send, f_recv,
):
    group = lax.axis_index("group")
    me = lax.axis_index("dev")
    here = Place(me, devs)
    core, mate, chip = here.core, here.mate, here.chip
    blocks, block, width = table.shape
    own_blocks = feat_hbm.shape[0]
    rows = own_blocks * block
    hub_start = own_blocks + devs
    capacity = vals_hbm.shape[0]
    share = hub_row.shape[0]
    chips = devs // 2
    messages = devs - 1

    def fetch(src, dst, which):
        copy = pltpu.make_async_copy(src, dst, local.at[which])
        copy.start()
        return copy

    early = [
        fetch(feat_hbm, table.at[pl.ds(0, own_blocks)], 0),
        fetch(lists_hbm, lists, 1),
        fetch(meta_hbm, meta, 2),
    ]

    def to_plane(src, dst, send, recv, peer):
        return pltpu.make_async_remote_copy(
            src_ref=src, dst_ref=dst, send_sem=send, recv_sem=recv,
            device_id={"dev": peer}, device_id_type=MESH,
        )

    def to_column(src, dst, send, recv, peer):
        return pltpu.make_async_remote_copy(
            src_ref=src, dst_ref=dst, send_sem=send, recv_sem=recv,
            device_id={"group": peer}, device_id_type=MESH,
        )

    def above(step):
        return lax.rem(group + step, groups)

    barrier = pltpu.get_barrier_semaphore()
    for n in range(messages):
        pl.semaphore_signal(
            barrier, inc=1, device_id={"dev": here.target(n)}, device_id_type=MESH
        )
    for step in range(1, groups):
        pl.semaphore_signal(
            barrier, inc=1, device_id={"group": above(step)}, device_id_type=MESH
        )
    late = [
        fetch(vals_hbm, vals.at[pl.ds(0, capacity)], 3),
        fetch(ws_hbm, ws, 4),
        fetch(wn_hbm, wn, 5),
        fetch(bias_hbm, bias, 6),
        fetch(cot_hbm, cot, 7),
    ]
    for copy in early:
        copy.wait()

    lane = lax.broadcasted_iota(I32, (block, LANES), 1)
    owned = pl.ds(0, own_blocks)

    def onehot(column, ids):
        return jnp.concatenate(
            [
                jnp.where(column == ids + LANES * r, 1.0, 0.0).astype(BF16)
                for r in range(rows // LANES)
            ],
            axis=1,
        )

    def pick(matrix):
        return jnp.dot(matrix, table[owned].reshape(rows, width), preferred_element_type=F32)

    hubs_row = meta[pl.ds(3, 1), :]
    picked = pick(onehot(column_of(hubs_row, block)[: 2 * share], lane[: 2 * share]))[:share]
    hub_row[...] = picked
    hub_pair[core] = picked

    def fill(low, high):
        parts = [
            onehot(column_of(lists[pl.ds(here.target(n), 1), :], block), lane)
            for n in range(low, high)
        ]
        got = pick(jnp.concatenate(parts, axis=0)).astype(BF16)
        halo_out[pl.ds(low, high - low)] = got.reshape(high - low, block, width)

    def halo_copy(n):
        return to_plane(
            halo_out.at[n], table.at[own_blocks + me], h_send.at[n], h_recv.at[me], here.target(n)
        )

    def from_plane(dst, send, recv, peer):
        return to_plane(dst, dst, send, recv, peer)

    spans = [(low, min(low + PART, messages)) for low in range(0, messages, PART)]

    def ship(span):
        for n in range(*span):
            halo_copy(n).start()

    hub_mate = to_plane(hub_row, hub_pair.at[core], m_sem.at[0], m_sem.at[1], mate)

    def hub_spread(n):
        return to_plane(
            hub_send, hub_plane.at[chip], a_send.at[n], a_recv.at[chip], here.across(n)
        )

    def hub_block(owner, side):
        return table.at[hub_start + owner * 2 + side]

    half_chips = chips // 2

    def hub_up(step):
        return to_column(
            hub_plane.at[pl.ds(core * half_chips, half_chips)],
            hub_in_table(group, core),
            z_send.at[step], z_recv.at[group], above(step),
        )

    def hub_in_table(owner, side):
        return hub_table.at[pl.ds((owner * 2 + side) * half_chips, half_chips)]

    hub_table = table.at[pl.ds(hub_start, blocks - hub_start)].reshape(
        (blocks - hub_start) * half_chips, 2 * share, width
    )

    fill(*spans[0])
    pl.semaphore_wait(barrier, devs + groups - 2)
    hub_mate.start()
    ship(spans[0])
    fill(*spans[1])
    ship(spans[1])

    hub_mate.wait_recv()
    both = hub_pair[...].reshape(2 * share, width).astype(BF16)
    hub_send[...] = both
    hub_plane[chip] = both
    for n in range(1, chips):
        hub_spread(n).start()

    for span in spans[2:4]:
        fill(*span)
        ship(span)

    for n in range(1, chips):
        source = lax.div(here.across(n), 2)
        from_plane(hub_plane.at[source], a_send.at[n], a_recv.at[source], mate).wait_recv()
    for step in range(1, groups):
        hub_up(step).start()
    hub_table[pl.ds(group * chips, chips)] = hub_plane[...]

    for span in spans[4:]:
        fill(*span)
        ship(span)

    count = meta[pl.ds(2, 1), :]
    src = meta[pl.ds(0, 1), :]
    tgt = meta[pl.ds(1, 1), :]
    ahead = slot_plan(tgt, src, count, own_blocks)
    back = slot_plan(src, tgt, count, blocks)
    for at, row in enumerate(ahead):
        plan_v[pl.ds(at, 1), :] = row
    for at, row in enumerate(back):
        plan_v[pl.ds(ROWS_OF_PLAN + at, 1), :] = row
    plan_copy = fetch(plan_v, plan_s, 8)
    table[own_blocks + me] = jnp.zeros((block, width), BF16)
    vals[capacity] = jnp.zeros((block, block), BF16)
    turned[capacity] = jnp.zeros((block, block), BF16)
    runs[0] = jnp.zeros((block, width), F32)
    for copy in late:
        copy.wait()

    def turn(step, _):
        for u in range(UNROLL):
            k = step * UNROLL + u
            turned[k] = vals[k].T
        return _

    lax.fori_loop(0, capacity // UNROLL, turn, 0)

    def span_of(t):
        return pl.ds(pl.multiple_of(t * 2 * block, 2 * block), 2 * block)

    def own_part(t, _):
        own = table[pl.ds(t * 2, 2)].reshape(2 * block, width)
        own_pre[span_of(t), :] = (
            jnp.dot(own, ws[...], preferred_element_type=F32) + bias[...]
        )
        return _

    lax.fori_loop(0, own_blocks // 2, own_part, 0)
    plan_copy.wait()

    def pass_on(step):
        owner = lax.rem(group + groups - step, groups)
        part = hub_in_table(owner, core)
        to_column(part, part, z_send.at[step], z_recv.at[owner], owner).wait_recv()
        to_plane(part, part, c_send.at[owner], c_recv.at[owner], mate).start()

    for step in range(1, groups):
        pass_on(step)

    for step in range(1, groups):
        owner = lax.rem(group + groups - step, groups)
        sent, got = hub_in_table(owner, core), hub_in_table(owner, 1 - core)
        to_plane(sent, sent, c_send.at[owner], c_recv.at[owner], mate).wait_send()
        to_plane(got, got, c_send.at[owner], c_recv.at[owner], mate).wait_recv()
    for n in range(messages):
        source = here.source(n)
        from_plane(
            table.at[own_blocks + source], h_send.at[n], h_recv.at[source], source
        ).wait_recv()

    def forward(step, _):
        for u in range(UNROLL):
            p = step * UNROLL + u
            left = jnp.concatenate([vals[plan_s[0, p]], vals[plan_s[1, p]]], axis=1)
            right = jnp.concatenate([table[plan_s[2, p]], table[plan_s[3, p]]], axis=0)
            runs[p + 1] = runs[plan_s[4, p]] + jnp.dot(left, right, preferred_element_type=F32)
        return _

    lax.fori_loop(0, pl.cdiv(capacity + own_blocks, 2 * UNROLL), forward, 0)

    def dense(t, _):
        at = span_of(t)
        near = jnp.concatenate(
            [runs[plan_s[5, t * 2]], runs[plan_s[5, t * 2 + 1]]], axis=0
        ).astype(BF16)
        aggb[at, :] = near
        pre = own_pre[at, :] + jnp.dot(near, wn[...], preferred_element_type=F32)
        sigmoid = jax.nn.sigmoid(pre)
        output[at, :] = (pre * sigmoid).astype(BF16)
        slope = sigmoid * (1.0 + pre * (1.0 - sigmoid))
        dpre = (cot[at, :].astype(F32) * slope).astype(BF16)
        dpre_ref[at, :] = dpre
        dagg[pl.ds(t * 2, 2)] = (
            lax.dot_general(dpre, wn[...], LAST, preferred_element_type=F32)
            .astype(BF16)
            .reshape(2, block, width)
        )
        return _

    lax.fori_loop(0, own_blocks // 2, dense, 0)

    part_rows = wsend.shape[1]
    dpre_all = dpre_ref[...]
    gself = lax.dot_general(
        table[owned].reshape(rows, width), dpre_all, FIRST, preferred_element_type=F32
    )
    gneigh = lax.dot_general(aggb[...], dpre_all, FIRST, preferred_element_type=F32)
    gbias = jnp.sum(dpre_all.astype(F32), axis=0, keepdims=True)
    half = devs // 2
    wide = pl.ds(0, width)
    wsend[pl.ds(0, half), :, wide] = gself.astype(BF16).reshape(half, part_rows, width)
    wsend[pl.ds(half, half), :, wide] = gneigh.astype(BF16).reshape(half, part_rows, width)
    line = lax.broadcasted_iota(I32, (part_rows, LANES), 0)
    sums = jnp.where(line == 0, gbias[:, :LANES], jnp.where(line == 1, gbias[:, LANES:], 0.0))
    wsend[:, :, pl.ds(width, LANES)] = jnp.broadcast_to(
        sums.astype(BF16)[None], (devs, part_rows, LANES)
    )

    def w_copy(n):
        peer = here.target(n)
        return to_plane(wsend.at[peer], w_in.at[me], w_send.at[n], w_recv.at[me], peer)

    for n in range(messages):
        w_copy(n).start()
    w_in[me] = wsend[me]
    for n in range(messages):
        halo_copy(n).wait_send()

    def backward(step, _):
        for u in range(UNROLL):
            p = step * UNROLL + u
            left = jnp.concatenate(
                [turned[plan_s[ROWS_OF_PLAN, p]], turned[plan_s[ROWS_OF_PLAN + 1, p]]], axis=1
            )
            right = jnp.concatenate(
                [dagg[plan_s[ROWS_OF_PLAN + 2, p]], dagg[plan_s[ROWS_OF_PLAN + 3, p]]], axis=0
            )
            runs[p + 1] = runs[plan_s[ROWS_OF_PLAN + 4, p]] + jnp.dot(
                left, right, preferred_element_type=F32
            )
        return _

    lax.fori_loop(0, pl.cdiv(capacity + blocks, 2 * UNROLL), backward, 0)

    def dtable(b):
        return runs[plan_s[ROWS_OF_PLAN + 5, b]]

    def back_copy(n):
        return to_plane(halo_out.at[n], halo_in.at[me], g_send.at[n], g_recv.at[me], here.target(n))

    for n in range(messages):
        halo_out[n] = dtable(own_blocks + here.target(n)).astype(BF16)
        back_copy(n).start()
    for k in range(groups):
        pair_out[k] = dtable(hub_start + 2 * k + 1 - core).astype(BF16)
    pair = to_plane(pair_out, pair_in, p_sem.at[0], p_sem.at[1], mate)
    pair.start()

    for n in range(messages):
        source = here.source(n)
        from_plane(w_in.at[source], w_send.at[n], w_recv.at[source], source).wait_recv()
    wz_in[group] = jnp.sum(w_in[...].astype(F32), axis=0).astype(BF16)

    def y_copy(step):
        return to_column(
            wz_in.at[group], wz_in.at[group], y_send.at[step], y_recv.at[group], above(step)
        )

    for step in range(1, groups):
        y_copy(step).start()

    pair.wait_recv()
    for k in range(groups):
        z_out[k] = (dtable(hub_start + 2 * k + core) + pair_in[k].astype(F32)).astype(BF16)

    def s_copy(step):
        return to_column(
            z_out.at[above(step)], z_in.at[group], s_send.at[step], s_recv.at[group], above(step)
        )

    for step in range(1, groups):
        s_copy(step).start()
    z_in[group] = z_out[group]

    def begin(t, _):
        at = span_of(t)
        own = jnp.concatenate([dtable(t * 2), dtable(t * 2 + 1)], axis=0)
        acc[at, :] = own + lax.dot_general(
            dpre_ref[at, :], ws[...], LAST, preferred_element_type=F32
        )
        return _

    lax.fori_loop(0, own_blocks // 2, begin, 0)

    for step in range(1, groups):
        peer = above(step)
        to_column(
            wz_in.at[peer], wz_in.at[peer], y_send.at[step], y_recv.at[peer], peer
        ).wait_recv()
    total = jnp.sum(wz_in[...].astype(F32), axis=0)
    wfin[me] = total[:, :width].astype(BF16)
    bias_out[...] = total[:8, width:]

    def f_copy(n):
        return to_plane(
            wfin.at[me], wfin.at[me], f_send.at[n], f_recv.at[me], here.target(n)
        )

    for n in range(messages):
        f_copy(n).start()

    def scatter(span):
        ids, got = [], []
        for n in range(*span):
            source = here.source(n)
            from_plane(halo_in.at[source], g_send.at[n], g_recv.at[source], source).wait_recv()
            ids.append(lists[pl.ds(source, 1), :])
            got.append(halo_in[source])
        ids = jnp.concatenate(ids, axis=1)
        got = jnp.concatenate(got, axis=0)

        def add(t, _):
            node = lax.broadcasted_iota(I32, (2 * block, ids.shape[1]), 0) + t * (2 * block)
            chosen = jnp.where(node == ids, 1.0, 0.0).astype(BF16)
            acc[span_of(t), :] += jnp.dot(chosen, got, preferred_element_type=F32)
            return _

        lax.fori_loop(0, own_blocks // 2, add, 0)

    for span in spans[:3]:
        scatter(span)

    for step in range(1, groups):
        peer = above(step)
        to_column(
            z_out.at[peer], z_in.at[peer], s_send.at[step], s_recv.at[peer], peer
        ).wait_recv()
    row_out[...] = jnp.sum(z_in[...].astype(F32), axis=0).reshape(row_out.shape)

    def row_copy(k):
        return to_plane(
            row_out.at[k], row_in.at[chip], r_send.at[k], r_recv.at[chip], core * chips + k
        )

    for k in range(chips):
        @pl.when(core * chips + k != me)
        def _():
            row_copy(k).start()

        @pl.when(core * chips + k == me)
        def _():
            row_in[chip] = row_out[k]

    for span in spans[3:]:
        scatter(span)

    side = lax.div(me, chips)
    for k in range(chips):
        sender = k * 2 + side

        @pl.when(sender != me)
        def _():
            to_plane(row_out.at[k], row_in.at[k], r_send.at[k], r_recv.at[k], sender).wait_recv()

    hub_sum = jnp.sum(row_in[...], axis=0)
    top = hub_sum.astype(BF16).astype(F32)
    both = jnp.concatenate([top, hub_sum - top], axis=0).astype(BF16)
    hub_ids = meta[pl.ds(3, 1), :][:, : 2 * share]

    def finish(t, _):
        at = span_of(t)
        node = lax.broadcasted_iota(I32, (2 * block, 2 * share), 0) + t * (2 * block)
        chosen = jnp.where(node == hub_ids, 1.0, 0.0).astype(BF16)
        grad[at, :] = (
            acc[at, :] + jnp.dot(chosen, both, preferred_element_type=F32)
        ).astype(BF16)
        return _

    lax.fori_loop(0, own_blocks // 2, finish, 0)

    for n in range(messages):
        source = here.source(n)
        from_plane(wfin.at[source], f_send.at[n], f_recv.at[source], source).wait_recv()
    wout[...] = wfin[...]

    hub_mate.wait_send()
    pair.wait_send()
    for n in range(1, chips):
        hub_spread(n).wait_send()
    for step in range(1, groups):
        hub_up(step).wait_send()
        y_copy(step).wait_send()
        s_copy(step).wait_send()
    for n in range(messages):
        w_copy(n).wait_send()
        back_copy(n).wait_send()
        f_copy(n).wait_send()
    for k in range(chips):
        @pl.when(core * chips + k != me)
        def _():
            row_copy(k).wait_send()


def layer_call(meta, lists, features, values, ws, wn, bias, cot, groups, devs, share):
    own_blocks, block, width = features.shape
    rows = own_blocks * block
    capacity = values.shape[0]
    hubs = groups * devs * share
    blocks = own_blocks + devs + hubs // block
    chips = devs // 2
    part_rows = 2 * width // devs
    most = UNROLL * pl.cdiv(capacity + blocks, 2 * UNROLL)
    dma = pltpu.SemaphoreType.DMA
    vm = pltpu.VMEM
    anywhere = pl.BlockSpec(memory_space=pl.ANY)
    vmem = pl.BlockSpec(memory_space=pltpu.VMEM)
    return pl.pallas_call(
        functools.partial(layer_kernel, groups, devs),
        out_shape=(
            jax.ShapeDtypeStruct((rows, width), BF16),
            jax.ShapeDtypeStruct((rows, width), BF16),
            jax.ShapeDtypeStruct((devs, part_rows, width), BF16),
            jax.ShapeDtypeStruct((8, LANES), F32),
        ),
        in_specs=[anywhere] * 8,
        out_specs=[vmem] * 4,
        scratch_shapes=[
            vm(meta.shape, I32), vm(lists.shape, I32),
            vm((capacity + 1, block, block), BF16), vm((capacity + 1, block, block), BF16),
            vm((width, width), BF16), vm((width, width), BF16), vm((1, width), F32),
            vm((rows, width), BF16),
            vm((blocks, block, width), BF16), vm((most + 1, block, width), F32),
            vm((rows, width), F32), vm((rows, width), BF16), vm((rows, width), BF16),
            vm((own_blocks, block, width), BF16), vm((rows, width), F32),
            vm((devs, block, width), BF16), vm((devs, block, width), BF16),
            vm((share, width), F32), vm((2, share, width), F32),
            vm((2 * share, width), BF16), vm((chips, 2 * share, width), BF16),
            vm((groups, block, width), BF16), vm((groups, block, width), BF16),
            vm((groups, block, width), BF16), vm((groups, block, width), BF16),
            vm((chips, share, width), F32), vm((chips, share, width), F32),
            vm((devs, part_rows, width + LANES), BF16), vm((devs, part_rows, width + LANES), BF16),
            vm((groups, part_rows, width + LANES), BF16), vm((devs, part_rows, width), BF16),
            vm((2 * ROWS_OF_PLAN, LANES), I32), pltpu.SMEM((2 * ROWS_OF_PLAN, LANES), I32),
            dma((9,)), dma((devs,)), dma((devs,)), dma((2,)), dma((chips,)), dma((chips,)),
            dma((groups,)), dma((groups,)), dma((groups,)), dma((groups,)),
            dma((devs,)), dma((devs,)), dma((2,)), dma((groups,)), dma((groups,)),
            dma((chips,)), dma((chips,)),
            dma((devs,)), dma((devs,)), dma((groups,)), dma((groups,)), dma((devs,)), dma((devs,)),
        ],
        compiler_params=pltpu.CompilerParams(
            collective_id=0, has_side_effects=True, vmem_limit_bytes=56 * MIB
        ),
        name="layer",
    )(meta, lists, features, values, ws, wn, bias, cot)


def shards(groups, devs, features, weight_self, weight_neigh, bias, cotangent, hub_rows,
           halo_send, block_src, block_tgt, block_count, block_vals):
    rows, width = features.shape
    scale = 1.0 / math.sqrt(rows * groups * devs)
    share = hub_rows.shape[0]
    block = block_vals.shape[-1]
    unused = jnp.full((LANES - 2 * share,), -1, I32)
    meta = jnp.stack(
        [
            block_src[0, 0],
            block_tgt[0, 0],
            jnp.broadcast_to(block_count[0, 0], (LANES,)),
            jnp.concatenate([hub_rows, hub_rows, unused]),
        ]
    )
    meta = jnp.concatenate([meta, jnp.zeros((4, LANES), I32)])
    output, grad, wout, bias_out = layer_call(
        meta, halo_send[0, 0], features.reshape(-1, block, width), block_vals[0, 0],
        weight_self, weight_neigh, bias[None], cotangent, groups, devs, share,
    )
    wgrad = wout.reshape(2, width, width).astype(F32) * scale
    return output, grad, wgrad[0], wgrad[1], bias_out[:2].reshape(width) * scale


def solution(mesh):
    groups, devs = mesh.shape["group"], mesh.shape["dev"]
    return jax.shard_map(
        functools.partial(shards, groups, devs),
        mesh=mesh,
        in_specs=(
            P(("group", "dev"), None),
            P(),
            P(),
            P(),
            P(("group", "dev"), None),
            P(("group", "dev")),
            P("group", "dev", None, None),
            P("group", "dev", None),
            P("group", "dev", None),
            P("group", "dev"),
            P("group", "dev", None, None, None),
        ),
        out_specs=(P(("group", "dev"), None), P(("group", "dev"), None), P(), P(), P()),
        check_vma=False,
    )
```

```python
import functools
import math
import random

import jax
import jax.numpy as jnp
from jax import lax
from jax.experimental import pallas as pl
from jax.experimental.pallas import tpu as pltpu
from jax.sharding import PartitionSpec as P

MESH = pl.DeviceIdType.MESH
LANES = 128
BF16 = jnp.bfloat16
F32 = jnp.float32
I32 = jnp.int32
FIRST = (((0,), (0,)), ((), ()))
LAST = (((1,), (1,)), ((), ()))
MIB = 1 << 20
PART = 4
UNROLL = 8
ROWS_OF_PLAN = 8
TILE = 512
LOW = 256


def send_order(devs):
    ys = devs // 8
    every = [(y, x, c) for y in range(ys) for x in range(4) for c in range(2)][1:]
    draw = random.Random(5)
    draw.shuffle(every)
    other = [(-y % ys, -x % 4, c) for y, x, c in every]
    return every, other


class Place:
    def __init__(self, me, devs):
        self.me = me
        self.ys = devs // 8
        self.y = lax.div(me, 8)
        self.x = lax.rem(lax.div(me, 2), 4)
        self.core = lax.rem(me, 2)
        self.mate = me + 1 - 2 * self.core
        self.chip = lax.div(me, 2)
        self.plans = send_order(devs)

    def at(self, offset, sign):
        y, x, c = offset
        y, x = (y, x) if sign > 0 else (self.ys - y, 4 - x)
        return (
            lax.rem(self.y + y, self.ys) * 8
            + lax.rem(self.x + x, 4) * 2
            + lax.rem(self.core + c, 2)
        )

    def target(self, n):
        first, second = self.plans
        return jnp.where(self.core == 0, self.at(first[n], 1), self.at(second[n], 1))

    def source(self, n):
        first, second = self.plans
        sender = lax.rem(self.core + first[n][2], 2)
        return jnp.where(sender == 0, self.at(first[n], -1), self.at(second[n], -1))

    def across(self, n):
        chips = 4 * self.ys
        return lax.rem(self.chip + n, chips) * 2 + self.core


def column_of(row, size):
    return jnp.broadcast_to(row, (size, size)).T


def slot_plan(key, other, count, limit):
    size = key.shape[1]
    down = lax.broadcasted_iota(I32, (size, size), 0)
    along = lax.broadcasted_iota(I32, (size, size), 1)
    live = down < count
    keys = column_of(key, size)
    others = column_of(other, size)

    def total(mask, value=1):
        return jnp.sum(jnp.where(mask, value, 0), axis=0, keepdims=True)

    earlier = (keys == key) & (down < along)
    rank = total(earlier & live)
    odd = rank & 1
    ranks = column_of(rank, size)
    odds = ranks & 1
    heads = live & (odds == 0)
    pair = total(heads & ((keys < key) | earlier)) - odd
    pairs = column_of(pair, size)
    match = live & (pairs == along)
    left = match & (odds == 0)
    right = match & (odds == 1)
    has_right = total(right)
    place = along[:1]
    return [
        total(left, down),
        total(right, down) + (1 - has_right) * size,
        total(left, others),
        total(right, others),
        place * (1 - total(match & (ranks == 0))),
        total(heads & (keys <= along)) * jnp.minimum(total(live & (keys == along)), 1),
    ]


def layer_kernel(
    groups, devs,
    hub_rows, counts, src_hbm, tgt_hbm, lists_hbm, feat_hbm, vals_hbm, ws_hbm, wn_hbm, bias_hbm, cot_hbm,
    output_hbm, grad_hbm, wout, bias_out,
    src_v, tgt_v, output, grad, bias_sum, wide, lists, vals, turned, ws, wn, bias, cot,
    table, runs, own_pre, dpre_ref, dagg, acc,
    halo_out, halo_in, hub_row, hub_pair, hub_send, hub_plane,
    pair_out, pair_in, z_out, z_in, row_out, row_in, wsend, w_in, wz_in, wfin,
    plan_v, plan_s,
    local, h_send, h_recv, m_sem, a_send, a_recv, z_send, z_recv, c_send, c_recv,
    g_send, g_recv, p_sem, s_send, s_recv, r_send, r_recv,
    w_send, w_recv, y_send, y_recv, f_send, f_recv,
):
    group = lax.axis_index("group")
    me = lax.axis_index("dev")
    here = Place(me, devs)
    core, mate, chip = here.core, here.mate, here.chip
    blocks, block, width = table.shape
    own_blocks = feat_hbm.shape[0]
    rows = own_blocks * block
    hub_start = own_blocks + devs
    capacity = vals_hbm.shape[0]
    share = hub_row.shape[0]
    chips = devs // 2
    messages = devs - 1

    def fetch(src, dst, which):
        copy = pltpu.make_async_copy(src, dst, local.at[which])
        copy.start()
        return copy

    early = [
        fetch(feat_hbm, table.at[pl.ds(0, own_blocks)], 0),
        fetch(lists_hbm, lists, 1),
    ]

    def to_plane(src, dst, send, recv, peer):
        return pltpu.make_async_remote_copy(
            src_ref=src, dst_ref=dst, send_sem=send, recv_sem=recv,
            device_id={"dev": peer}, device_id_type=MESH,
        )

    def to_column(src, dst, send, recv, peer):
        return pltpu.make_async_remote_copy(
            src_ref=src, dst_ref=dst, send_sem=send, recv_sem=recv,
            device_id={"group": peer}, device_id_type=MESH,
        )

    def above(step):
        return lax.rem(group + step, groups)

    barrier = pltpu.get_barrier_semaphore()
    for n in range(messages):
        pl.semaphore_signal(
            barrier, inc=1, device_id={"dev": here.target(n)}, device_id_type=MESH
        )
    for step in range(1, groups):
        pl.semaphore_signal(
            barrier, inc=1, device_id={"group": above(step)}, device_id_type=MESH
        )
    late = [
        fetch(vals_hbm, vals.at[pl.ds(0, capacity)], 3),
        fetch(ws_hbm, ws, 4),
        fetch(wn_hbm, wn, 5),
        fetch(bias_hbm, bias, 6),
        fetch(cot_hbm, cot, 7),
        fetch(src_hbm, src_v, 2),
        fetch(tgt_hbm, tgt_v, 9),
    ]
    for copy in early:
        copy.wait()

    lane = lax.broadcasted_iota(I32, (block, LANES), 1)
    owned = pl.ds(0, own_blocks)

    def onehot(column):
        low = column & (LOW - 1)
        high = lax.shift_right_logical(column, 8).astype(F32).astype(BF16)
        high = jnp.concatenate([high] * (LOW // LANES), axis=1)
        ones = jnp.concatenate(
            [
                jnp.where(low == lane[: column.shape[0]] + LANES * r, 1.0, 0.0)
                for r in range(LOW // LANES)
            ],
            axis=1,
        ).astype(BF16)
        none = jnp.zeros_like(ones)
        return jnp.concatenate(
            [jnp.where(high == float(t), ones, none) for t in range(rows // LOW)], axis=1
        )

    def pick(matrix):
        return jnp.dot(matrix, table[owned].reshape(rows, width), preferred_element_type=F32)

    hub_ids = jnp.full((1, block), rows, I32)
    for k in range(share):
        hub_ids = jnp.where((lane[:1] == k) | (lane[:1] == k + share), hub_rows[k], hub_ids)
    picked = pick(onehot(column_of(hub_ids, block)[: 2 * share]))[:share]
    hub_row[...] = picked
    hub_pair[core] = picked

    def fill(low, high):
        parts = [
            onehot(column_of(lists[pl.ds(here.target(n), 1), :], block))
            for n in range(low, high)
        ]
        got = pick(jnp.concatenate(parts, axis=0)).astype(BF16)
        halo_out[pl.ds(low, high - low)] = got.reshape(high - low, block, width)

    def halo_copy(n):
        return to_plane(
            halo_out.at[n], table.at[own_blocks + me], h_send.at[n], h_recv.at[me], here.target(n)
        )

    def from_plane(dst, send, recv, peer):
        return to_plane(dst, dst, send, recv, peer)

    spans = [(low, min(low + PART, messages)) for low in range(0, messages, PART)]

    def ship(span):
        for n in range(*span):
            halo_copy(n).start()

    hub_mate = to_plane(hub_row, hub_pair.at[core], m_sem.at[0], m_sem.at[1], mate)

    def hub_spread(n):
        return to_plane(
            hub_send, hub_plane.at[chip], a_send.at[n], a_recv.at[chip], here.across(n)
        )

    def hub_block(owner, side):
        return table.at[hub_start + owner * 2 + side]

    half_chips = chips // 2

    def hub_up(step):
        return to_column(
            hub_plane.at[pl.ds(core * half_chips, half_chips)],
            hub_in_table(group, core),
            z_send.at[step], z_recv.at[group], above(step),
        )

    def hub_in_table(owner, side):
        return hub_table.at[pl.ds((owner * 2 + side) * half_chips, half_chips)]

    hub_table = table.at[pl.ds(hub_start, blocks - hub_start)].reshape(
        (blocks - hub_start) * half_chips, 2 * share, width
    )

    fill(*spans[0])
    pl.semaphore_wait(barrier, devs + groups - 2)
    hub_mate.start()
    ship(spans[0])
    fill(*spans[1])

    hub_mate.wait_recv()
    both = hub_pair[...].reshape(2 * share, width).astype(BF16)
    hub_send[...] = both
    hub_plane[chip] = both
    for n in range(1, chips):
        hub_spread(n).start()
    ship(spans[1])

    for span in spans[2:]:
        fill(*span)
        ship(span)

    for n in range(1, chips):
        source = lax.div(here.across(n), 2)
        from_plane(hub_plane.at[source], a_send.at[n], a_recv.at[source], mate).wait_recv()
    for step in range(1, groups):
        hub_up(step).start()
    hub_table[pl.ds(group * chips, chips)] = hub_plane[...]

    for copy in late:
        copy.wait()
    count = counts[0, 0]
    src = src_v[...]
    tgt = tgt_v[...]
    ahead = slot_plan(tgt, src, count, own_blocks)
    back = slot_plan(src, tgt, count, blocks)
    for at, row in enumerate(ahead):
        plan_v[pl.ds(at, 1), :] = row
    for at, row in enumerate(back):
        plan_v[pl.ds(ROWS_OF_PLAN + at, 1), :] = row
    plan_copy = fetch(plan_v, plan_s, 8)
    table[own_blocks + me] = jnp.zeros((block, width), BF16)
    vals[capacity] = jnp.zeros((block, block), BF16)
    turned[capacity] = jnp.zeros((block, block), BF16)
    runs[0] = jnp.zeros((block, width), F32)
    wide[pl.ds(2 * width, 16), :] = jnp.ones((16, rows), BF16)

    def turn(step, _):
        for u in range(UNROLL):
            k = step * UNROLL + u
            turned[k] = vals[k].T
        return _

    lax.fori_loop(0, capacity // UNROLL, turn, 0)

    def span_of(t):
        return pl.ds(pl.multiple_of(t * 2 * block, 2 * block), 2 * block)

    def own_part(t, _):
        own = table[pl.ds(t * 2, 2)].reshape(2 * block, width)
        own_pre[span_of(t), :] = (
            jnp.dot(own, ws[...], preferred_element_type=F32) + bias[...]
        )
        wide[pl.ds(0, width), span_of(t)] = own.T
        return _

    lax.fori_loop(0, own_blocks // 2, own_part, 0)
    plan_copy.wait()

    def pass_on(step):
        owner = lax.rem(group + groups - step, groups)
        part = hub_in_table(owner, core)
        to_column(part, part, z_send.at[step], z_recv.at[owner], owner).wait_recv()
        to_plane(part, part, c_send.at[owner], c_recv.at[owner], mate).start()

    for step in range(1, groups):
        pass_on(step)

    for step in range(1, groups):
        owner = lax.rem(group + groups - step, groups)
        sent, got = hub_in_table(owner, core), hub_in_table(owner, 1 - core)
        to_plane(sent, sent, c_send.at[owner], c_recv.at[owner], mate).wait_send()
        to_plane(got, got, c_send.at[owner], c_recv.at[owner], mate).wait_recv()
    for n in range(messages):
        source = here.source(n)
        from_plane(
            table.at[own_blocks + source], h_send.at[n], h_recv.at[source], source
        ).wait_recv()

    def forward(step, _):
        for u in range(UNROLL):
            p = step * UNROLL + u
            left = jnp.concatenate([vals[plan_s[0, p]], vals[plan_s[1, p]]], axis=1)
            right = jnp.concatenate([table[plan_s[2, p]], table[plan_s[3, p]]], axis=0)
            runs[p + 1] = runs[plan_s[4, p]] + jnp.dot(left, right, preferred_element_type=F32)
        return _

    lax.fori_loop(0, pl.cdiv(capacity + own_blocks, 2 * UNROLL), forward, 0)

    def dense_part(t):
        at = span_of(t)
        near = jnp.concatenate(
            [runs[plan_s[5, t * 2]], runs[plan_s[5, t * 2 + 1]]], axis=0
        ).astype(BF16)
        wide[pl.ds(width, width), at] = near.T
        pre = own_pre[at, :] + jnp.dot(near, wn[...], preferred_element_type=F32)
        sigmoid = 0.5 * jnp.tanh(0.5 * pre) + 0.5
        result = pre * sigmoid
        output[at, :] = result.astype(BF16)
        slope = sigmoid + result * (1.0 - sigmoid)
        dpre = (cot[at, :].astype(F32) * slope).astype(BF16)
        dpre_ref[at, :] = dpre
        dagg[pl.ds(t * 2, 2)] = (
            lax.dot_general(dpre, wn[...], LAST, preferred_element_type=F32)
            .astype(BF16)
            .reshape(2, block, width)
        )

    def dense(step, _):
        dense_part(step * 2)
        dense_part(step * 2 + 1)
        return _

    lax.fori_loop(0, own_blocks // 4, dense, 0)
    output_copy = fetch(output, output_hbm, 10)

    part_rows = wsend.shape[1]
    sums = jnp.dot(wide[...], dpre_ref[...], preferred_element_type=F32)
    wsend[:, :, pl.ds(0, width)] = (
        sums[: 2 * width].astype(BF16).reshape(devs, part_rows, width)
    )
    gbias = sums[2 * width : 2 * width + 1]
    line = lax.broadcasted_iota(I32, (part_rows, LANES), 0)
    sums = jnp.where(line == 0, gbias[:, :LANES], jnp.where(line == 1, gbias[:, LANES:], 0.0))
    wsend[:, :, pl.ds(width, LANES)] = jnp.broadcast_to(
        sums.astype(BF16)[None], (devs, part_rows, LANES)
    )

    def w_copy(n):
        peer = here.target(n)
        return to_plane(wsend.at[peer], w_in.at[me], w_send.at[n], w_recv.at[me], peer)

    for n in range(messages):
        w_copy(n).start()
    w_in[me] = wsend[me]
    for n in range(messages):
        halo_copy(n).wait_send()

    def backward(step, _):
        for u in range(UNROLL):
            p = step * UNROLL + u
            left = jnp.concatenate(
                [turned[plan_s[ROWS_OF_PLAN, p]], turned[plan_s[ROWS_OF_PLAN + 1, p]]], axis=1
            )
            right = jnp.concatenate(
                [dagg[plan_s[ROWS_OF_PLAN + 2, p]], dagg[plan_s[ROWS_OF_PLAN + 3, p]]], axis=0
            )
            runs[p + 1] = runs[plan_s[ROWS_OF_PLAN + 4, p]] + jnp.dot(
                left, right, preferred_element_type=F32
            )
        return _

    lax.fori_loop(0, pl.cdiv(capacity + blocks, 2 * UNROLL), backward, 0)

    def dtable(b):
        return runs[plan_s[ROWS_OF_PLAN + 5, b]]

    def back_copy(n):
        return to_plane(halo_out.at[n], halo_in.at[me], g_send.at[n], g_recv.at[me], here.target(n))

    for n in range(messages):
        halo_out[n] = dtable(own_blocks + here.target(n)).astype(BF16)
        back_copy(n).start()
    for k in range(groups):
        pair_out[k] = dtable(hub_start + 2 * k + 1 - core).astype(BF16)
    pair = to_plane(pair_out, pair_in, p_sem.at[0], p_sem.at[1], mate)
    pair.start()

    for n in range(messages):
        source = here.source(n)
        from_plane(w_in.at[source], w_send.at[n], w_recv.at[source], source).wait_recv()
    wz_in[group] = jnp.sum(w_in[...].astype(F32), axis=0).astype(BF16)

    def y_copy(step):
        return to_column(
            wz_in.at[group], wz_in.at[group], y_send.at[step], y_recv.at[group], above(step)
        )

    for step in range(1, groups):
        y_copy(step).start()

    pair.wait_recv()
    for k in range(groups):
        z_out[k] = (dtable(hub_start + 2 * k + core) + pair_in[k].astype(F32)).astype(BF16)

    def s_copy(step):
        return to_column(
            z_out.at[above(step)], z_in.at[group], s_send.at[step], s_recv.at[group], above(step)
        )

    for step in range(1, groups):
        s_copy(step).start()
    z_in[group] = z_out[group]

    def begin(t, _):
        at = span_of(t)
        own = jnp.concatenate([dtable(t * 2), dtable(t * 2 + 1)], axis=0)
        acc[at, :] = own + lax.dot_general(
            dpre_ref[at, :], ws[...], LAST, preferred_element_type=F32
        )
        return _

    lax.fori_loop(0, own_blocks // 2, begin, 0)

    for step in range(1, groups):
        peer = above(step)
        to_column(
            wz_in.at[peer], wz_in.at[peer], y_send.at[step], y_recv.at[peer], peer
        ).wait_recv()
    total = jnp.sum(wz_in[...].astype(F32), axis=0)
    wfin[me] = total[:, :width].astype(BF16)
    bias_sum[...] = total[:8, width:]
    bias_copy = fetch(bias_sum, bias_out, 11)

    def f_copy(n):
        return to_plane(
            wfin.at[me], wfin.at[me], f_send.at[n], f_recv.at[me], here.target(n)
        )

    for n in range(messages):
        f_copy(n).start()

    def scatter(span):
        ids, got = [], []
        for n in range(*span):
            source = here.source(n)
            from_plane(halo_in.at[source], g_send.at[n], g_recv.at[source], source).wait_recv()
            ids.append(lists[pl.ds(source, 1), :])
            got.append(halo_in[source])
        ids = jnp.concatenate(ids, axis=1)
        got = jnp.concatenate(got, axis=0)
        low = ids & (TILE - 1)
        node = lax.broadcasted_iota(I32, (TILE, ids.shape[1]), 0)
        ones = jnp.where(node == low, 1.0, 0.0).astype(BF16)
        for t in range(rows // TILE):
            here_too = jnp.where(ids - low == t * TILE, 1.0, 0.0).astype(BF16)
            acc[pl.ds(t * TILE, TILE), :] += jnp.dot(
                ones * here_too, got, preferred_element_type=F32
            )

    wider = [(low, min(low + 2 * PART, messages)) for low in range(0, messages, 2 * PART)]
    for span in wider[:2]:
        scatter(span)

    for step in range(1, groups):
        peer = above(step)
        to_column(
            z_out.at[peer], z_in.at[peer], s_send.at[step], s_recv.at[peer], peer
        ).wait_recv()
    row_out[...] = jnp.sum(z_in[...].astype(F32), axis=0).reshape(row_out.shape)

    def row_copy(k):
        return to_plane(
            row_out.at[k], row_in.at[chip], r_send.at[k], r_recv.at[chip], core * chips + k
        )

    for k in range(chips):
        @pl.when(core * chips + k != me)
        def _():
            row_copy(k).start()

        @pl.when(core * chips + k == me)
        def _():
            row_in[chip] = row_out[k]

    for span in wider[2:]:
        scatter(span)

    side = lax.div(me, chips)
    for k in range(chips):
        sender = k * 2 + side

        @pl.when(sender != me)
        def _():
            to_plane(row_out.at[k], row_in.at[k], r_send.at[k], r_recv.at[k], sender).wait_recv()

    hub_sum = jnp.sum(row_in[...], axis=0)
    top = hub_sum.astype(BF16).astype(F32)
    both = jnp.concatenate([top, hub_sum - top], axis=0).astype(BF16)
    hub_ids = hub_ids[:, : 2 * share]

    def result_copy(t):
        at = pl.ds(t * TILE, TILE)
        return pltpu.make_async_copy(grad.at[at], grad_hbm.at[at], local.at[13 + t])

    for t in range(rows // TILE):
        at = pl.ds(t * TILE, TILE)
        node = lax.broadcasted_iota(I32, (TILE, 2 * share), 0) + t * TILE
        chosen = jnp.where(node == hub_ids, 1.0, 0.0).astype(BF16)
        grad[at, :] = (
            acc[at, :] + jnp.dot(chosen, both, preferred_element_type=F32)
        ).astype(BF16)
        result_copy(t).start()

    for n in range(messages):
        source = here.source(n)
        from_plane(wfin.at[source], f_send.at[n], f_recv.at[source], source).wait_recv()
    wout_copy = fetch(wfin, wout, 12)

    hub_mate.wait_send()
    pair.wait_send()
    for n in range(1, chips):
        hub_spread(n).wait_send()
    for step in range(1, groups):
        hub_up(step).wait_send()
        y_copy(step).wait_send()
        s_copy(step).wait_send()
    for n in range(messages):
        w_copy(n).wait_send()
        back_copy(n).wait_send()
        f_copy(n).wait_send()
    for k in range(chips):
        @pl.when(core * chips + k != me)
        def _():
            row_copy(k).wait_send()

    for copy in (output_copy, bias_copy, wout_copy):
        copy.wait()
    for t in range(rows // TILE):
        result_copy(t).wait()


def layer_call(hub_rows, count, src, tgt, lists, features, values, ws, wn, bias, cot, groups, devs, share):
    own_blocks, block, width = features.shape
    rows = own_blocks * block
    capacity = values.shape[0]
    hubs = groups * devs * share
    blocks = own_blocks + devs + hubs // block
    chips = devs // 2
    part_rows = 2 * width // devs
    most = UNROLL * pl.cdiv(capacity + blocks, 2 * UNROLL)
    dma = pltpu.SemaphoreType.DMA
    vm = pltpu.VMEM
    anywhere = pl.BlockSpec(memory_space=pl.ANY)
    smem = pl.BlockSpec(memory_space=pltpu.SMEM)
    return pl.pallas_call(
        functools.partial(layer_kernel, groups, devs),
        out_shape=(
            jax.ShapeDtypeStruct((rows, width), BF16),
            jax.ShapeDtypeStruct((rows, width), BF16),
            jax.ShapeDtypeStruct((devs, part_rows, width), BF16),
            jax.ShapeDtypeStruct((8, LANES), F32),
        ),
        in_specs=[smem] * 2 + [anywhere] * 9,
        out_specs=[anywhere] * 4,
        scratch_shapes=[
            vm(src.shape, I32), vm(tgt.shape, I32), vm((rows, width), BF16), vm((rows, width), BF16),
            vm((8, LANES), F32), vm((2 * width + 16, rows), BF16), vm(lists.shape, I32),
            vm((capacity + 1, block, block), BF16), vm((capacity + 1, block, block), BF16),
            vm((width, width), BF16), vm((width, width), BF16), vm((1, width), F32),
            vm((rows, width), BF16),
            vm((blocks, block, width), BF16), vm((most + 1, block, width), F32),
            vm((rows, width), F32), vm((rows, width), BF16),
            vm((own_blocks, block, width), BF16), vm((rows, width), F32),
            vm((devs, block, width), BF16), vm((devs, block, width), BF16),
            vm((share, width), F32), vm((2, share, width), F32),
            vm((2 * share, width), BF16), vm((chips, 2 * share, width), BF16),
            vm((groups, block, width), BF16), vm((groups, block, width), BF16),
            vm((groups, block, width), BF16), vm((groups, block, width), BF16),
            vm((chips, share, width), F32), vm((chips, share, width), F32),
            vm((devs, part_rows, width + LANES), BF16), vm((devs, part_rows, width + LANES), BF16),
            vm((groups, part_rows, width + LANES), BF16), vm((devs, part_rows, width), BF16),
            vm((2 * ROWS_OF_PLAN, LANES), I32), pltpu.SMEM((2 * ROWS_OF_PLAN, LANES), I32),
            dma((13 + rows // TILE,)), dma((devs,)), dma((devs,)), dma((2,)), dma((chips,)), dma((chips,)),
            dma((groups,)), dma((groups,)), dma((groups,)), dma((groups,)),
            dma((devs,)), dma((devs,)), dma((2,)), dma((groups,)), dma((groups,)),
            dma((chips,)), dma((chips,)),
            dma((devs,)), dma((devs,)), dma((groups,)), dma((groups,)), dma((devs,)), dma((devs,)),
        ],
        compiler_params=pltpu.CompilerParams(
            collective_id=0, has_side_effects=True, vmem_limit_bytes=56 * MIB
        ),
        name="layer",
    )(hub_rows, count, src, tgt, lists, features, values, ws, wn, bias, cot)


def finish_kernel(
    scale, output_in, grad_in, weights_in, bias_in,
    output, grad, grad_self, grad_neigh, grad_bias,
    weights, sums, self_v, neigh_v, bias_v, sems,
):
    def move(src, dst, which):
        copy = pltpu.make_async_copy(src, dst, sems.at[which])
        copy.start()
        return copy

    first = [move(weights_in, weights, 0), move(bias_in, sums, 1)]
    moved = [move(output_in, output, 2), move(grad_in, grad, 3)]
    for copy in first:
        copy.wait()
    half = weights.shape[0] // 2
    self_v[...] = weights[pl.ds(0, half)].reshape(self_v.shape).astype(F32) * scale
    moved.append(move(self_v, grad_self, 0))
    neigh_v[...] = weights[pl.ds(half, half)].reshape(neigh_v.shape).astype(F32) * scale
    moved.append(move(neigh_v, grad_neigh, 1))
    bias_v[...] = jnp.concatenate([sums[pl.ds(0, 1), :], sums[pl.ds(1, 1), :]], axis=1) * scale
    moved.append(move(bias_v, grad_bias, 4))
    for copy in moved:
        copy.wait()


def finish_call(scale, output, grad, weights, bias):
    width = output.shape[1]
    vm = pltpu.VMEM
    anywhere = pl.BlockSpec(memory_space=pl.ANY)
    square = jax.ShapeDtypeStruct((width, width), F32)
    line = jax.ShapeDtypeStruct((1, width), F32)
    return pl.pallas_call(
        functools.partial(finish_kernel, scale),
        out_shape=(
            jax.ShapeDtypeStruct(output.shape, BF16), jax.ShapeDtypeStruct(grad.shape, BF16),
            square, square, line,
        ),
        in_specs=[anywhere] * 4,
        out_specs=[anywhere] * 5,
        scratch_shapes=[
            vm(weights.shape, BF16), vm(bias.shape, F32),
            vm((width, width), F32), vm((width, width), F32), vm((1, width), F32),
            pltpu.SemaphoreType.DMA((5,)),
        ],
        compiler_params=pltpu.CompilerParams(vmem_limit_bytes=63 * MIB),
        name="finish",
    )(output, grad, weights, bias)


def shards(groups, devs, features, weight_self, weight_neigh, bias, cotangent, hub_rows,
           halo_send, block_src, block_tgt, block_count, block_vals):
    rows, width = features.shape
    scale = 1.0 / math.sqrt(rows * groups * devs)
    block = block_vals.shape[-1]
    results = layer_call(
        hub_rows, block_count, block_src[0], block_tgt[0],
        halo_send[0, 0], features.reshape(-1, block, width), block_vals[0, 0],
        weight_self, weight_neigh, bias[None], cotangent, groups, devs, hub_rows.shape[0],
    )
    output, grad, grad_self, grad_neigh, grad_bias = finish_call(scale, *results)
    return output, grad, grad_self, grad_neigh, grad_bias.reshape(width)


def solution(mesh):
    groups, devs = mesh.shape["group"], mesh.shape["dev"]
    return jax.shard_map(
        functools.partial(shards, groups, devs),
        mesh=mesh,
        in_specs=(
            P(("group", "dev"), None),
            P(),
            P(),
            P(),
            P(("group", "dev"), None),
            P(("group", "dev")),
            P("group", "dev", None, None),
            P("group", "dev", None),
            P("group", "dev", None),
            P("group", "dev"),
            P("group", "dev", None, None, None),
        ),
        out_specs=(P(("group", "dev"), None), P(("group", "dev"), None), P(), P(), P()),
        check_vma=False,
    )
```

```python
import functools
import math
import random

import jax
import jax.numpy as jnp
from jax import lax
from jax.experimental import pallas as pl
from jax.experimental.pallas import tpu as pltpu
from jax.sharding import PartitionSpec as P

MESH = pl.DeviceIdType.MESH
LANES = 128
BF16 = jnp.bfloat16
F32 = jnp.float32
I32 = jnp.int32
FIRST = (((0,), (0,)), ((), ()))
LAST = (((1,), (1,)), ((), ()))
MIB = 1 << 20
PART = 4
UNROLL = 8
ROWS_OF_PLAN = 8
TILE = 512
LOW = 256


def send_order(devs):
    ys = devs // 8
    every = [(y, x, c) for y in range(ys) for x in range(4) for c in range(2)][1:]
    draw = random.Random(1)
    draw.shuffle(every)
    other = [(-y % ys, -x % 4, c) for y, x, c in every]
    return every, other


class Place:
    def __init__(self, me, devs):
        self.me = me
        self.ys = devs // 8
        self.y = lax.div(me, 8)
        self.x = lax.rem(lax.div(me, 2), 4)
        self.core = lax.rem(me, 2)
        self.mate = me + 1 - 2 * self.core
        self.chip = lax.div(me, 2)
        self.plans = send_order(devs)

    def at(self, offset, sign):
        y, x, c = offset
        y, x = (y, x) if sign > 0 else (self.ys - y, 4 - x)
        return (
            lax.rem(self.y + y, self.ys) * 8
            + lax.rem(self.x + x, 4) * 2
            + lax.rem(self.core + c, 2)
        )

    def target(self, n):
        first, second = self.plans
        return jnp.where(self.core == 0, self.at(first[n], 1), self.at(second[n], 1))

    def source(self, n):
        first, second = self.plans
        sender = lax.rem(self.core + first[n][2], 2)
        return jnp.where(sender == 0, self.at(first[n], -1), self.at(second[n], -1))

    def across(self, n):
        chips = 4 * self.ys
        return lax.rem(self.chip + n, chips) * 2 + self.core


def column_of(row, size):
    return jnp.broadcast_to(row, (size, size)).T


def slot_plan(key, other, count, limit):
    size = key.shape[1]
    down = lax.broadcasted_iota(I32, (size, size), 0)
    along = lax.broadcasted_iota(I32, (size, size), 1)
    live = down < count
    keys = column_of(key, size)
    others = column_of(other, size)

    def total(mask, value=1):
        return jnp.sum(jnp.where(mask, value, 0), axis=0, keepdims=True)

    earlier = (keys == key) & (down < along)
    rank = total(earlier & live)
    odd = rank & 1
    ranks = column_of(rank, size)
    odds = ranks & 1
    heads = live & (odds == 0)
    pair = total(heads & ((keys < key) | earlier)) - odd
    pairs = column_of(pair, size)
    match = live & (pairs == along)
    left = match & (odds == 0)
    right = match & (odds == 1)
    has_right = total(right)
    place = along[:1]
    return [
        total(left, down),
        total(right, down) + (1 - has_right) * size,
        total(left, others),
        total(right, others),
        place * (1 - total(match & (ranks == 0))),
        total(heads & (keys <= along)) * jnp.minimum(total(live & (keys == along)), 1),
    ]


def layer_kernel(
    groups, devs,
    hub_rows, counts, src_hbm, tgt_hbm, lists_hbm, feat_hbm, vals_hbm, ws_hbm, wn_hbm, bias_hbm, cot_hbm,
    output_hbm, grad_hbm, wout, bias_out,
    src_v, tgt_v, output, grad, wide, lists, vals, turned, ws, wn, bias, cot,
    table, runs, own_pre, dpre_ref, dagg, acc,
    halo_out, halo_in, hub_row, hub_pair, hub_send, hub_plane,
    pair_out, pair_in, z_out, z_in, row_out, row_in, wsend, wz_in, wmid, w_in, wplane, wall,
    plan_v, plan_s,
    local, h_send, h_recv, m_sem, a_send, a_recv, z_send, z_recv, c_send, c_recv,
    g_send, g_recv, p_sem, s_send, s_recv, r_send, r_recv,
    w_send, w_recv, y_send, y_recv, f_send, f_recv, u_send, u_recv,
):
    group = lax.axis_index("group")
    me = lax.axis_index("dev")
    here = Place(me, devs)
    core, mate, chip = here.core, here.mate, here.chip
    blocks, block, width = table.shape
    own_blocks = feat_hbm.shape[0]
    rows = own_blocks * block
    hub_start = own_blocks + devs
    capacity = vals_hbm.shape[0]
    share = hub_row.shape[0]
    chips = devs // 2
    messages = devs - 1

    def fetch(src, dst, which):
        copy = pltpu.make_async_copy(src, dst, local.at[which])
        copy.start()
        return copy

    early = [
        fetch(feat_hbm, table.at[pl.ds(0, own_blocks)], 0),
        fetch(lists_hbm, lists, 1),
    ]

    def to_plane(src, dst, send, recv, peer):
        return pltpu.make_async_remote_copy(
            src_ref=src, dst_ref=dst, send_sem=send, recv_sem=recv,
            device_id={"dev": peer}, device_id_type=MESH,
        )

    def to_column(src, dst, send, recv, peer):
        return pltpu.make_async_remote_copy(
            src_ref=src, dst_ref=dst, send_sem=send, recv_sem=recv,
            device_id={"group": peer}, device_id_type=MESH,
        )

    def above(step):
        return lax.rem(group + step, groups)

    barrier = pltpu.get_barrier_semaphore()
    for n in range(messages):
        pl.semaphore_signal(
            barrier, inc=1, device_id={"dev": here.target(n)}, device_id_type=MESH
        )
    for step in range(1, groups):
        pl.semaphore_signal(
            barrier, inc=1, device_id={"group": above(step)}, device_id_type=MESH
        )
    late = [
        fetch(vals_hbm, vals.at[pl.ds(0, capacity)], 3),
        fetch(ws_hbm, ws, 4),
        fetch(wn_hbm, wn, 5),
        fetch(bias_hbm, bias, 6),
        fetch(cot_hbm, cot, 7),
        fetch(src_hbm, src_v, 2),
        fetch(tgt_hbm, tgt_v, 9),
    ]
    for copy in early:
        copy.wait()

    lane = lax.broadcasted_iota(I32, (block, LANES), 1)
    owned = pl.ds(0, own_blocks)

    def onehot(column):
        low = column & (LOW - 1)
        high = lax.shift_right_logical(column, 8).astype(F32).astype(BF16)
        high = jnp.concatenate([high] * (LOW // LANES), axis=1)
        ones = jnp.concatenate(
            [
                jnp.where(low == lane[: column.shape[0]] + LANES * r, 1.0, 0.0)
                for r in range(LOW // LANES)
            ],
            axis=1,
        ).astype(BF16)
        none = jnp.zeros_like(ones)
        return jnp.concatenate(
            [jnp.where(high == float(t), ones, none) for t in range(rows // LOW)], axis=1
        )

    def pick(matrix):
        return jnp.dot(matrix, table[owned].reshape(rows, width), preferred_element_type=F32)

    hub_ids = jnp.full((1, block), rows, I32)
    for k in range(share):
        hub_ids = jnp.where((lane[:1] == k) | (lane[:1] == k + share), hub_rows[k], hub_ids)
    picked = pick(onehot(column_of(hub_ids, block)[: 2 * share]))[:share]
    hub_row[...] = picked
    hub_pair[core] = picked

    def fill(low, high):
        parts = [
            onehot(column_of(lists[pl.ds(here.target(n), 1), :], block))
            for n in range(low, high)
        ]
        got = pick(jnp.concatenate(parts, axis=0)).astype(BF16)
        halo_out[pl.ds(low, high - low)] = got.reshape(high - low, block, width)

    def halo_copy(n):
        return to_plane(
            halo_out.at[n], table.at[own_blocks + me], h_send.at[n], h_recv.at[me], here.target(n)
        )

    def from_plane(dst, send, recv, peer):
        return to_plane(dst, dst, send, recv, peer)

    spans = [(low, min(low + PART, messages)) for low in range(0, messages, PART)]

    def ship(span):
        for n in range(*span):
            halo_copy(n).start()

    hub_mate = to_plane(hub_row, hub_pair.at[core], m_sem.at[0], m_sem.at[1], mate)

    def hub_spread(n):
        return to_plane(
            hub_send, hub_plane.at[chip], a_send.at[n], a_recv.at[chip], here.across(n)
        )

    def hub_block(owner, side):
        return table.at[hub_start + owner * 2 + side]

    half_chips = chips // 2

    def hub_up(step):
        return to_column(
            hub_plane.at[pl.ds(core * half_chips, half_chips)],
            hub_in_table(group, core),
            z_send.at[step], z_recv.at[group], above(step),
        )

    def hub_in_table(owner, side):
        return hub_table.at[pl.ds((owner * 2 + side) * half_chips, half_chips)]

    hub_table = table.at[pl.ds(hub_start, blocks - hub_start)].reshape(
        (blocks - hub_start) * half_chips, 2 * share, width
    )

    fill(*spans[0])
    pl.semaphore_wait(barrier, devs + groups - 2)
    hub_mate.start()
    ship(spans[0])
    fill(*spans[1])

    hub_mate.wait_recv()
    both = hub_pair[...].reshape(2 * share, width).astype(BF16)
    hub_send[...] = both
    hub_plane[chip] = both
    spreads = core == lax.div(chip, half_chips)

    @pl.when(spreads)
    def _():
        for n in range(1, chips):
            hub_spread(n).start()

    ship(spans[1])

    for span in spans[2:]:
        fill(*span)
        ship(span)

    for n in range(half_chips):
        source = core * half_chips + n

        @pl.when(source != chip)
        def _():
            from_plane(hub_plane.at[source], a_send.at[n], a_recv.at[source], mate).wait_recv()

    for step in range(1, groups):
        hub_up(step).start()
    hub_table[pl.ds((group * 2 + core) * half_chips, half_chips)] = hub_plane[
        pl.ds(core * half_chips, half_chips)
    ]

    def hub_over(owner):
        part = hub_in_table(owner, core)
        return to_plane(part, part, c_send.at[owner], c_recv.at[owner], mate)

    hub_over(group).start()

    for copy in late:
        copy.wait()
    count = counts[0, 0]
    src = src_v[...]
    tgt = tgt_v[...]
    ahead = slot_plan(tgt, src, count, own_blocks)
    back = slot_plan(lax.rem(src + blocks - own_blocks, blocks), tgt, count, blocks)
    for at, row in enumerate(ahead):
        plan_v[pl.ds(at, 1), :] = row
    for at, row in enumerate(back):
        plan_v[pl.ds(ROWS_OF_PLAN + at, 1), :] = row
    plan_copy = fetch(plan_v, plan_s, 8)
    table[own_blocks + me] = jnp.zeros((block, width), BF16)
    vals[capacity] = jnp.zeros((block, block), BF16)
    turned[capacity] = jnp.zeros((block, block), BF16)
    runs[0] = jnp.zeros((block, width), F32)
    wide[pl.ds(2 * width, 16), :] = jnp.ones((16, rows), BF16)

    def turn(step, _):
        for u in range(UNROLL):
            k = step * UNROLL + u
            turned[k] = vals[k].T
        return _

    lax.fori_loop(0, capacity // UNROLL, turn, 0)

    def span_of(t):
        return pl.ds(pl.multiple_of(t * 2 * block, 2 * block), 2 * block)

    def own_part(t, _):
        own = table[pl.ds(t * 2, 2)].reshape(2 * block, width)
        own_pre[span_of(t), :] = (
            jnp.dot(own, ws[...], preferred_element_type=F32) + bias[...]
        )
        wide[pl.ds(0, width), span_of(t)] = own.T
        return _

    lax.fori_loop(0, own_blocks // 2, own_part, 0)
    plan_copy.wait()

    def pass_on(step):
        owner = lax.rem(group + groups - step, groups)
        part = hub_in_table(owner, core)
        to_column(part, part, z_send.at[step], z_recv.at[owner], owner).wait_recv()
        hub_over(owner).start()

    for step in range(1, groups):
        pass_on(step)

    for step in range(groups):
        owner = lax.rem(group + groups - step, groups)
        got = hub_in_table(owner, 1 - core)
        hub_over(owner).wait_send()
        to_plane(got, got, c_send.at[owner], c_recv.at[owner], mate).wait_recv()
    for n in range(messages):
        source = here.source(n)
        from_plane(
            table.at[own_blocks + source], h_send.at[n], h_recv.at[source], source
        ).wait_recv()

    def forward(step, _):
        for u in range(UNROLL):
            p = step * UNROLL + u
            left = jnp.concatenate([vals[plan_s[0, p]], vals[plan_s[1, p]]], axis=1)
            right = jnp.concatenate([table[plan_s[2, p]], table[plan_s[3, p]]], axis=0)
            runs[p + 1] = runs[plan_s[4, p]] + jnp.dot(left, right, preferred_element_type=F32)
        return _

    lax.fori_loop(0, pl.cdiv(capacity + own_blocks, 2 * UNROLL), forward, 0)

    def dense_part(t):
        at = span_of(t)
        near = jnp.concatenate(
            [runs[plan_s[5, t * 2]], runs[plan_s[5, t * 2 + 1]]], axis=0
        ).astype(BF16)
        wide[pl.ds(width, width), at] = near.T
        pre = own_pre[at, :] + jnp.dot(near, wn[...], preferred_element_type=F32)
        sigmoid = 0.5 * jnp.tanh(0.5 * pre) + 0.5
        result = pre * sigmoid
        output[at, :] = result.astype(BF16)
        slope = sigmoid + result * (1.0 - sigmoid)
        dpre = (cot[at, :].astype(F32) * slope).astype(BF16)
        dpre_ref[at, :] = dpre
        dagg[pl.ds(t * 2, 2)] = (
            lax.dot_general(dpre, wn[...], LAST, preferred_element_type=F32)
            .astype(BF16)
            .reshape(2, block, width)
        )

    def dense(step, _):
        dense_part(step * 2)
        dense_part(step * 2 + 1)
        return _

    lax.fori_loop(0, own_blocks // 4, dense, 0)
    output_copy = fetch(output, output_hbm, 10)

    sums = jnp.dot(wide[...], dpre_ref[...], preferred_element_type=F32)
    pieces, part_rows = wsend.shape[1], wsend.shape[2]
    wsend[:, pl.ds(0, pieces - 1)] = (
        sums[: 2 * width].astype(BF16).reshape(groups, pieces - 1, part_rows, width)
    )
    wsend[:, pieces - 1] = jnp.broadcast_to(
        sums[2 * width :].astype(BF16)[None], (groups, part_rows, width)
    )

    def w_up(step):
        return to_column(
            wsend.at[above(step)], wz_in.at[group], y_send.at[step], y_recv.at[group], above(step)
        )

    for step in range(1, groups):
        w_up(step).start()
    wz_in[group] = wsend[group]
    for n in range(messages):
        halo_copy(n).wait_send()

    def backward(step, _):
        for u in range(UNROLL):
            p = step * UNROLL + u
            left = jnp.concatenate(
                [turned[plan_s[ROWS_OF_PLAN, p]], turned[plan_s[ROWS_OF_PLAN + 1, p]]], axis=1
            )
            right = jnp.concatenate(
                [dagg[plan_s[ROWS_OF_PLAN + 2, p]], dagg[plan_s[ROWS_OF_PLAN + 3, p]]], axis=0
            )
            runs[p + 1] = runs[plan_s[ROWS_OF_PLAN + 4, p]] + jnp.dot(
                left, right, preferred_element_type=F32
            )
        return _

    halo_steps = pl.cdiv(capacity + devs, 2 * UNROLL)
    lax.fori_loop(0, halo_steps, backward, 0)

    def dtable(key):
        return runs[plan_s[ROWS_OF_PLAN + 5, key]]

    hub_key, own_key = devs, blocks - own_blocks

    def back_copy(n):
        return to_plane(halo_out.at[n], halo_in.at[me], g_send.at[n], g_recv.at[me], here.target(n))

    for n in range(messages):
        halo_out[n] = dtable(here.target(n)).astype(BF16)
        back_copy(n).start()
    lax.fori_loop(halo_steps, pl.cdiv(capacity + blocks, 2 * UNROLL), backward, 0)
    for k in range(groups):
        pair_out[k] = dtable(hub_key + 2 * k + 1 - core).astype(BF16)
    pair = to_plane(pair_out, pair_in, p_sem.at[0], p_sem.at[1], mate)
    pair.start()

    def begin(t, _):
        at = span_of(t)
        own = jnp.concatenate(
            [dtable(own_key + t * 2), dtable(own_key + t * 2 + 1)], axis=0
        )
        acc[at, :] = own + lax.dot_general(
            dpre_ref[at, :], ws[...], LAST, preferred_element_type=F32
        )
        return _

    lax.fori_loop(0, own_blocks // 2, begin, 0)

    pair.wait_recv()
    for k in range(groups):
        z_out[k] = (dtable(hub_key + 2 * k + core) + pair_in[k].astype(F32)).astype(BF16)

    def s_copy(step):
        return to_column(
            z_out.at[above(step)], z_in.at[group], s_send.at[step], s_recv.at[group], above(step)
        )

    for step in range(1, groups):
        s_copy(step).start()
    z_in[group] = z_out[group]

    for step in range(1, groups):
        peer = above(step)
        to_column(
            wz_in.at[peer], wz_in.at[peer], y_send.at[step], y_recv.at[peer], peer
        ).wait_recv()
    wmid[...] = jnp.sum(wz_in[...].astype(F32), axis=0).astype(BF16)
    apart = devs // pieces
    piece = lax.div(me, apart)
    summing = (lax.rem(me, apart) == 0) & (piece < pieces)

    def w_copy(k):
        return to_plane(wmid.at[k], w_in.at[me], w_send.at[k], w_recv.at[me], k * apart)

    for k in range(pieces):
        @pl.when(me != k * apart)
        def _():
            w_copy(k).start()

    def w_spread(n):
        return to_plane(
            wplane.at[piece], wplane.at[piece], f_send.at[n], f_recv.at[piece], here.target(n)
        )

    @pl.when(summing)
    def _():
        w_in[me] = wmid[piece]
        for n in range(messages):
            source = here.source(n)
            from_plane(w_in.at[source], f_send.at[n], w_recv.at[source], source).wait_recv()
        wplane[piece] = jnp.sum(w_in[...].astype(F32), axis=0).astype(BF16)
        for n in range(messages):
            w_spread(n).start()

    def scatter(span):
        ids, got = [], []
        for n in range(*span):
            source = here.source(n)
            from_plane(halo_in.at[source], g_send.at[n], g_recv.at[source], source).wait_recv()
            ids.append(lists[pl.ds(source, 1), :])
            got.append(halo_in[source])
        ids = jnp.concatenate(ids, axis=1)
        got = jnp.concatenate(got, axis=0)
        low = ids & (TILE - 1)
        node = lax.broadcasted_iota(I32, (TILE, ids.shape[1]), 0)
        ones = jnp.where(node == low, 1.0, 0.0).astype(BF16)
        for t in range(rows // TILE):
            here_too = jnp.where(ids - low == t * TILE, 1.0, 0.0).astype(BF16)
            acc[pl.ds(t * TILE, TILE), :] += jnp.dot(
                ones * here_too, got, preferred_element_type=F32
            )

    edges = [0, 8, 16, 24, 28, messages]
    wider = list(zip(edges[:-1], edges[1:]))
    for span in wider[:1]:
        scatter(span)

    for step in range(1, groups):
        peer = above(step)
        to_column(
            z_out.at[peer], z_in.at[peer], s_send.at[step], s_recv.at[peer], peer
        ).wait_recv()
    row_out[...] = jnp.sum(z_in[...].astype(F32), axis=0).reshape(row_out.shape)

    def row_copy(k):
        return to_plane(
            row_out.at[k], row_in.at[chip], r_send.at[k], r_recv.at[chip], core * chips + k
        )

    for k in range(chips):
        @pl.when(core * chips + k != me)
        def _():
            row_copy(k).start()

        @pl.when(core * chips + k == me)
        def _():
            row_in[chip] = row_out[k]

    for k in range(pieces):
        @pl.when(me != k * apart)
        def _():
            from_plane(wplane.at[k], f_send.at[k], f_recv.at[k], k * apart).wait_recv()

    def w_around(step):
        return to_column(
            wplane.at[pl.ds(0, pieces - 1)], wall.at[group], u_send.at[step], u_recv.at[group],
            above(step),
        )

    for step in range(1, groups):
        w_around(step).start()
    wall[group] = wplane[pl.ds(0, pieces - 1)]
    bias_copy = fetch(wplane.at[pieces - 1], bias_out, 11)

    for span in wider[1:]:
        scatter(span)

    side = lax.div(me, chips)
    for k in range(chips):
        sender = k * 2 + side

        @pl.when(sender != me)
        def _():
            to_plane(row_out.at[k], row_in.at[k], r_send.at[k], r_recv.at[k], sender).wait_recv()

    hub_sum = jnp.sum(row_in[...], axis=0)
    top = hub_sum.astype(BF16).astype(F32)
    both = jnp.concatenate([top, hub_sum - top], axis=0).astype(BF16)
    hub_ids = hub_ids[:, : 2 * share]

    def result_copy(t):
        at = pl.ds(t * TILE, TILE)
        return pltpu.make_async_copy(grad.at[at], grad_hbm.at[at], local.at[13 + t])

    for t in range(rows // TILE):
        at = pl.ds(t * TILE, TILE)
        node = lax.broadcasted_iota(I32, (TILE, 2 * share), 0) + t * TILE
        chosen = jnp.where(node == hub_ids, 1.0, 0.0).astype(BF16)
        grad[at, :] = (
            acc[at, :] + jnp.dot(chosen, both, preferred_element_type=F32)
        ).astype(BF16)
        result_copy(t).start()

    for step in range(1, groups):
        peer = above(step)
        to_column(
            wall.at[peer], wall.at[peer], u_send.at[step], u_recv.at[peer], peer
        ).wait_recv()
    wout_copy = fetch(wall, wout, 12)

    hub_mate.wait_send()
    pair.wait_send()

    @pl.when(spreads)
    def _():
        for n in range(1, chips):
            hub_spread(n).wait_send()

    for step in range(1, groups):
        hub_up(step).wait_send()
        w_up(step).wait_send()
        w_around(step).wait_send()
        s_copy(step).wait_send()
    for n in range(messages):
        back_copy(n).wait_send()
    for k in range(pieces):
        @pl.when(me != k * apart)
        def _():
            w_copy(k).wait_send()

    @pl.when(summing)
    def _():
        for n in range(messages):
            w_spread(n).wait_send()

    for k in range(chips):
        @pl.when(core * chips + k != me)
        def _():
            row_copy(k).wait_send()

    for copy in (output_copy, bias_copy, wout_copy):
        copy.wait()
    for t in range(rows // TILE):
        result_copy(t).wait()


def layer_call(hub_rows, count, src, tgt, lists, features, values, ws, wn, bias, cot, groups, devs, share):
    own_blocks, block, width = features.shape
    rows = own_blocks * block
    capacity = values.shape[0]
    hubs = groups * devs * share
    blocks = own_blocks + devs + hubs // block
    chips = devs // 2
    part_rows = 16
    pieces = 2 * width // groups // part_rows + 1
    most = UNROLL * pl.cdiv(capacity + blocks, 2 * UNROLL)
    dma = pltpu.SemaphoreType.DMA
    vm = pltpu.VMEM
    anywhere = pl.BlockSpec(memory_space=pl.ANY)
    smem = pl.BlockSpec(memory_space=pltpu.SMEM)
    return pl.pallas_call(
        functools.partial(layer_kernel, groups, devs),
        out_shape=(
            jax.ShapeDtypeStruct((rows, width), BF16),
            jax.ShapeDtypeStruct((rows, width), BF16),
            jax.ShapeDtypeStruct((groups, pieces - 1, part_rows, width), BF16),
            jax.ShapeDtypeStruct((part_rows, width), BF16),
        ),
        in_specs=[smem] * 2 + [anywhere] * 9,
        out_specs=[anywhere] * 4,
        scratch_shapes=[
            vm(src.shape, I32), vm(tgt.shape, I32), vm((rows, width), BF16), vm((rows, width), BF16),
            vm((2 * width + 16, rows), BF16), vm(lists.shape, I32),
            vm((capacity + 1, block, block), BF16), vm((capacity + 1, block, block), BF16),
            vm((width, width), BF16), vm((width, width), BF16), vm((1, width), F32),
            vm((rows, width), BF16),
            vm((blocks, block, width), BF16), vm((most + 1, block, width), F32),
            vm((rows, width), F32), vm((rows, width), BF16),
            vm((own_blocks, block, width), BF16), vm((rows, width), F32),
            vm((devs, block, width), BF16), vm((devs, block, width), BF16),
            vm((share, width), F32), vm((2, share, width), F32),
            vm((2 * share, width), BF16), vm((chips, 2 * share, width), BF16),
            vm((groups, block, width), BF16), vm((groups, block, width), BF16),
            vm((groups, block, width), BF16), vm((groups, block, width), BF16),
            vm((chips, share, width), F32), vm((chips, share, width), F32),
            vm((groups, pieces, part_rows, width), BF16), vm((groups, pieces, part_rows, width), BF16),
            vm((pieces, part_rows, width), BF16), vm((devs, part_rows, width), BF16),
            vm((pieces, part_rows, width), BF16), vm((groups, pieces - 1, part_rows, width), BF16),
            vm((2 * ROWS_OF_PLAN, LANES), I32), pltpu.SMEM((2 * ROWS_OF_PLAN, LANES), I32),
            dma((13 + rows // TILE,)), dma((devs,)), dma((devs,)), dma((2,)), dma((chips,)), dma((chips,)),
            dma((groups,)), dma((groups,)), dma((groups,)), dma((groups,)),
            dma((devs,)), dma((devs,)), dma((2,)), dma((groups,)), dma((groups,)),
            dma((chips,)), dma((chips,)),
            dma((pieces,)), dma((devs,)), dma((groups,)), dma((groups,)), dma((devs,)), dma((pieces,)),
            dma((groups,)), dma((groups,)),
        ],
        compiler_params=pltpu.CompilerParams(
            collective_id=0, has_side_effects=True, vmem_limit_bytes=56 * MIB
        ),
        name="layer",
    )(hub_rows, count, src, tgt, lists, features, values, ws, wn, bias, cot)


def finish_kernel(
    scale, output_in, grad_in, weights_in, bias_in,
    output, grad, grad_self, grad_neigh, grad_bias,
    weights, sums, self_v, neigh_v, bias_v, staged, sems,
):
    def move(src, dst, which):
        copy = pltpu.make_async_copy(src, dst, sems.at[which])
        copy.start()
        return copy

    first = [move(weights_in, weights, 0), move(bias_in, sums, 1)]
    rows = staged.shape[2]
    whole = [(output_in, output), (grad_in, grad)]
    pieces = [(which, part) for part in range(staged.shape[1]) for which in range(2)]

    def place(part):
        return pl.ds(part * rows, rows)

    inward = [
        move(whole[which][0].at[place(part)], staged.at[which, part], 5 + n)
        for n, (which, part) in enumerate(pieces)
    ]
    for copy in first:
        copy.wait()
    half = weights.shape[0] // 2
    self_v[...] = weights[pl.ds(0, half)].reshape(self_v.shape).astype(F32) * scale
    moved = [move(self_v, grad_self, 2)]
    neigh_v[...] = weights[pl.ds(half, half)].reshape(neigh_v.shape).astype(F32) * scale
    moved.append(move(neigh_v, grad_neigh, 3))
    bias_v[...] = sums[pl.ds(0, 1), :].astype(F32) * scale
    moved.append(move(bias_v, grad_bias, 4))
    for n, (which, part) in enumerate(pieces):
        inward[n].wait()
        moved.append(move(staged.at[which, part], whole[which][1].at[place(part)], 5 + n))
    for copy in moved:
        copy.wait()


def finish_call(scale, output, grad, weights, bias):
    rows, width = output.shape
    vm = pltpu.VMEM
    anywhere = pl.BlockSpec(memory_space=pl.ANY)
    square = jax.ShapeDtypeStruct((width, width), F32)
    line = jax.ShapeDtypeStruct((1, width), F32)
    return pl.pallas_call(
        functools.partial(finish_kernel, scale),
        out_shape=(
            jax.ShapeDtypeStruct(output.shape, BF16), jax.ShapeDtypeStruct(grad.shape, BF16),
            square, square, line,
        ),
        in_specs=[anywhere] * 4,
        out_specs=[anywhere] * 5,
        scratch_shapes=[
            vm(weights.shape, BF16), vm(bias.shape, BF16),
            vm((width, width), F32), vm((width, width), F32), vm((1, width), F32),
            vm((2, rows // TILE, TILE, width), BF16),
            pltpu.SemaphoreType.DMA((5 + 2 * (rows // TILE),)),
        ],
        compiler_params=pltpu.CompilerParams(vmem_limit_bytes=63 * MIB),
        name="finish",
    )(output, grad, weights, bias)


def shards(groups, devs, features, weight_self, weight_neigh, bias, cotangent, hub_rows,
           halo_send, block_src, block_tgt, block_count, block_vals):
    rows, width = features.shape
    scale = 1.0 / math.sqrt(rows * groups * devs)
    block = block_vals.shape[-1]
    results = layer_call(
        hub_rows, block_count, block_src[0], block_tgt[0],
        halo_send[0, 0], features.reshape(-1, block, width), block_vals[0, 0],
        weight_self, weight_neigh, bias[None], cotangent, groups, devs, hub_rows.shape[0],
    )
    output, grad, grad_self, grad_neigh, grad_bias = finish_call(scale, *results)
    return output, grad, grad_self, grad_neigh, grad_bias.reshape(width)


def solution(mesh):
    groups, devs = mesh.shape["group"], mesh.shape["dev"]
    return jax.shard_map(
        functools.partial(shards, groups, devs),
        mesh=mesh,
        in_specs=(
            P(("group", "dev"), None),
            P(),
            P(),
            P(),
            P(("group", "dev"), None),
            P(("group", "dev")),
            P("group", "dev", None, None),
            P("group", "dev", None),
            P("group", "dev", None),
            P("group", "dev"),
            P("group", "dev", None, None, None),
        ),
        out_specs=(P(("group", "dev"), None), P(("group", "dev"), None), P(), P(), P()),
        check_vma=False,
    )
```

```python
import functools
import math
import random

import jax
import jax.numpy as jnp
from jax import lax
from jax.experimental import pallas as pl
from jax.experimental.pallas import tpu as pltpu
from jax.sharding import PartitionSpec as P

MESH = pl.DeviceIdType.MESH
LANES = 128
BF16 = jnp.bfloat16
F32 = jnp.float32
I32 = jnp.int32
FIRST = (((0,), (0,)), ((), ()))
LAST = (((1,), (1,)), ((), ()))
MIB = 1 << 20
PART = 4
UNROLL = 8
ROWS_OF_PLAN = 8
TILE = 512
LOW = 256


def send_order(devs):
    ys = devs // 8
    every = [(y, x, c) for y in range(ys) for x in range(4) for c in range(2)][1:]
    draw = random.Random(1)
    draw.shuffle(every)
    other = [(-y % ys, -x % 4, c) for y, x, c in every]
    return every, other


class Place:
    def __init__(self, me, devs):
        self.me = me
        self.ys = devs // 8
        self.y = lax.div(me, 8)
        self.x = lax.rem(lax.div(me, 2), 4)
        self.core = lax.rem(me, 2)
        self.mate = me + 1 - 2 * self.core
        self.chip = lax.div(me, 2)
        self.plans = send_order(devs)

    def at(self, offset, sign):
        y, x, c = offset
        y, x = (y, x) if sign > 0 else (self.ys - y, 4 - x)
        return (
            lax.rem(self.y + y, self.ys) * 8
            + lax.rem(self.x + x, 4) * 2
            + lax.rem(self.core + c, 2)
        )

    def target(self, n):
        first, second = self.plans
        return jnp.where(self.core == 0, self.at(first[n], 1), self.at(second[n], 1))

    def source(self, n):
        first, second = self.plans
        sender = lax.rem(self.core + first[n][2], 2)
        return jnp.where(sender == 0, self.at(first[n], -1), self.at(second[n], -1))

    def across(self, n):
        chips = 4 * self.ys
        return lax.rem(self.chip + n, chips) * 2 + self.core


def column_of(row, size):
    return jnp.broadcast_to(row, (size, size)).T


def slot_plan(key, other, count, limit):
    size = key.shape[1]
    down = lax.broadcasted_iota(I32, (size, size), 0)
    along = lax.broadcasted_iota(I32, (size, size), 1)
    live = down < count
    keys = column_of(key, size)
    others = column_of(other, size)

    def total(mask, value=1):
        return jnp.sum(jnp.where(mask, value, 0), axis=0, keepdims=True)

    earlier = (keys == key) & (down < along)
    rank = total(earlier & live)
    odd = rank & 1
    ranks = column_of(rank, size)
    odds = ranks & 1
    heads = live & (odds == 0)
    pair = total(heads & ((keys < key) | earlier)) - odd
    pairs = column_of(pair, size)
    match = live & (pairs == along)
    left = match & (odds == 0)
    right = match & (odds == 1)
    has_right = total(right)
    place = along[:1]
    return [
        total(left, down),
        total(right, down) + (1 - has_right) * size,
        total(left, others),
        total(right, others),
        place * (1 - total(match & (ranks == 0))),
        total(heads & (keys <= along)) * jnp.minimum(total(live & (keys == along)), 1),
    ]


def layer_kernel(
    groups, devs,
    hub_rows, counts, src_hbm, tgt_hbm, lists_hbm, feat_hbm, vals_hbm, ws_hbm, wn_hbm, bias_hbm, cot_hbm,
    output_hbm, grad_hbm, wout, bias_out,
    src_v, tgt_v, output, grad, bias_sum, wide, lists, vals, turned, ws, wn, bias, cot,
    table, runs, own_pre, dpre_ref, dagg, acc,
    halo_out, halo_in, hub_row, hub_pair, hub_send, hub_plane,
    pair_out, pair_in, z_out, z_in, row_out, row_in, wsend, wmate, wpair, w_in, wz_in, wfin,
    plan_v, plan_s,
    local, h_send, h_recv, m_sem, a_send, a_recv, z_send, z_recv, c_send, c_recv,
    g_send, g_recv, p_sem, s_send, s_recv, r_send, r_recv,
    w_send, w_recv, y_send, y_recv, f_send, f_recv,
):
    group = lax.axis_index("group")
    me = lax.axis_index("dev")
    here = Place(me, devs)
    core, mate, chip = here.core, here.mate, here.chip
    blocks, block, width = table.shape
    own_blocks = feat_hbm.shape[0]
    rows = own_blocks * block
    hub_start = own_blocks + devs
    capacity = vals_hbm.shape[0]
    share = hub_row.shape[0]
    chips = devs // 2
    messages = devs - 1

    def fetch(src, dst, which):
        copy = pltpu.make_async_copy(src, dst, local.at[which])
        copy.start()
        return copy

    early = [
        fetch(feat_hbm, table.at[pl.ds(0, own_blocks)], 0),
        fetch(lists_hbm, lists, 1),
    ]

    def to_plane(src, dst, send, recv, peer):
        return pltpu.make_async_remote_copy(
            src_ref=src, dst_ref=dst, send_sem=send, recv_sem=recv,
            device_id={"dev": peer}, device_id_type=MESH,
        )

    def to_column(src, dst, send, recv, peer):
        return pltpu.make_async_remote_copy(
            src_ref=src, dst_ref=dst, send_sem=send, recv_sem=recv,
            device_id={"group": peer}, device_id_type=MESH,
        )

    def above(step):
        return lax.rem(group + step, groups)

    barrier = pltpu.get_barrier_semaphore()
    for n in range(messages):
        pl.semaphore_signal(
            barrier, inc=1, device_id={"dev": here.target(n)}, device_id_type=MESH
        )
    for step in range(1, groups):
        pl.semaphore_signal(
            barrier, inc=1, device_id={"group": above(step)}, device_id_type=MESH
        )
    late = [
        fetch(vals_hbm, vals.at[pl.ds(0, capacity)], 3),
        fetch(ws_hbm, ws, 4),
        fetch(wn_hbm, wn, 5),
        fetch(bias_hbm, bias, 6),
        fetch(cot_hbm, cot, 7),
        fetch(src_hbm, src_v, 2),
        fetch(tgt_hbm, tgt_v, 9),
    ]
    for copy in early:
        copy.wait()

    lane = lax.broadcasted_iota(I32, (block, LANES), 1)
    owned = pl.ds(0, own_blocks)

    def onehot(column):
        low = column & (LOW - 1)
        high = lax.shift_right_logical(column, 8).astype(F32).astype(BF16)
        high = jnp.concatenate([high] * (LOW // LANES), axis=1)
        ones = jnp.concatenate(
            [
                jnp.where(low == lane[: column.shape[0]] + LANES * r, 1.0, 0.0)
                for r in range(LOW // LANES)
            ],
            axis=1,
        ).astype(BF16)
        none = jnp.zeros_like(ones)
        return jnp.concatenate(
            [jnp.where(high == float(t), ones, none) for t in range(rows // LOW)], axis=1
        )

    def pick(matrix):
        return jnp.dot(matrix, table[owned].reshape(rows, width), preferred_element_type=F32)

    hub_ids = jnp.full((1, block), rows, I32)
    for k in range(share):
        hub_ids = jnp.where((lane[:1] == k) | (lane[:1] == k + share), hub_rows[k], hub_ids)
    picked = pick(onehot(column_of(hub_ids, block)[: 2 * share]))[:share]
    hub_row[...] = picked
    hub_pair[core] = picked

    def fill(low, high):
        parts = [
            onehot(column_of(lists[pl.ds(here.target(n), 1), :], block))
            for n in range(low, high)
        ]
        got = pick(jnp.concatenate(parts, axis=0)).astype(BF16)
        halo_out[pl.ds(low, high - low)] = got.reshape(high - low, block, width)

    def halo_copy(n):
        return to_plane(
            halo_out.at[n], table.at[own_blocks + me], h_send.at[n], h_recv.at[me], here.target(n)
        )

    def from_plane(dst, send, recv, peer):
        return to_plane(dst, dst, send, recv, peer)

    spans = [(low, min(low + PART, messages)) for low in range(0, messages, PART)]

    def ship(span):
        for n in range(*span):
            halo_copy(n).start()

    hub_mate = to_plane(hub_row, hub_pair.at[core], m_sem.at[0], m_sem.at[1], mate)

    def hub_spread(n):
        return to_plane(
            hub_send, hub_plane.at[chip], a_send.at[n], a_recv.at[chip], here.across(n)
        )

    def hub_block(owner, side):
        return table.at[hub_start + owner * 2 + side]

    half_chips = chips // 2

    def hub_up(step):
        return to_column(
            hub_plane.at[pl.ds(core * half_chips, half_chips)],
            hub_in_table(group, core),
            z_send.at[step], z_recv.at[group], above(step),
        )

    def hub_in_table(owner, side):
        return hub_table.at[pl.ds((owner * 2 + side) * half_chips, half_chips)]

    hub_table = table.at[pl.ds(hub_start, blocks - hub_start)].reshape(
        (blocks - hub_start) * half_chips, 2 * share, width
    )

    fill(*spans[0])
    pl.semaphore_wait(barrier, devs + groups - 2)
    hub_mate.start()
    ship(spans[0])
    fill(*spans[1])

    hub_mate.wait_recv()
    both = hub_pair[...].reshape(2 * share, width).astype(BF16)
    hub_send[...] = both
    hub_plane[chip] = both
    spreads = core == lax.div(chip, half_chips)

    @pl.when(spreads)
    def _():
        for n in range(1, chips):
            hub_spread(n).start()

    ship(spans[1])

    for span in spans[2:]:
        fill(*span)
        ship(span)

    for n in range(half_chips):
        source = core * half_chips + n

        @pl.when(source != chip)
        def _():
            from_plane(hub_plane.at[source], a_send.at[n], a_recv.at[source], mate).wait_recv()

    for step in range(1, groups):
        hub_up(step).start()
    hub_table[pl.ds((group * 2 + core) * half_chips, half_chips)] = hub_plane[
        pl.ds(core * half_chips, half_chips)
    ]

    def hub_over(owner):
        part = hub_in_table(owner, core)
        return to_plane(part, part, c_send.at[owner], c_recv.at[owner], mate)

    hub_over(group).start()

    for copy in late:
        copy.wait()
    count = counts[0, 0]
    src = src_v[...]
    tgt = tgt_v[...]
    ahead = slot_plan(tgt, src, count, own_blocks)
    back = slot_plan(lax.rem(src + blocks - own_blocks, blocks), tgt, count, blocks)
    for at, row in enumerate(ahead):
        plan_v[pl.ds(at, 1), :] = row
    for at, row in enumerate(back):
        plan_v[pl.ds(ROWS_OF_PLAN + at, 1), :] = row
    plan_copy = fetch(plan_v, plan_s, 8)
    table[own_blocks + me] = jnp.zeros((block, width), BF16)
    vals[capacity] = jnp.zeros((block, block), BF16)
    turned[capacity] = jnp.zeros((block, block), BF16)
    runs[0] = jnp.zeros((block, width), F32)
    wide[pl.ds(2 * width, 16), :] = jnp.ones((16, rows), BF16)

    def turn(step, _):
        for u in range(UNROLL):
            k = step * UNROLL + u
            turned[k] = vals[k].T
        return _

    lax.fori_loop(0, capacity // UNROLL, turn, 0)

    def span_of(t):
        return pl.ds(pl.multiple_of(t * 2 * block, 2 * block), 2 * block)

    def own_part(t, _):
        own = table[pl.ds(t * 2, 2)].reshape(2 * block, width)
        own_pre[span_of(t), :] = (
            jnp.dot(own, ws[...], preferred_element_type=F32) + bias[...]
        )
        wide[pl.ds(0, width), span_of(t)] = own.T
        return _

    lax.fori_loop(0, own_blocks // 2, own_part, 0)
    plan_copy.wait()

    def pass_on(step):
        owner = lax.rem(group + groups - step, groups)
        part = hub_in_table(owner, core)
        to_column(part, part, z_send.at[step], z_recv.at[owner], owner).wait_recv()
        hub_over(owner).start()

    for step in range(1, groups):
        pass_on(step)

    for step in range(groups):
        owner = lax.rem(group + groups - step, groups)
        got = hub_in_table(owner, 1 - core)
        hub_over(owner).wait_send()
        to_plane(got, got, c_send.at[owner], c_recv.at[owner], mate).wait_recv()
    for n in range(messages):
        source = here.source(n)
        from_plane(
            table.at[own_blocks + source], h_send.at[n], h_recv.at[source], source
        ).wait_recv()

    def forward(step, _):
        for u in range(UNROLL):
            p = step * UNROLL + u
            left = jnp.concatenate([vals[plan_s[0, p]], vals[plan_s[1, p]]], axis=1)
            right = jnp.concatenate([table[plan_s[2, p]], table[plan_s[3, p]]], axis=0)
            runs[p + 1] = runs[plan_s[4, p]] + jnp.dot(left, right, preferred_element_type=F32)
        return _

    lax.fori_loop(0, pl.cdiv(capacity + own_blocks, 2 * UNROLL), forward, 0)

    def dense_part(t):
        at = span_of(t)
        near = jnp.concatenate(
            [runs[plan_s[5, t * 2]], runs[plan_s[5, t * 2 + 1]]], axis=0
        ).astype(BF16)
        wide[pl.ds(width, width), at] = near.T
        pre = own_pre[at, :] + jnp.dot(near, wn[...], preferred_element_type=F32)
        sigmoid = 0.5 * jnp.tanh(0.5 * pre) + 0.5
        result = pre * sigmoid
        output[at, :] = result.astype(BF16)
        slope = sigmoid + result * (1.0 - sigmoid)
        dpre = (cot[at, :].astype(F32) * slope).astype(BF16)
        dpre_ref[at, :] = dpre
        dagg[pl.ds(t * 2, 2)] = (
            lax.dot_general(dpre, wn[...], LAST, preferred_element_type=F32)
            .astype(BF16)
            .reshape(2, block, width)
        )

    def dense(step, _):
        dense_part(step * 2)
        dense_part(step * 2 + 1)
        return _

    lax.fori_loop(0, own_blocks // 4, dense, 0)
    output_copy = fetch(output, output_hbm, 10)

    sums = jnp.dot(wide[...], dpre_ref[...], preferred_element_type=F32)
    part_rows = wsend.shape[2]
    wsend[:, :, :, pl.ds(0, width)] = (
        sums[: 2 * width].astype(BF16).reshape(2, chips, part_rows, width)
    )
    line = lax.broadcasted_iota(I32, (part_rows, LANES), 0)
    gbias = sums[2 * width : 2 * width + 1]
    gbias = jnp.where(line == 0, gbias[:, :LANES], jnp.where(line == 1, gbias[:, LANES:], 0.0))
    wsend[:, :, :, pl.ds(width, LANES)] = jnp.broadcast_to(
        gbias.astype(BF16)[None, None], (2, chips, part_rows, LANES)
    )
    w_mate = to_plane(wsend.at[1 - core], wmate, m_sem.at[2], m_sem.at[3], mate)
    w_mate.start()
    for n in range(messages):
        halo_copy(n).wait_send()

    def backward(step, _):
        for u in range(UNROLL):
            p = step * UNROLL + u
            left = jnp.concatenate(
                [turned[plan_s[ROWS_OF_PLAN, p]], turned[plan_s[ROWS_OF_PLAN + 1, p]]], axis=1
            )
            right = jnp.concatenate(
                [dagg[plan_s[ROWS_OF_PLAN + 2, p]], dagg[plan_s[ROWS_OF_PLAN + 3, p]]], axis=0
            )
            runs[p + 1] = runs[plan_s[ROWS_OF_PLAN + 4, p]] + jnp.dot(
                left, right, preferred_element_type=F32
            )
        return _

    halo_steps = pl.cdiv(capacity + devs, 2 * UNROLL)
    early_steps = halo_steps // 2 - 1
    lax.fori_loop(0, early_steps, backward, 0)
    w_mate.wait_recv()
    wpair[...] = (wsend[core].astype(F32) + wmate[...].astype(F32)).astype(BF16)

    def w_copy(n):
        target = here.across(n)
        return to_plane(
            wpair.at[lax.div(target, 2)], w_in.at[chip], w_send.at[n], w_recv.at[chip], target
        )

    for n in range(1, chips):
        w_copy(n).start()
    w_in[chip] = wpair[chip]
    lax.fori_loop(early_steps, halo_steps, backward, 0)

    def dtable(key):
        return runs[plan_s[ROWS_OF_PLAN + 5, key]]

    hub_key, own_key = devs, blocks - own_blocks

    def back_copy(n):
        return to_plane(halo_out.at[n], halo_in.at[me], g_send.at[n], g_recv.at[me], here.target(n))

    for n in range(messages):
        halo_out[n] = dtable(here.target(n)).astype(BF16)
        back_copy(n).start()
    lax.fori_loop(halo_steps, pl.cdiv(capacity + blocks, 2 * UNROLL), backward, 0)
    for k in range(groups):
        pair_out[k] = dtable(hub_key + 2 * k + 1 - core).astype(BF16)
    pair = to_plane(pair_out, pair_in, p_sem.at[0], p_sem.at[1], mate)
    pair.start()

    for n in range(1, chips):
        source = here.across(n)
        at = lax.div(source, 2)
        from_plane(w_in.at[at], w_send.at[n], w_recv.at[at], source).wait_recv()
    wz_in[group] = jnp.sum(w_in[...].astype(F32), axis=0).astype(BF16)

    def y_copy(step):
        return to_column(
            wz_in.at[group], wz_in.at[group], y_send.at[step], y_recv.at[group], above(step)
        )

    for step in range(1, groups):
        y_copy(step).start()

    def begin(t, _):
        at = span_of(t)
        own = jnp.concatenate(
            [dtable(own_key + t * 2), dtable(own_key + t * 2 + 1)], axis=0
        )
        acc[at, :] = own + lax.dot_general(
            dpre_ref[at, :], ws[...], LAST, preferred_element_type=F32
        )
        return _

    lax.fori_loop(0, own_blocks // 2, begin, 0)

    pair.wait_recv()
    for k in range(groups):
        z_out[k] = (dtable(hub_key + 2 * k + core) + pair_in[k].astype(F32)).astype(BF16)

    def s_copy(step):
        return to_column(
            z_out.at[above(step)], z_in.at[group], s_send.at[step], s_recv.at[group], above(step)
        )

    for step in range(1, groups):
        s_copy(step).start()
    z_in[group] = z_out[group]

    for step in range(1, groups):
        peer = above(step)
        to_column(
            wz_in.at[peer], wz_in.at[peer], y_send.at[step], y_recv.at[peer], peer
        ).wait_recv()
    total = jnp.sum(wz_in[...].astype(F32), axis=0)
    wfin[core, chip] = total[:, :width].astype(BF16)
    bias_sum[...] = total[:8, width:]
    bias_copy = fetch(bias_sum, bias_out, 11)

    def f_copy(n):
        part = wfin.at[core, chip]
        return to_plane(part, part, f_send.at[n], f_recv.at[chip], here.across(n))

    for n in range(1, chips):
        f_copy(n).start()

    def scatter(span):
        ids, got = [], []
        for n in range(*span):
            source = here.source(n)
            from_plane(halo_in.at[source], g_send.at[n], g_recv.at[source], source).wait_recv()
            ids.append(lists[pl.ds(source, 1), :])
            got.append(halo_in[source])
        ids = jnp.concatenate(ids, axis=1)
        got = jnp.concatenate(got, axis=0)
        low = ids & (TILE - 1)
        node = lax.broadcasted_iota(I32, (TILE, ids.shape[1]), 0)
        ones = jnp.where(node == low, 1.0, 0.0).astype(BF16)
        for t in range(rows // TILE):
            here_too = jnp.where(ids - low == t * TILE, 1.0, 0.0).astype(BF16)
            acc[pl.ds(t * TILE, TILE), :] += jnp.dot(
                ones * here_too, got, preferred_element_type=F32
            )

    edges = [0, 8, 16, 24, 28, messages]
    wider = list(zip(edges[:-1], edges[1:]))
    for span in wider[:1]:
        scatter(span)

    for step in range(1, groups):
        peer = above(step)
        to_column(
            z_out.at[peer], z_in.at[peer], s_send.at[step], s_recv.at[peer], peer
        ).wait_recv()
    row_out[...] = jnp.sum(z_in[...].astype(F32), axis=0).reshape(row_out.shape)

    def row_copy(k):
        return to_plane(
            row_out.at[k], row_in.at[chip], r_send.at[k], r_recv.at[chip], core * chips + k
        )

    for k in range(chips):
        @pl.when(core * chips + k != me)
        def _():
            row_copy(k).start()

        @pl.when(core * chips + k == me)
        def _():
            row_in[chip] = row_out[k]

    scatter(wider[1])
    for n in range(1, chips):
        source = here.across(n)
        at = lax.div(source, 2)
        from_plane(wfin.at[core, at], f_send.at[n], f_recv.at[at], source).wait_recv()
    f_mate = to_plane(wfin.at[core], wfin.at[core], m_sem.at[4], m_sem.at[5], mate)
    f_mate.start()
    for span in wider[2:]:
        scatter(span)

    side = lax.div(me, chips)
    for k in range(chips):
        sender = k * 2 + side

        @pl.when(sender != me)
        def _():
            to_plane(row_out.at[k], row_in.at[k], r_send.at[k], r_recv.at[k], sender).wait_recv()

    hub_sum = jnp.sum(row_in[...], axis=0)
    top = hub_sum.astype(BF16).astype(F32)
    both = jnp.concatenate([top, hub_sum - top], axis=0).astype(BF16)
    hub_ids = hub_ids[:, : 2 * share]

    def result_copy(t):
        at = pl.ds(t * TILE, TILE)
        return pltpu.make_async_copy(grad.at[at], grad_hbm.at[at], local.at[13 + t])

    for t in range(rows // TILE):
        at = pl.ds(t * TILE, TILE)
        node = lax.broadcasted_iota(I32, (TILE, 2 * share), 0) + t * TILE
        chosen = jnp.where(node == hub_ids, 1.0, 0.0).astype(BF16)
        grad[at, :] = (
            acc[at, :] + jnp.dot(chosen, both, preferred_element_type=F32)
        ).astype(BF16)
        result_copy(t).start()

    other = wfin.at[1 - core]
    from_plane(other, m_sem.at[4], m_sem.at[5], mate).wait_recv()
    wout_copy = fetch(wfin, wout, 12)

    hub_mate.wait_send()
    pair.wait_send()

    @pl.when(spreads)
    def _():
        for n in range(1, chips):
            hub_spread(n).wait_send()

    for step in range(1, groups):
        hub_up(step).wait_send()
        y_copy(step).wait_send()
        s_copy(step).wait_send()
    for n in range(messages):
        back_copy(n).wait_send()
    for n in range(1, chips):
        w_copy(n).wait_send()
        f_copy(n).wait_send()
    w_mate.wait_send()
    f_mate.wait_send()
    for k in range(chips):
        @pl.when(core * chips + k != me)
        def _():
            row_copy(k).wait_send()

    for copy in (output_copy, bias_copy, wout_copy):
        copy.wait()
    for t in range(rows // TILE):
        result_copy(t).wait()


def layer_call(hub_rows, count, src, tgt, lists, features, values, ws, wn, bias, cot, groups, devs, share):
    own_blocks, block, width = features.shape
    rows = own_blocks * block
    capacity = values.shape[0]
    hubs = groups * devs * share
    blocks = own_blocks + devs + hubs // block
    chips = devs // 2
    part_rows = width // chips
    most = UNROLL * pl.cdiv(capacity + blocks, 2 * UNROLL)
    dma = pltpu.SemaphoreType.DMA
    vm = pltpu.VMEM
    anywhere = pl.BlockSpec(memory_space=pl.ANY)
    smem = pl.BlockSpec(memory_space=pltpu.SMEM)
    return pl.pallas_call(
        functools.partial(layer_kernel, groups, devs),
        out_shape=(
            jax.ShapeDtypeStruct((rows, width), BF16),
            jax.ShapeDtypeStruct((rows, width), BF16),
            jax.ShapeDtypeStruct((2, chips, part_rows, width), BF16),
            jax.ShapeDtypeStruct((8, LANES), F32),
        ),
        in_specs=[smem] * 2 + [anywhere] * 9,
        out_specs=[anywhere] * 4,
        scratch_shapes=[
            vm(src.shape, I32), vm(tgt.shape, I32), vm((rows, width), BF16), vm((rows, width), BF16),
            vm((8, LANES), F32), vm((2 * width + 16, rows), BF16), vm(lists.shape, I32),
            vm((capacity + 1, block, block), BF16), vm((capacity + 1, block, block), BF16),
            vm((width, width), BF16), vm((width, width), BF16), vm((1, width), F32),
            vm((rows, width), BF16),
            vm((blocks, block, width), BF16), vm((most + 1, block, width), F32),
            vm((rows, width), F32), vm((rows, width), BF16),
            vm((own_blocks, block, width), BF16), vm((rows, width), F32),
            vm((devs, block, width), BF16), vm((devs, block, width), BF16),
            vm((share, width), F32), vm((2, share, width), F32),
            vm((2 * share, width), BF16), vm((chips, 2 * share, width), BF16),
            vm((groups, block, width), BF16), vm((groups, block, width), BF16),
            vm((groups, block, width), BF16), vm((groups, block, width), BF16),
            vm((chips, share, width), F32), vm((chips, share, width), F32),
            vm((2, chips, part_rows, width + LANES), BF16), vm((chips, part_rows, width + LANES), BF16),
            vm((chips, part_rows, width + LANES), BF16), vm((chips, part_rows, width + LANES), BF16),
            vm((groups, part_rows, width + LANES), BF16), vm((2, chips, part_rows, width), BF16),
            vm((2 * ROWS_OF_PLAN, LANES), I32), pltpu.SMEM((2 * ROWS_OF_PLAN, LANES), I32),
            dma((13 + rows // TILE,)), dma((devs,)), dma((devs,)), dma((6,)), dma((chips,)), dma((chips,)),
            dma((groups,)), dma((groups,)), dma((groups,)), dma((groups,)),
            dma((devs,)), dma((devs,)), dma((2,)), dma((groups,)), dma((groups,)),
            dma((chips,)), dma((chips,)),
            dma((chips,)), dma((chips,)), dma((groups,)), dma((groups,)), dma((chips,)), dma((chips,)),
        ],
        compiler_params=pltpu.CompilerParams(
            collective_id=0, has_side_effects=True, vmem_limit_bytes=56 * MIB
        ),
        name="layer",
    )(hub_rows, count, src, tgt, lists, features, values, ws, wn, bias, cot)


def finish_kernel(
    scale, output_in, grad_in, weights_in, bias_in,
    output, grad, grad_self, grad_neigh, grad_bias,
    weights, sums, self_v, neigh_v, bias_v, staged, sems,
):
    def move(src, dst, which):
        copy = pltpu.make_async_copy(src, dst, sems.at[which])
        copy.start()
        return copy

    first = [move(weights_in, weights, 0), move(bias_in, sums, 1)]
    rows = staged.shape[2]
    whole = [(output_in, output), (grad_in, grad)]
    pieces = [(which, part) for part in range(staged.shape[1]) for which in range(2)]

    def place(part):
        return pl.ds(part * rows, rows)

    inward = [
        move(whole[which][0].at[place(part)], staged.at[which, part], 5 + n)
        for n, (which, part) in enumerate(pieces)
    ]
    for copy in first:
        copy.wait()
    self_v[...] = weights[0].reshape(self_v.shape).astype(F32) * scale
    moved = [move(self_v, grad_self, 2)]
    neigh_v[...] = weights[1].reshape(neigh_v.shape).astype(F32) * scale
    moved.append(move(neigh_v, grad_neigh, 3))
    bias_v[...] = jnp.concatenate([sums[pl.ds(0, 1), :], sums[pl.ds(1, 1), :]], axis=1) * scale
    moved.append(move(bias_v, grad_bias, 4))
    for n, (which, part) in enumerate(pieces):
        inward[n].wait()
        moved.append(move(staged.at[which, part], whole[which][1].at[place(part)], 5 + n))
    for copy in moved:
        copy.wait()


def finish_call(scale, output, grad, weights, bias):
    rows, width = output.shape
    vm = pltpu.VMEM
    anywhere = pl.BlockSpec(memory_space=pl.ANY)
    square = jax.ShapeDtypeStruct((width, width), F32)
    line = jax.ShapeDtypeStruct((1, width), F32)
    return pl.pallas_call(
        functools.partial(finish_kernel, scale),
        out_shape=(
            jax.ShapeDtypeStruct(output.shape, BF16), jax.ShapeDtypeStruct(grad.shape, BF16),
            square, square, line,
        ),
        in_specs=[anywhere] * 4,
        out_specs=[anywhere] * 5,
        scratch_shapes=[
            vm(weights.shape, BF16), vm(bias.shape, F32),
            vm((width, width), F32), vm((width, width), F32), vm((1, width), F32),
            vm((2, rows // TILE, TILE, width), BF16),
            pltpu.SemaphoreType.DMA((5 + 2 * (rows // TILE),)),
        ],
        compiler_params=pltpu.CompilerParams(vmem_limit_bytes=63 * MIB),
        name="finish",
    )(output, grad, weights, bias)


def shards(groups, devs, features, weight_self, weight_neigh, bias, cotangent, hub_rows,
           halo_send, block_src, block_tgt, block_count, block_vals):
    rows, width = features.shape
    scale = 1.0 / math.sqrt(rows * groups * devs)
    block = block_vals.shape[-1]
    results = layer_call(
        hub_rows, block_count, block_src[0], block_tgt[0],
        halo_send[0, 0], features.reshape(-1, block, width), block_vals[0, 0],
        weight_self, weight_neigh, bias[None], cotangent, groups, devs, hub_rows.shape[0],
    )
    output, grad, grad_self, grad_neigh, grad_bias = finish_call(scale, *results)
    return output, grad, grad_self, grad_neigh, grad_bias.reshape(width)


def solution(mesh):
    groups, devs = mesh.shape["group"], mesh.shape["dev"]
    return jax.shard_map(
        functools.partial(shards, groups, devs),
        mesh=mesh,
        in_specs=(
            P(("group", "dev"), None),
            P(),
            P(),
            P(),
            P(("group", "dev"), None),
            P(("group", "dev")),
            P("group", "dev", None, None),
            P("group", "dev", None),
            P("group", "dev", None),
            P("group", "dev"),
            P("group", "dev", None, None, None),
        ),
        out_specs=(P(("group", "dev"), None), P(("group", "dev"), None), P(), P(), P()),
        check_vma=False,
    )
```

```python
import functools
import math
import random

import jax
import jax.numpy as jnp
from jax import lax
from jax.experimental import pallas as pl
from jax.experimental.pallas import tpu as pltpu
from jax.sharding import PartitionSpec as P

MESH = pl.DeviceIdType.MESH
LANES = 128
BF16 = jnp.bfloat16
F32 = jnp.float32
I32 = jnp.int32
FIRST = (((0,), (0,)), ((), ()))
LAST = (((1,), (1,)), ((), ()))
MIB = 1 << 20
PART = 4
UNROLL = 8
AHEAD = 24
BACK = 16
ROWS_OF_PLAN = 8
TILE = 512
LOW = 256


def send_order(devs):
    ys = devs // 8
    every = [(y, x, c) for y in range(ys) for x in range(4) for c in range(2)][1:]
    draw = random.Random(1)
    draw.shuffle(every)
    other = [(-y % ys, -x % 4, c) for y, x, c in every]
    return every, other


class Place:
    def __init__(self, me, devs):
        self.me = me
        self.ys = devs // 8
        self.y = lax.div(me, 8)
        self.x = lax.rem(lax.div(me, 2), 4)
        self.core = lax.rem(me, 2)
        self.mate = me + 1 - 2 * self.core
        self.chip = lax.div(me, 2)
        self.plans = send_order(devs)

    def at(self, offset, sign):
        y, x, c = offset
        y, x = (y, x) if sign > 0 else (self.ys - y, 4 - x)
        return (
            lax.rem(self.y + y, self.ys) * 8
            + lax.rem(self.x + x, 4) * 2
            + lax.rem(self.core + c, 2)
        )

    def target(self, n):
        first, second = self.plans
        return jnp.where(self.core == 0, self.at(first[n], 1), self.at(second[n], 1))

    def source(self, n):
        first, second = self.plans
        sender = lax.rem(self.core + first[n][2], 2)
        return jnp.where(sender == 0, self.at(first[n], -1), self.at(second[n], -1))

    def across(self, n):
        chips = 4 * self.ys
        return lax.rem(self.chip + n, chips) * 2 + self.core


def column_of(row, size):
    return jnp.broadcast_to(row, (size, size)).T


def slot_plan(key, other, count, limit):
    size = key.shape[1]
    down = lax.broadcasted_iota(I32, (size, size), 0)
    along = lax.broadcasted_iota(I32, (size, size), 1)
    live = down < count
    keys = column_of(key, size)
    others = column_of(other, size)

    def total(mask, value=1):
        return jnp.sum(jnp.where(mask, value, 0), axis=0, keepdims=True)

    earlier = (keys == key) & (down < along)
    rank = total(earlier & live)
    odd = rank & 1
    ranks = column_of(rank, size)
    odds = ranks & 1
    heads = live & (odds == 0)
    pair = total(heads & ((keys < key) | earlier)) - odd
    pairs = column_of(pair, size)
    match = live & (pairs == along)
    left = match & (odds == 0)
    right = match & (odds == 1)
    has_right = total(right)
    return [
        total(left, down),
        total(right, down) + (1 - has_right) * size,
        total(left, others),
        total(right, others),
        1 - total(match & (ranks == 0)),
        total(heads & (keys <= along)) * jnp.minimum(total(live & (keys == along)), 1),
    ]


def layer_kernel(
    groups, devs,
    hub_rows, counts, src_hbm, tgt_hbm, lists_hbm, feat_hbm, vals_hbm, ws_hbm, wn_hbm, bias_hbm, cot_hbm,
    output_hbm, grad_hbm, wout, bias_out,
    src_v, tgt_v, output, grad, bias_sum, wide, lists, vals, turned, ws, wn, bias, cot,
    table, runs, own_pre, dpre_ref, dagg, acc,
    halo_out, halo_in, hub_row, hub_pair, hub_send, hub_plane,
    pair_out, pair_in, z_out, z_in, row_out, row_in, wsend, wmate, wpair, w_in, wz_in, wfin,
    plan_v, plan_s,
    local, h_send, h_recv, m_sem, a_send, a_recv, z_send, z_recv, c_send, c_recv,
    g_send, g_recv, p_sem, s_send, s_recv, r_send, r_recv,
    w_send, w_recv, y_send, y_recv, f_send, f_recv,
):
    group = lax.axis_index("group")
    me = lax.axis_index("dev")
    here = Place(me, devs)
    core, mate, chip = here.core, here.mate, here.chip
    blocks, block, width = table.shape
    own_blocks = feat_hbm.shape[0]
    rows = own_blocks * block
    hub_start = own_blocks + devs
    capacity = vals_hbm.shape[0]
    share = hub_row.shape[0]
    chips = devs // 2
    messages = devs - 1

    def fetch(src, dst, which):
        copy = pltpu.make_async_copy(src, dst, local.at[which])
        copy.start()
        return copy

    early = [
        fetch(feat_hbm, table.at[pl.ds(0, own_blocks)], 0),
        fetch(lists_hbm, lists, 1),
    ]

    def to_plane(src, dst, send, recv, peer):
        return pltpu.make_async_remote_copy(
            src_ref=src, dst_ref=dst, send_sem=send, recv_sem=recv,
            device_id={"dev": peer}, device_id_type=MESH,
        )

    def to_column(src, dst, send, recv, peer):
        return pltpu.make_async_remote_copy(
            src_ref=src, dst_ref=dst, send_sem=send, recv_sem=recv,
            device_id={"group": peer}, device_id_type=MESH,
        )

    def above(step):
        return lax.rem(group + step, groups)

    barrier = pltpu.get_barrier_semaphore()
    for n in range(messages):
        pl.semaphore_signal(
            barrier, inc=1, device_id={"dev": here.target(n)}, device_id_type=MESH
        )
    for step in range(1, groups):
        pl.semaphore_signal(
            barrier, inc=1, device_id={"group": above(step)}, device_id_type=MESH
        )
    late = [
        fetch(vals_hbm, vals.at[pl.ds(0, capacity)], 3),
        fetch(ws_hbm, ws, 4),
        fetch(wn_hbm, wn, 5),
        fetch(bias_hbm, bias, 6),
        fetch(cot_hbm, cot, 7),
        fetch(src_hbm, src_v, 2),
        fetch(tgt_hbm, tgt_v, 9),
    ]
    for copy in early:
        copy.wait()

    lane = lax.broadcasted_iota(I32, (block, LANES), 1)
    owned = pl.ds(0, own_blocks)

    def onehot(column):
        low = column & (LOW - 1)
        high = lax.shift_right_logical(column, 8).astype(F32).astype(BF16)
        high = jnp.concatenate([high] * (LOW // LANES), axis=1)
        ones = jnp.concatenate(
            [
                jnp.where(low == lane[: column.shape[0]] + LANES * r, 1.0, 0.0)
                for r in range(LOW // LANES)
            ],
            axis=1,
        ).astype(BF16)
        none = jnp.zeros_like(ones)
        return jnp.concatenate(
            [jnp.where(high == float(t), ones, none) for t in range(rows // LOW)], axis=1
        )

    def pick(matrix):
        return jnp.dot(matrix, table[owned].reshape(rows, width), preferred_element_type=F32)

    hub_ids = jnp.full((1, block), rows, I32)
    for k in range(share):
        hub_ids = jnp.where((lane[:1] == k) | (lane[:1] == k + share), hub_rows[k], hub_ids)
    picked = pick(onehot(column_of(hub_ids, block)[: 2 * share]))[:share]
    hub_row[...] = picked
    hub_pair[core] = picked

    def fill(low, high):
        parts = [
            onehot(column_of(lists[pl.ds(here.target(n), 1), :], block))
            for n in range(low, high)
        ]
        got = pick(jnp.concatenate(parts, axis=0)).astype(BF16)
        halo_out[pl.ds(low, high - low)] = got.reshape(high - low, block, width)

    def halo_copy(n):
        return to_plane(
            halo_out.at[n], table.at[own_blocks + me], h_send.at[n], h_recv.at[me], here.target(n)
        )

    def from_plane(dst, send, recv, peer):
        return to_plane(dst, dst, send, recv, peer)

    spans = [(low, min(low + PART, messages)) for low in range(0, messages, PART)]

    def ship(span):
        for n in range(*span):
            halo_copy(n).start()

    hub_mate = to_plane(hub_row, hub_pair.at[core], m_sem.at[0], m_sem.at[1], mate)

    def hub_spread(n):
        return to_plane(
            hub_send, hub_plane.at[chip], a_send.at[n], a_recv.at[chip], here.across(n)
        )

    def hub_block(owner, side):
        return table.at[hub_start + owner * 2 + side]

    half_chips = chips // 2

    def hub_up(step):
        return to_column(
            hub_plane.at[pl.ds(core * half_chips, half_chips)],
            hub_in_table(group, core),
            z_send.at[step], z_recv.at[group], above(step),
        )

    def hub_in_table(owner, side):
        return hub_table.at[pl.ds((owner * 2 + side) * half_chips, half_chips)]

    hub_table = table.at[pl.ds(hub_start, blocks - hub_start)].reshape(
        (blocks - hub_start) * half_chips, 2 * share, width
    )

    fill(*spans[0])
    pl.semaphore_wait(barrier, devs + groups - 2)
    hub_mate.start()
    ship(spans[0])
    fill(*spans[1])

    hub_mate.wait_recv()
    both = hub_pair[...].reshape(2 * share, width).astype(BF16)
    hub_send[...] = both
    hub_plane[chip] = both
    spreads = core == lax.div(chip, half_chips)

    @pl.when(spreads)
    def _():
        for n in range(1, chips):
            hub_spread(n).start()

    ship(spans[1])

    for span in spans[2:]:
        fill(*span)
        ship(span)

    for n in range(half_chips):
        source = core * half_chips + n

        @pl.when(source != chip)
        def _():
            from_plane(hub_plane.at[source], a_send.at[n], a_recv.at[source], mate).wait_recv()

    for step in range(1, groups):
        hub_up(step).start()
    hub_table[pl.ds((group * 2 + core) * half_chips, half_chips)] = hub_plane[
        pl.ds(core * half_chips, half_chips)
    ]

    def hub_over(owner):
        part = hub_in_table(owner, core)
        return to_plane(part, part, c_send.at[owner], c_recv.at[owner], mate)

    hub_over(group).start()

    for copy in late:
        copy.wait()
    count = counts[0, 0]
    src = src_v[...]
    tgt = tgt_v[...]
    ahead = slot_plan(tgt, src, count, own_blocks)
    back = slot_plan(lax.rem(src + blocks - own_blocks, blocks), tgt, count, blocks)
    for at, row in enumerate(ahead):
        plan_v[pl.ds(at, 1), :] = row
    for at, row in enumerate(back):
        plan_v[pl.ds(ROWS_OF_PLAN + at, 1), :] = row
    plan_copy = fetch(plan_v, plan_s, 8)
    table[own_blocks + me] = jnp.zeros((block, width), BF16)
    vals[capacity] = jnp.zeros((block, block), BF16)
    turned[capacity] = jnp.zeros((block, block), BF16)
    runs[0] = jnp.zeros((block, width), F32)
    wide[pl.ds(2 * width, 16), :] = jnp.ones((16, rows), BF16)

    def turn(step, _):
        for u in range(UNROLL):
            k = step * UNROLL + u
            turned[k] = vals[k].T
        return _

    lax.fori_loop(0, capacity // UNROLL, turn, 0)

    def span_of(t):
        return pl.ds(pl.multiple_of(t * 2 * block, 2 * block), 2 * block)

    def own_part(t, _):
        own = table[pl.ds(t * 2, 2)].reshape(2 * block, width)
        own_pre[span_of(t), :] = (
            jnp.dot(own, ws[...], preferred_element_type=F32) + bias[...]
        )
        wide[pl.ds(0, width), span_of(t)] = own.T
        return _

    lax.fori_loop(0, own_blocks // 2, own_part, 0)
    plan_copy.wait()

    def pass_on(step):
        owner = lax.rem(group + groups - step, groups)
        part = hub_in_table(owner, core)
        to_column(part, part, z_send.at[step], z_recv.at[owner], owner).wait_recv()
        hub_over(owner).start()

    for step in range(1, groups):
        pass_on(step)

    for step in range(groups):
        owner = lax.rem(group + groups - step, groups)
        got = hub_in_table(owner, 1 - core)
        hub_over(owner).wait_send()
        to_plane(got, got, c_send.at[owner], c_recv.at[owner], mate).wait_recv()
    for n in range(messages):
        source = here.source(n)
        from_plane(
            table.at[own_blocks + source], h_send.at[n], h_recv.at[source], source
        ).wait_recv()

    def run_totals(low, high, unroll, start, row, weights, tiles):
        def body(step, total):
            for u in range(unroll):
                p = step * unroll + u
                left = jnp.concatenate(
                    [weights[plan_s[row, p]], weights[plan_s[row + 1, p]]], axis=1
                )
                right = jnp.concatenate(
                    [tiles[plan_s[row + 2, p]], tiles[plan_s[row + 3, p]]], axis=0
                )
                total = total * plan_s[row + 4, p].astype(F32) + jnp.dot(
                    left, right, preferred_element_type=F32
                )
                runs[p + 1] = total
            return total

        return lax.fori_loop(low, high, body, start)

    nothing = jnp.zeros((block, width), F32)
    run_totals(0, pl.cdiv(capacity + own_blocks, 2 * AHEAD), AHEAD, nothing, 0, vals, table)

    def dense_part(t):
        at = span_of(t)
        near = jnp.concatenate(
            [runs[plan_s[5, t * 2]], runs[plan_s[5, t * 2 + 1]]], axis=0
        ).astype(BF16)
        wide[pl.ds(width, width), at] = near.T
        pre = own_pre[at, :] + jnp.dot(near, wn[...], preferred_element_type=F32)
        sigmoid = 0.5 * jnp.tanh(0.5 * pre) + 0.5
        result = pre * sigmoid
        output[at, :] = result.astype(BF16)
        slope = sigmoid + result * (1.0 - sigmoid)
        dpre = (cot[at, :].astype(F32) * slope).astype(BF16)
        dpre_ref[at, :] = dpre
        dagg[pl.ds(t * 2, 2)] = (
            lax.dot_general(dpre, wn[...], LAST, preferred_element_type=F32)
            .astype(BF16)
            .reshape(2, block, width)
        )

    def dense(step, _):
        for u in range(4):
            dense_part(step * 4 + u)
        return _

    lax.fori_loop(0, own_blocks // 8, dense, 0)
    output_copy = fetch(output, output_hbm, 10)

    sums = jnp.dot(wide[...], dpre_ref[...], preferred_element_type=F32)
    part_rows = wsend.shape[2]
    wsend[:, :, :, pl.ds(0, width)] = (
        sums[: 2 * width].astype(BF16).reshape(2, chips, part_rows, width)
    )
    line = lax.broadcasted_iota(I32, (part_rows, LANES), 0)
    gbias = sums[2 * width : 2 * width + 1]
    gbias = jnp.where(line == 0, gbias[:, :LANES], jnp.where(line == 1, gbias[:, LANES:], 0.0))
    wsend[:, :, :, pl.ds(width, LANES)] = jnp.broadcast_to(
        gbias.astype(BF16)[None, None], (2, chips, part_rows, LANES)
    )
    w_mate = to_plane(wsend.at[1 - core], wmate, m_sem.at[2], m_sem.at[3], mate)
    w_mate.start()
    for n in range(messages):
        halo_copy(n).wait_send()

    def backward(low, high, start):
        return run_totals(low, high, BACK, start, ROWS_OF_PLAN, turned, dagg)

    halo_steps = pl.cdiv(capacity + devs, 2 * BACK)
    early_steps = halo_steps // 2
    reached = backward(0, early_steps, nothing)
    w_mate.wait_recv()
    wpair[...] = (wsend[core].astype(F32) + wmate[...].astype(F32)).astype(BF16)

    def w_copy(n):
        target = here.across(n)
        return to_plane(
            wpair.at[lax.div(target, 2)], w_in.at[chip], w_send.at[n], w_recv.at[chip], target
        )

    for n in range(1, chips):
        w_copy(n).start()
    w_in[chip] = wpair[chip]
    reached = backward(early_steps, halo_steps, reached)

    def dtable(key):
        return runs[plan_s[ROWS_OF_PLAN + 5, key]]

    hub_key, own_key = devs, blocks - own_blocks

    def back_copy(n):
        return to_plane(halo_out.at[n], halo_in.at[me], g_send.at[n], g_recv.at[me], here.target(n))

    for n in range(messages):
        halo_out[n] = dtable(here.target(n)).astype(BF16)
        back_copy(n).start()
    backward(halo_steps, pl.cdiv(capacity + blocks, 2 * BACK), reached)
    for k in range(groups):
        pair_out[k] = dtable(hub_key + 2 * k + 1 - core).astype(BF16)
    pair = to_plane(pair_out, pair_in, p_sem.at[0], p_sem.at[1], mate)
    pair.start()

    for n in range(1, chips):
        source = here.across(n)
        at = lax.div(source, 2)
        from_plane(w_in.at[at], w_send.at[n], w_recv.at[at], source).wait_recv()
    wz_in[group] = jnp.sum(w_in[...].astype(F32), axis=0).astype(BF16)

    def y_copy(step):
        return to_column(
            wz_in.at[group], wz_in.at[group], y_send.at[step], y_recv.at[group], above(step)
        )

    for step in range(1, groups):
        y_copy(step).start()

    def begin(t, _):
        at = span_of(t)
        own = jnp.concatenate(
            [dtable(own_key + t * 2), dtable(own_key + t * 2 + 1)], axis=0
        )
        acc[at, :] = own + lax.dot_general(
            dpre_ref[at, :], ws[...], LAST, preferred_element_type=F32
        )
        return _

    lax.fori_loop(0, own_blocks // 2, begin, 0)

    pair.wait_recv()
    for k in range(groups):
        z_out[k] = (dtable(hub_key + 2 * k + core) + pair_in[k].astype(F32)).astype(BF16)

    def s_copy(step):
        return to_column(
            z_out.at[above(step)], z_in.at[group], s_send.at[step], s_recv.at[group], above(step)
        )

    for step in range(1, groups):
        s_copy(step).start()
    z_in[group] = z_out[group]

    for step in range(1, groups):
        peer = above(step)
        to_column(
            wz_in.at[peer], wz_in.at[peer], y_send.at[step], y_recv.at[peer], peer
        ).wait_recv()
    total = jnp.sum(wz_in[...].astype(F32), axis=0)
    wfin[core, chip] = total[:, :width].astype(BF16)
    bias_sum[...] = total[:8, width:]
    bias_copy = fetch(bias_sum, bias_out, 11)

    def f_copy(n):
        part = wfin.at[core, chip]
        return to_plane(part, part, f_send.at[n], f_recv.at[chip], here.across(n))

    for n in range(1, chips):
        f_copy(n).start()

    def scatter(span):
        ids, got = [], []
        for n in range(*span):
            source = here.source(n)
            from_plane(halo_in.at[source], g_send.at[n], g_recv.at[source], source).wait_recv()
            ids.append(lists[pl.ds(source, 1), :])
            got.append(halo_in[source])
        ids = jnp.concatenate(ids, axis=1)
        got = jnp.concatenate(got, axis=0)
        low = ids & (TILE - 1)
        node = lax.broadcasted_iota(I32, (TILE, ids.shape[1]), 0)
        ones = jnp.where(node == low, 1.0, 0.0).astype(BF16)
        for t in range(rows // TILE):
            here_too = jnp.where(ids - low == t * TILE, 1.0, 0.0).astype(BF16)
            acc[pl.ds(t * TILE, TILE), :] += jnp.dot(
                ones * here_too, got, preferred_element_type=F32
            )

    edges = [0, 8, 16, 24, 28, messages]
    wider = list(zip(edges[:-1], edges[1:]))
    for span in wider[:1]:
        scatter(span)

    for step in range(1, groups):
        peer = above(step)
        to_column(
            z_out.at[peer], z_in.at[peer], s_send.at[step], s_recv.at[peer], peer
        ).wait_recv()
    row_out[...] = jnp.sum(z_in[...].astype(F32), axis=0).reshape(row_out.shape)

    def row_copy(k):
        return to_plane(
            row_out.at[k], row_in.at[chip], r_send.at[k], r_recv.at[chip], core * chips + k
        )

    for k in range(chips):
        @pl.when(core * chips + k != me)
        def _():
            row_copy(k).start()

        @pl.when(core * chips + k == me)
        def _():
            row_in[chip] = row_out[k]

    scatter(wider[1])
    for n in range(1, chips):
        source = here.across(n)
        at = lax.div(source, 2)
        from_plane(wfin.at[core, at], f_send.at[n], f_recv.at[at], source).wait_recv()
    f_mate = to_plane(wfin.at[core], wfin.at[core], m_sem.at[4], m_sem.at[5], mate)
    f_mate.start()
    for span in wider[2:]:
        scatter(span)

    side = lax.div(me, chips)
    for k in range(chips):
        sender = k * 2 + side

        @pl.when(sender != me)
        def _():
            to_plane(row_out.at[k], row_in.at[k], r_send.at[k], r_recv.at[k], sender).wait_recv()

    hub_sum = jnp.sum(row_in[...], axis=0)
    top = hub_sum.astype(BF16).astype(F32)
    both = jnp.concatenate([top, hub_sum - top], axis=0).astype(BF16)
    hub_ids = hub_ids[:, : 2 * share]

    def result_copy(t):
        at = pl.ds(t * TILE, TILE)
        return pltpu.make_async_copy(grad.at[at], grad_hbm.at[at], local.at[13 + t])

    for t in range(rows // TILE):
        at = pl.ds(t * TILE, TILE)
        node = lax.broadcasted_iota(I32, (TILE, 2 * share), 0) + t * TILE
        chosen = jnp.where(node == hub_ids, 1.0, 0.0).astype(BF16)
        grad[at, :] = (
            acc[at, :] + jnp.dot(chosen, both, preferred_element_type=F32)
        ).astype(BF16)
        result_copy(t).start()

    other = wfin.at[1 - core]
    from_plane(other, m_sem.at[4], m_sem.at[5], mate).wait_recv()
    wout_copy = fetch(wfin, wout, 12)

    hub_mate.wait_send()
    pair.wait_send()

    @pl.when(spreads)
    def _():
        for n in range(1, chips):
            hub_spread(n).wait_send()

    for step in range(1, groups):
        hub_up(step).wait_send()
        y_copy(step).wait_send()
        s_copy(step).wait_send()
    for n in range(messages):
        back_copy(n).wait_send()
    for n in range(1, chips):
        w_copy(n).wait_send()
        f_copy(n).wait_send()
    w_mate.wait_send()
    f_mate.wait_send()
    for k in range(chips):
        @pl.when(core * chips + k != me)
        def _():
            row_copy(k).wait_send()

    for copy in (output_copy, bias_copy, wout_copy):
        copy.wait()
    for t in range(rows // TILE):
        result_copy(t).wait()


def layer_call(hub_rows, count, src, tgt, lists, features, values, ws, wn, bias, cot, groups, devs, share):
    own_blocks, block, width = features.shape
    rows = own_blocks * block
    capacity = values.shape[0]
    hubs = groups * devs * share
    blocks = own_blocks + devs + hubs // block
    chips = devs // 2
    part_rows = width // chips
    most = max(
        AHEAD * pl.cdiv(capacity + own_blocks, 2 * AHEAD), BACK * pl.cdiv(capacity + blocks, 2 * BACK)
    )
    dma = pltpu.SemaphoreType.DMA
    vm = pltpu.VMEM
    anywhere = pl.BlockSpec(memory_space=pl.ANY)
    smem = pl.BlockSpec(memory_space=pltpu.SMEM)
    return pl.pallas_call(
        functools.partial(layer_kernel, groups, devs),
        out_shape=(
            jax.ShapeDtypeStruct((rows, width), BF16),
            jax.ShapeDtypeStruct((rows, width), BF16),
            jax.ShapeDtypeStruct((2, chips, part_rows, width), BF16),
            jax.ShapeDtypeStruct((8, LANES), F32),
        ),
        in_specs=[smem] * 2 + [anywhere] * 9,
        out_specs=[anywhere] * 4,
        scratch_shapes=[
            vm(src.shape, I32), vm(tgt.shape, I32), vm((rows, width), BF16), vm((rows, width), BF16),
            vm((8, LANES), F32), vm((2 * width + 16, rows), BF16), vm(lists.shape, I32),
            vm((capacity + 1, block, block), BF16), vm((capacity + 1, block, block), BF16),
            vm((width, width), BF16), vm((width, width), BF16), vm((1, width), F32),
            vm((rows, width), BF16),
            vm((blocks, block, width), BF16), vm((most + 1, block, width), F32),
            vm((rows, width), F32), vm((rows, width), BF16),
            vm((own_blocks, block, width), BF16), vm((rows, width), F32),
            vm((devs, block, width), BF16), vm((devs, block, width), BF16),
            vm((share, width), F32), vm((2, share, width), F32),
            vm((2 * share, width), BF16), vm((chips, 2 * share, width), BF16),
            vm((groups, block, width), BF16), vm((groups, block, width), BF16),
            vm((groups, block, width), BF16), vm((groups, block, width), BF16),
            vm((chips, share, width), F32), vm((chips, share, width), F32),
            vm((2, chips, part_rows, width + LANES), BF16), vm((chips, part_rows, width + LANES), BF16),
            vm((chips, part_rows, width + LANES), BF16), vm((chips, part_rows, width + LANES), BF16),
            vm((groups, part_rows, width + LANES), BF16), vm((2, chips, part_rows, width), BF16),
            vm((2 * ROWS_OF_PLAN, LANES), I32), pltpu.SMEM((2 * ROWS_OF_PLAN, LANES), I32),
            dma((13 + rows // TILE,)), dma((devs,)), dma((devs,)), dma((6,)), dma((chips,)), dma((chips,)),
            dma((groups,)), dma((groups,)), dma((groups,)), dma((groups,)),
            dma((devs,)), dma((devs,)), dma((2,)), dma((groups,)), dma((groups,)),
            dma((chips,)), dma((chips,)),
            dma((chips,)), dma((chips,)), dma((groups,)), dma((groups,)), dma((chips,)), dma((chips,)),
        ],
        compiler_params=pltpu.CompilerParams(
            collective_id=0, has_side_effects=True, vmem_limit_bytes=56 * MIB
        ),
        name="layer",
    )(hub_rows, count, src, tgt, lists, features, values, ws, wn, bias, cot)


def finish_kernel(
    scale, output_in, grad_in, weights_in, bias_in,
    output, grad, grad_self, grad_neigh, grad_bias,
    weights, sums, self_v, neigh_v, bias_v, staged, sems,
):
    def move(src, dst, which):
        copy = pltpu.make_async_copy(src, dst, sems.at[which])
        copy.start()
        return copy

    first = [move(weights_in, weights, 0), move(bias_in, sums, 1)]
    rows = staged.shape[2]
    whole = [(output_in, output), (grad_in, grad)]
    pieces = [(which, part) for part in range(staged.shape[1]) for which in range(2)]

    def place(part):
        return pl.ds(part * rows, rows)

    inward = [
        move(whole[which][0].at[place(part)], staged.at[which, part], 5 + n)
        for n, (which, part) in enumerate(pieces)
    ]
    for copy in first:
        copy.wait()
    self_v[...] = weights[0].reshape(self_v.shape).astype(F32) * scale
    moved = [move(self_v, grad_self, 2)]
    neigh_v[...] = weights[1].reshape(neigh_v.shape).astype(F32) * scale
    moved.append(move(neigh_v, grad_neigh, 3))
    bias_v[...] = jnp.concatenate([sums[pl.ds(0, 1), :], sums[pl.ds(1, 1), :]], axis=1) * scale
    moved.append(move(bias_v, grad_bias, 4))
    for n, (which, part) in enumerate(pieces):
        inward[n].wait()
        moved.append(move(staged.at[which, part], whole[which][1].at[place(part)], 5 + n))
    for copy in moved:
        copy.wait()


def finish_call(scale, output, grad, weights, bias):
    rows, width = output.shape
    vm = pltpu.VMEM
    anywhere = pl.BlockSpec(memory_space=pl.ANY)
    square = jax.ShapeDtypeStruct((width, width), F32)
    line = jax.ShapeDtypeStruct((1, width), F32)
    return pl.pallas_call(
        functools.partial(finish_kernel, scale),
        out_shape=(
            jax.ShapeDtypeStruct(output.shape, BF16), jax.ShapeDtypeStruct(grad.shape, BF16),
            square, square, line,
        ),
        in_specs=[anywhere] * 4,
        out_specs=[anywhere] * 5,
        scratch_shapes=[
            vm(weights.shape, BF16), vm(bias.shape, F32),
            vm((width, width), F32), vm((width, width), F32), vm((1, width), F32),
            vm((2, rows // TILE, TILE, width), BF16),
            pltpu.SemaphoreType.DMA((5 + 2 * (rows // TILE),)),
        ],
        compiler_params=pltpu.CompilerParams(vmem_limit_bytes=63 * MIB),
        name="finish",
    )(output, grad, weights, bias)


def shards(groups, devs, features, weight_self, weight_neigh, bias, cotangent, hub_rows,
           halo_send, block_src, block_tgt, block_count, block_vals):
    rows, width = features.shape
    scale = 1.0 / math.sqrt(rows * groups * devs)
    block = block_vals.shape[-1]
    results = layer_call(
        hub_rows, block_count, block_src[0], block_tgt[0],
        halo_send[0, 0], features.reshape(-1, block, width), block_vals[0, 0],
        weight_self, weight_neigh, bias[None], cotangent, groups, devs, hub_rows.shape[0],
    )
    output, grad, grad_self, grad_neigh, grad_bias = finish_call(scale, *results)
    return output, grad, grad_self, grad_neigh, grad_bias.reshape(width)


def solution(mesh):
    groups, devs = mesh.shape["group"], mesh.shape["dev"]
    return jax.shard_map(
        functools.partial(shards, groups, devs),
        mesh=mesh,
        in_specs=(
            P(("group", "dev"), None),
            P(),
            P(),
            P(),
            P(("group", "dev"), None),
            P(("group", "dev")),
            P("group", "dev", None, None),
            P("group", "dev", None),
            P("group", "dev", None),
            P("group", "dev"),
            P("group", "dev", None, None, None),
        ),
        out_specs=(P(("group", "dev"), None), P(("group", "dev"), None), P(), P(), P()),
        check_vma=False,
    )
```

```python
import functools
import math
import random

import jax
import jax.numpy as jnp
from jax import lax
from jax.experimental import pallas as pl
from jax.experimental.pallas import tpu as pltpu
from jax.sharding import PartitionSpec as P

MESH = pl.DeviceIdType.MESH
LANES = 128
BF16 = jnp.bfloat16
F32 = jnp.float32
I32 = jnp.int32
FIRST = (((0,), (0,)), ((), ()))
LAST = (((1,), (1,)), ((), ()))
MIB = 1 << 20
PART = 4
UNROLL = 8
AHEAD = 24
BACK = 16
ROWS_OF_PLAN = 8
TILE = 512
LOW = 256


def send_order(devs):
    ys = devs // 8
    every = [(y, x, c) for y in range(ys) for x in range(4) for c in range(2)][1:]
    draw = random.Random(1)
    draw.shuffle(every)
    other = [(-y % ys, -x % 4, c) for y, x, c in every]
    return every, other


class Place:
    def __init__(self, me, devs):
        self.me = me
        self.ys = devs // 8
        self.y = lax.div(me, 8)
        self.x = lax.rem(lax.div(me, 2), 4)
        self.core = lax.rem(me, 2)
        self.mate = me + 1 - 2 * self.core
        self.chip = lax.div(me, 2)
        self.plans = send_order(devs)

    def at(self, offset, sign):
        y, x, c = offset
        y, x = (y, x) if sign > 0 else (self.ys - y, 4 - x)
        return (
            lax.rem(self.y + y, self.ys) * 8
            + lax.rem(self.x + x, 4) * 2
            + lax.rem(self.core + c, 2)
        )

    def target(self, n):
        first, second = self.plans
        return jnp.where(self.core == 0, self.at(first[n], 1), self.at(second[n], 1))

    def source(self, n):
        first, second = self.plans
        sender = lax.rem(self.core + first[n][2], 2)
        return jnp.where(sender == 0, self.at(first[n], -1), self.at(second[n], -1))

    def across(self, n):
        chips = 4 * self.ys
        return lax.rem(self.chip + n, chips) * 2 + self.core


def column_of(row, size):
    return jnp.broadcast_to(row, (size, size)).T


def slot_plan(key, other, count, limit):
    size = key.shape[1]
    down = lax.broadcasted_iota(I32, (size, size), 0)
    along = lax.broadcasted_iota(I32, (size, size), 1)
    live = down < count
    keys = column_of(key, size)
    others = column_of(other, size)

    def total(mask, value=1):
        return jnp.sum(jnp.where(mask, value, 0), axis=0, keepdims=True)

    earlier = (keys == key) & (down < along)
    rank = total(earlier & live)
    odd = rank & 1
    ranks = column_of(rank, size)
    odds = ranks & 1
    heads = live & (odds == 0)
    pair = total(heads & ((keys < key) | earlier)) - odd
    pairs = column_of(pair, size)
    match = live & (pairs == along)
    left = match & (odds == 0)
    right = match & (odds == 1)
    has_right = total(right)
    return [
        total(left, down),
        total(right, down) + (1 - has_right) * size,
        total(left, others),
        total(right, others),
        1 - total(match & (ranks == 0)),
        total(heads & (keys <= along)) * jnp.minimum(total(live & (keys == along)), 1),
    ]


def layer_kernel(
    groups, devs,
    hub_rows, counts, src_hbm, tgt_hbm, lists_hbm, feat_hbm, vals_hbm, ws_hbm, wn_hbm, bias_hbm, cot_hbm,
    output_hbm, grad_hbm, wout, bias_out,
    src_v, tgt_v, output, grad, bias_sum, wide, lists, vals, turned, ws, wn, bias, cot,
    table, runs, own_pre, dpre_ref, dagg, acc,
    halo_out, halo_back, halo_in, hub_row, hub_pair, hub_send, hub_plane,
    pair_out, pair_in, z_out, z_in, row_out, row_in, wsend, wmate, wpair, w_in, wz_in, wfin,
    plan_v, plan_s,
    local, h_send, h_recv, m_sem, a_send, a_recv, z_send, z_recv, c_send, c_recv,
    g_send, g_recv, p_sem, s_send, s_recv, r_send, r_recv,
    w_send, w_recv, y_send, y_recv, f_send, f_recv,
):
    group = lax.axis_index("group")
    me = lax.axis_index("dev")
    here = Place(me, devs)
    core, mate, chip = here.core, here.mate, here.chip
    blocks, block, width = table.shape
    own_blocks = feat_hbm.shape[0]
    rows = own_blocks * block
    hub_start = own_blocks + devs
    capacity = vals_hbm.shape[0]
    share = hub_row.shape[0]
    chips = devs // 2
    messages = devs - 1

    def fetch(src, dst, which):
        copy = pltpu.make_async_copy(src, dst, local.at[which])
        copy.start()
        return copy

    early = [
        fetch(feat_hbm, table.at[pl.ds(0, own_blocks)], 0),
        fetch(lists_hbm, lists, 1),
    ]

    def to_plane(src, dst, send, recv, peer):
        return pltpu.make_async_remote_copy(
            src_ref=src, dst_ref=dst, send_sem=send, recv_sem=recv,
            device_id={"dev": peer}, device_id_type=MESH,
        )

    def to_column(src, dst, send, recv, peer):
        return pltpu.make_async_remote_copy(
            src_ref=src, dst_ref=dst, send_sem=send, recv_sem=recv,
            device_id={"group": peer}, device_id_type=MESH,
        )

    def above(step):
        return lax.rem(group + step, groups)

    barrier = pltpu.get_barrier_semaphore()
    for n in range(messages):
        pl.semaphore_signal(
            barrier, inc=1, device_id={"dev": here.target(n)}, device_id_type=MESH
        )
    for step in range(1, groups):
        pl.semaphore_signal(
            barrier, inc=1, device_id={"group": above(step)}, device_id_type=MESH
        )
    for copy in early:
        copy.wait()
    late = [
        fetch(vals_hbm, vals.at[pl.ds(0, capacity)], 3),
        fetch(ws_hbm, ws, 4),
        fetch(wn_hbm, wn, 5),
        fetch(bias_hbm, bias, 6),
        fetch(cot_hbm, cot, 7),
        fetch(src_hbm, src_v, 2),
        fetch(tgt_hbm, tgt_v, 9),
    ]

    lane = lax.broadcasted_iota(I32, (block, LANES), 1)
    owned = pl.ds(0, own_blocks)

    def onehot(column):
        low = column & (LOW - 1)
        high = lax.shift_right_logical(column, 8).astype(F32).astype(BF16)
        high = jnp.concatenate([high] * (LOW // LANES), axis=1)
        ones = jnp.concatenate(
            [
                jnp.where(low == lane[: column.shape[0]] + LANES * r, 1.0, 0.0)
                for r in range(LOW // LANES)
            ],
            axis=1,
        ).astype(BF16)
        none = jnp.zeros_like(ones)
        return jnp.concatenate(
            [jnp.where(high == float(t), ones, none) for t in range(rows // LOW)], axis=1
        )

    def pick(matrix):
        return jnp.dot(matrix, table[owned].reshape(rows, width), preferred_element_type=F32)

    def fill(low, high):
        parts = [
            onehot(column_of(lists[pl.ds(here.target(n), 1), :], block))
            for n in range(low, high)
        ]
        got = pick(jnp.concatenate(parts, axis=0)).astype(BF16)
        halo_out[pl.ds(low, high - low)] = got.reshape(high - low, block, width)

    def halo_copy(n):
        return to_plane(
            halo_out.at[n], table.at[own_blocks + me], h_send.at[n], h_recv.at[me], here.target(n)
        )

    def from_plane(dst, send, recv, peer):
        return to_plane(dst, dst, send, recv, peer)

    starts = [0, 2] + list(range(2 + PART, messages, PART))
    spans = list(zip(starts, starts[1:] + [messages]))

    def ship(span):
        for n in range(*span):
            halo_copy(n).start()

    hub_mate = to_plane(hub_row, hub_pair.at[core], m_sem.at[0], m_sem.at[1], mate)

    def hub_spread(n):
        return to_plane(
            hub_send, hub_plane.at[chip], a_send.at[n], a_recv.at[chip], here.across(n)
        )

    def hub_block(owner, side):
        return table.at[hub_start + owner * 2 + side]

    half_chips = chips // 2

    def hub_up(step):
        return to_column(
            hub_plane.at[pl.ds(core * half_chips, half_chips)],
            hub_in_table(group, core),
            z_send.at[step], z_recv.at[group], above(step),
        )

    def hub_in_table(owner, side):
        return hub_table.at[pl.ds((owner * 2 + side) * half_chips, half_chips)]

    hub_table = table.at[pl.ds(hub_start, blocks - hub_start)].reshape(
        (blocks - hub_start) * half_chips, 2 * share, width
    )

    fill(*spans[0])
    pl.semaphore_wait(barrier, devs + groups - 2)
    ship(spans[0])
    hub_ids = jnp.full((1, block), rows, I32)
    for k in range(share):
        hub_ids = jnp.where((lane[:1] == k) | (lane[:1] == k + share), hub_rows[k], hub_ids)
    picked = pick(onehot(column_of(hub_ids, block)[: 2 * share]))[:share]
    hub_row[...] = picked
    hub_pair[core] = picked
    hub_mate.start()
    fill(*spans[1])

    hub_mate.wait_recv()
    both = hub_pair[...].reshape(2 * share, width).astype(BF16)
    hub_send[...] = both
    hub_plane[chip] = both
    spreads = core == lax.div(chip, half_chips)

    @pl.when(spreads)
    def _():
        for n in range(1, chips):
            hub_spread(n).start()

    ship(spans[1])

    for span in spans[2:]:
        fill(*span)
        ship(span)

    for n in range(half_chips):
        source = core * half_chips + n

        @pl.when(source != chip)
        def _():
            from_plane(hub_plane.at[source], a_send.at[n], a_recv.at[source], mate).wait_recv()

    for step in range(1, groups):
        hub_up(step).start()
    hub_table[pl.ds((group * 2 + core) * half_chips, half_chips)] = hub_plane[
        pl.ds(core * half_chips, half_chips)
    ]

    def hub_over(owner):
        part = hub_in_table(owner, core)
        return to_plane(part, part, c_send.at[owner], c_recv.at[owner], mate)

    hub_over(group).start()

    for copy in late:
        copy.wait()
    count = counts[0, 0]
    src = src_v[...]
    tgt = tgt_v[...]
    ahead = slot_plan(tgt, src, count, own_blocks)
    back = slot_plan(lax.rem(src + blocks - own_blocks, blocks), tgt, count, blocks)
    for at, row in enumerate(ahead):
        plan_v[pl.ds(at, 1), :] = row
    for at, row in enumerate(back):
        plan_v[pl.ds(ROWS_OF_PLAN + at, 1), :] = row
    plan_copy = fetch(plan_v, plan_s, 8)
    table[own_blocks + me] = jnp.zeros((block, width), BF16)
    vals[capacity] = jnp.zeros((block, block), BF16)
    turned[capacity] = jnp.zeros((block, block), BF16)
    runs[0] = jnp.zeros((block, width), F32)
    wide[pl.ds(2 * width, 16), :] = jnp.ones((16, rows), BF16)

    def turn(step, _):
        for u in range(UNROLL):
            k = step * UNROLL + u
            turned[k] = vals[k].T
        return _

    lax.fori_loop(0, capacity // UNROLL, turn, 0)

    def span_of(t):
        return pl.ds(pl.multiple_of(t * 2 * block, 2 * block), 2 * block)

    def own_part(t, _):
        own = table[pl.ds(t * 2, 2)].reshape(2 * block, width)
        own_pre[span_of(t), :] = (
            jnp.dot(own, ws[...], preferred_element_type=F32) + bias[...]
        )
        wide[pl.ds(0, width), span_of(t)] = own.T
        return _

    lax.fori_loop(0, own_blocks // 2, own_part, 0)
    plan_copy.wait()

    def pass_on(step):
        owner = lax.rem(group + groups - step, groups)
        part = hub_in_table(owner, core)
        to_column(part, part, z_send.at[step], z_recv.at[owner], owner).wait_recv()
        hub_over(owner).start()

    for step in range(1, groups):
        pass_on(step)

    for step in range(groups):
        owner = lax.rem(group + groups - step, groups)
        got = hub_in_table(owner, 1 - core)
        hub_over(owner).wait_send()
        to_plane(got, got, c_send.at[owner], c_recv.at[owner], mate).wait_recv()
    for n in range(messages):
        source = here.source(n)
        from_plane(
            table.at[own_blocks + source], h_send.at[n], h_recv.at[source], source
        ).wait_recv()

    def run_totals(low, high, unroll, start, row, weights, tiles):
        def body(step, total):
            for u in range(unroll):
                p = step * unroll + u
                left = jnp.concatenate(
                    [weights[plan_s[row, p]], weights[plan_s[row + 1, p]]], axis=1
                )
                right = jnp.concatenate(
                    [tiles[plan_s[row + 2, p]], tiles[plan_s[row + 3, p]]], axis=0
                )
                total = total * plan_s[row + 4, p].astype(F32) + jnp.dot(
                    left, right, preferred_element_type=F32
                )
                runs[p + 1] = total
            return total

        return lax.fori_loop(low, high, body, start)

    nothing = jnp.zeros((block, width), F32)
    run_totals(0, pl.cdiv(capacity + own_blocks, 2 * AHEAD), AHEAD, nothing, 0, vals, table)

    def dense_part(t):
        at = span_of(t)
        near = jnp.concatenate(
            [runs[plan_s[5, t * 2]], runs[plan_s[5, t * 2 + 1]]], axis=0
        ).astype(BF16)
        wide[pl.ds(width, width), at] = near.T
        pre = own_pre[at, :] + jnp.dot(near, wn[...], preferred_element_type=F32)
        sigmoid = 0.5 * jnp.tanh(0.5 * pre) + 0.5
        result = pre * sigmoid
        output[at, :] = result.astype(BF16)
        slope = sigmoid + result * (1.0 - sigmoid)
        dpre = (cot[at, :].astype(F32) * slope).astype(BF16)
        dpre_ref[at, :] = dpre
        dagg[pl.ds(t * 2, 2)] = (
            lax.dot_general(dpre, wn[...], LAST, preferred_element_type=F32)
            .astype(BF16)
            .reshape(2, block, width)
        )

    def dense(step, _):
        for u in range(4):
            dense_part(step * 4 + u)
        return _

    lax.fori_loop(0, own_blocks // 8, dense, 0)
    output_copy = fetch(output, output_hbm, 10)

    sums = jnp.dot(wide[...], dpre_ref[...], preferred_element_type=F32)
    part_rows = wsend.shape[2]
    wsend[:, :, :, pl.ds(0, width)] = (
        sums[: 2 * width].astype(BF16).reshape(2, chips, part_rows, width)
    )
    line = lax.broadcasted_iota(I32, (part_rows, LANES), 0)
    gbias = sums[2 * width : 2 * width + 1]
    gbias = jnp.where(line == 0, gbias[:, :LANES], jnp.where(line == 1, gbias[:, LANES:], 0.0))
    wsend[:, :, :, pl.ds(width, LANES)] = jnp.broadcast_to(
        gbias.astype(BF16)[None, None], (2, chips, part_rows, LANES)
    )
    w_mate = to_plane(wsend.at[1 - core], wmate, m_sem.at[2], m_sem.at[3], mate)
    w_mate.start()
    def backward(low, high, start):
        return run_totals(low, high, BACK, start, ROWS_OF_PLAN, turned, dagg)

    halo_steps = pl.cdiv(capacity + devs, 2 * BACK)
    early_steps = halo_steps // 2
    reached = backward(0, early_steps, nothing)
    w_mate.wait_recv()
    wpair[...] = (wsend[core].astype(F32) + wmate[...].astype(F32)).astype(BF16)

    def w_copy(n):
        target = here.across(n)
        return to_plane(
            wpair.at[lax.div(target, 2)], w_in.at[chip], w_send.at[n], w_recv.at[chip], target
        )

    for n in range(1, chips):
        w_copy(n).start()
    w_in[chip] = wpair[chip]
    reached = backward(early_steps, halo_steps, reached)

    def dtable(key):
        return runs[plan_s[ROWS_OF_PLAN + 5, key]]

    hub_key, own_key = devs, blocks - own_blocks

    def back_copy(n):
        return to_plane(halo_back.at[n], halo_in.at[me], g_send.at[n], g_recv.at[me], here.target(n))

    for n in range(messages):
        halo_back[n] = dtable(here.target(n)).astype(BF16)
        back_copy(n).start()
    backward(halo_steps, pl.cdiv(capacity + blocks, 2 * BACK), reached)
    for k in range(groups):
        pair_out[k] = dtable(hub_key + 2 * k + 1 - core).astype(BF16)
    pair = to_plane(pair_out, pair_in, p_sem.at[0], p_sem.at[1], mate)
    pair.start()

    for n in range(1, chips):
        source = here.across(n)
        at = lax.div(source, 2)
        from_plane(w_in.at[at], w_send.at[n], w_recv.at[at], source).wait_recv()
    wz_in[group] = jnp.sum(w_in[...].astype(F32), axis=0).astype(BF16)

    def y_copy(step):
        return to_column(
            wz_in.at[group], wz_in.at[group], y_send.at[step], y_recv.at[group], above(step)
        )

    for step in range(1, groups):
        y_copy(step).start()

    def begin(t, _):
        at = span_of(t)
        own = jnp.concatenate(
            [dtable(own_key + t * 2), dtable(own_key + t * 2 + 1)], axis=0
        )
        acc[at, :] = own + lax.dot_general(
            dpre_ref[at, :], ws[...], LAST, preferred_element_type=F32
        )
        return _

    lax.fori_loop(0, own_blocks // 2, begin, 0)

    for n in range(messages):
        halo_copy(n).wait_send()
    pair.wait_recv()
    for k in range(groups):
        z_out[k] = (dtable(hub_key + 2 * k + core) + pair_in[k].astype(F32)).astype(BF16)

    def s_copy(step):
        return to_column(
            z_out.at[above(step)], z_in.at[group], s_send.at[step], s_recv.at[group], above(step)
        )

    for step in range(1, groups):
        s_copy(step).start()
    z_in[group] = z_out[group]

    for step in range(1, groups):
        peer = above(step)
        to_column(
            wz_in.at[peer], wz_in.at[peer], y_send.at[step], y_recv.at[peer], peer
        ).wait_recv()
    total = jnp.sum(wz_in[...].astype(F32), axis=0)
    wfin[core, chip] = total[:, :width].astype(BF16)
    bias_sum[...] = total[:8, width:]
    bias_copy = fetch(bias_sum, bias_out, 11)

    def f_copy(n):
        part = wfin.at[core, chip]
        return to_plane(part, part, f_send.at[n], f_recv.at[chip], here.across(n))

    for n in range(1, chips):
        f_copy(n).start()

    def result_copy(t):
        at = pl.ds(t * TILE, TILE)
        return pltpu.make_async_copy(grad.at[at], grad_hbm.at[at], local.at[13 + t])

    def scatter(span, more_ids=(), more=(), last=False):
        ids, got = list(more_ids), list(more)
        for n in range(*span):
            source = here.source(n)
            from_plane(halo_in.at[source], g_send.at[n], g_recv.at[source], source).wait_recv()
            ids.append(lists[pl.ds(source, 1), :])
            got.append(halo_in[source])
        ids = jnp.concatenate(ids, axis=1)
        got = jnp.concatenate(got, axis=0)
        low = ids & (TILE - 1)
        node = lax.broadcasted_iota(I32, (TILE, ids.shape[1]), 0)
        ones = jnp.where(node == low, 1.0, 0.0).astype(BF16)
        for t in range(rows // TILE):
            here_too = jnp.where(ids - low == t * TILE, 1.0, 0.0).astype(BF16)
            at = pl.ds(t * TILE, TILE)
            added = acc[at, :] + jnp.dot(ones * here_too, got, preferred_element_type=F32)
            if last:
                grad[at, :] = added.astype(BF16)
                result_copy(t).start()
            else:
                acc[at, :] = added

    edges = [0, 8, 16, 24, 28, messages]
    wider = list(zip(edges[:-1], edges[1:]))
    for span in wider[:1]:
        scatter(span)

    for step in range(1, groups):
        peer = above(step)
        to_column(
            z_out.at[peer], z_in.at[peer], s_send.at[step], s_recv.at[peer], peer
        ).wait_recv()
    row_out[...] = jnp.sum(z_in[...].astype(F32), axis=0).reshape(row_out.shape)

    def row_copy(k):
        return to_plane(
            row_out.at[k], row_in.at[chip], r_send.at[k], r_recv.at[chip], core * chips + k
        )

    for k in range(chips):
        @pl.when(core * chips + k != me)
        def _():
            row_copy(k).start()

        @pl.when(core * chips + k == me)
        def _():
            row_in[chip] = row_out[k]

    scatter(wider[1])
    for n in range(1, chips):
        source = here.across(n)
        at = lax.div(source, 2)
        from_plane(wfin.at[core, at], f_send.at[n], f_recv.at[at], source).wait_recv()
    f_mate = to_plane(wfin.at[core], wfin.at[core], m_sem.at[4], m_sem.at[5], mate)
    f_mate.start()
    for span in wider[2:-1]:
        scatter(span)

    side = lax.div(me, chips)
    for k in range(chips):
        sender = k * 2 + side

        @pl.when(sender != me)
        def _():
            to_plane(row_out.at[k], row_in.at[k], r_send.at[k], r_recv.at[k], sender).wait_recv()

    hub_sum = jnp.sum(row_in[...], axis=0)
    top = hub_sum.astype(BF16).astype(F32)
    spare = jnp.zeros((block - 2 * share, width), F32)
    both = jnp.concatenate([top, hub_sum - top, spare], axis=0).astype(BF16)

    hub_mate.wait_send()
    pair.wait_send()

    @pl.when(spreads)
    def _():
        for n in range(1, chips):
            hub_spread(n).wait_send()

    for step in range(1, groups):
        hub_up(step).wait_send()
        y_copy(step).wait_send()
        s_copy(step).wait_send()
    for n in range(1, chips):
        w_copy(n).wait_send()
        f_copy(n).wait_send()
    w_mate.wait_send()
    f_mate.wait_send()
    for k in range(chips):
        @pl.when(core * chips + k != me)
        def _():
            row_copy(k).wait_send()

    other = wfin.at[1 - core]
    from_plane(other, m_sem.at[4], m_sem.at[5], mate).wait_recv()
    wout_copy = fetch(wfin, wout, 12)
    for n in range(wider[-2][0]):
        back_copy(n).wait_send()

    scatter(wider[-1], [hub_ids], [both], last=True)
    for n in range(wider[-2][0], messages):
        back_copy(n).wait_send()
    for copy in (output_copy, bias_copy, wout_copy):
        copy.wait()
    for t in range(rows // TILE):
        result_copy(t).wait()


def layer_call(hub_rows, count, src, tgt, lists, features, values, ws, wn, bias, cot, groups, devs, share):
    own_blocks, block, width = features.shape
    rows = own_blocks * block
    capacity = values.shape[0]
    hubs = groups * devs * share
    blocks = own_blocks + devs + hubs // block
    chips = devs // 2
    part_rows = width // chips
    most = max(
        AHEAD * pl.cdiv(capacity + own_blocks, 2 * AHEAD), BACK * pl.cdiv(capacity + blocks, 2 * BACK)
    )
    dma = pltpu.SemaphoreType.DMA
    vm = pltpu.VMEM
    anywhere = pl.BlockSpec(memory_space=pl.ANY)
    smem = pl.BlockSpec(memory_space=pltpu.SMEM)
    return pl.pallas_call(
        functools.partial(layer_kernel, groups, devs),
        out_shape=(
            jax.ShapeDtypeStruct((rows, width), BF16),
            jax.ShapeDtypeStruct((rows, width), BF16),
            jax.ShapeDtypeStruct((2, chips, part_rows, width), BF16),
            jax.ShapeDtypeStruct((8, LANES), F32),
        ),
        in_specs=[smem] * 2 + [anywhere] * 9,
        out_specs=[anywhere] * 4,
        scratch_shapes=[
            vm(src.shape, I32), vm(tgt.shape, I32), vm((rows, width), BF16), vm((rows, width), BF16),
            vm((8, LANES), F32), vm((2 * width + 16, rows), BF16), vm(lists.shape, I32),
            vm((capacity + 1, block, block), BF16), vm((capacity + 1, block, block), BF16),
            vm((width, width), BF16), vm((width, width), BF16), vm((1, width), F32),
            vm((rows, width), BF16),
            vm((blocks, block, width), BF16), vm((most + 1, block, width), F32),
            vm((rows, width), F32), vm((rows, width), BF16),
            vm((own_blocks, block, width), BF16), vm((rows, width), F32),
            vm((devs, block, width), BF16), vm((devs, block, width), BF16), vm((devs, block, width), BF16),
            vm((share, width), F32), vm((2, share, width), F32),
            vm((2 * share, width), BF16), vm((chips, 2 * share, width), BF16),
            vm((groups, block, width), BF16), vm((groups, block, width), BF16),
            vm((groups, block, width), BF16), vm((groups, block, width), BF16),
            vm((chips, share, width), F32), vm((chips, share, width), F32),
            vm((2, chips, part_rows, width + LANES), BF16), vm((chips, part_rows, width + LANES), BF16),
            vm((chips, part_rows, width + LANES), BF16), vm((chips, part_rows, width + LANES), BF16),
            vm((groups, part_rows, width + LANES), BF16), vm((2, chips, part_rows, width), BF16),
            vm((2 * ROWS_OF_PLAN, LANES), I32), pltpu.SMEM((2 * ROWS_OF_PLAN, LANES), I32),
            dma((13 + rows // TILE,)), dma((devs,)), dma((devs,)), dma((6,)), dma((chips,)), dma((chips,)),
            dma((groups,)), dma((groups,)), dma((groups,)), dma((groups,)),
            dma((devs,)), dma((devs,)), dma((2,)), dma((groups,)), dma((groups,)),
            dma((chips,)), dma((chips,)),
            dma((chips,)), dma((chips,)), dma((groups,)), dma((groups,)), dma((chips,)), dma((chips,)),
        ],
        compiler_params=pltpu.CompilerParams(
            collective_id=0, has_side_effects=True, vmem_limit_bytes=56 * MIB
        ),
        name="layer",
    )(hub_rows, count, src, tgt, lists, features, values, ws, wn, bias, cot)


def finish_kernel(
    scale, output_in, grad_in, weights_in, bias_in,
    output, grad, grad_self, grad_neigh, grad_bias,
    weights, sums, self_v, neigh_v, bias_v, staged, sems,
):
    def move(src, dst, which):
        copy = pltpu.make_async_copy(src, dst, sems.at[which])
        copy.start()
        return copy

    first = [move(weights_in, weights, 0), move(bias_in, sums, 1)]
    rows = staged.shape[2]
    whole = [(output_in, output), (grad_in, grad)]
    pieces = [(which, part) for part in range(staged.shape[1]) for which in range(2)]

    def place(part):
        return pl.ds(part * rows, rows)

    inward = [
        move(whole[which][0].at[place(part)], staged.at[which, part], 5 + n)
        for n, (which, part) in enumerate(pieces)
    ]
    for copy in first:
        copy.wait()
    self_v[...] = weights[0].reshape(self_v.shape).astype(F32) * scale
    moved = [move(self_v, grad_self, 2)]
    neigh_v[...] = weights[1].reshape(neigh_v.shape).astype(F32) * scale
    moved.append(move(neigh_v, grad_neigh, 3))
    bias_v[...] = jnp.concatenate([sums[pl.ds(0, 1), :], sums[pl.ds(1, 1), :]], axis=1) * scale
    moved.append(move(bias_v, grad_bias, 4))
    for n, (which, part) in enumerate(pieces):
        inward[n].wait()
        moved.append(move(staged.at[which, part], whole[which][1].at[place(part)], 5 + n))
    for copy in moved:
        copy.wait()


def finish_call(scale, output, grad, weights, bias):
    rows, width = output.shape
    vm = pltpu.VMEM
    anywhere = pl.BlockSpec(memory_space=pl.ANY)
    square = jax.ShapeDtypeStruct((width, width), F32)
    line = jax.ShapeDtypeStruct((1, width), F32)
    return pl.pallas_call(
        functools.partial(finish_kernel, scale),
        out_shape=(
            jax.ShapeDtypeStruct(output.shape, BF16), jax.ShapeDtypeStruct(grad.shape, BF16),
            square, square, line,
        ),
        in_specs=[anywhere] * 4,
        out_specs=[anywhere] * 5,
        scratch_shapes=[
            vm(weights.shape, BF16), vm(bias.shape, F32),
            vm((width, width), F32), vm((width, width), F32), vm((1, width), F32),
            vm((2, rows // TILE, TILE, width), BF16),
            pltpu.SemaphoreType.DMA((5 + 2 * (rows // TILE),)),
        ],
        compiler_params=pltpu.CompilerParams(vmem_limit_bytes=63 * MIB),
        name="finish",
    )(output, grad, weights, bias)


def shards(groups, devs, features, weight_self, weight_neigh, bias, cotangent, hub_rows,
           halo_send, block_src, block_tgt, block_count, block_vals):
    rows, width = features.shape
    scale = 1.0 / math.sqrt(rows * groups * devs)
    block = block_vals.shape[-1]
    results = layer_call(
        hub_rows, block_count, block_src[0], block_tgt[0],
        halo_send[0, 0], features.reshape(-1, block, width), block_vals[0, 0],
        weight_self, weight_neigh, bias[None], cotangent, groups, devs, hub_rows.shape[0],
    )
    output, grad, grad_self, grad_neigh, grad_bias = finish_call(scale, *results)
    return output, grad, grad_self, grad_neigh, grad_bias.reshape(width)


def solution(mesh):
    groups, devs = mesh.shape["group"], mesh.shape["dev"]
    return jax.shard_map(
        functools.partial(shards, groups, devs),
        mesh=mesh,
        in_specs=(
            P(("group", "dev"), None),
            P(),
            P(),
            P(),
            P(("group", "dev"), None),
            P(("group", "dev")),
            P("group", "dev", None, None),
            P("group", "dev", None),
            P("group", "dev", None),
            P("group", "dev"),
            P("group", "dev", None, None, None),
        ),
        out_specs=(P(("group", "dev"), None), P(("group", "dev"), None), P(), P(), P()),
        check_vma=False,
    )
```

```python
import functools
import math
import random

import jax
import jax.numpy as jnp
from jax import lax
from jax.experimental import pallas as pl
from jax.experimental.pallas import tpu as pltpu
from jax.sharding import PartitionSpec as P

MESH = pl.DeviceIdType.MESH
LANES = 128
BF16 = jnp.bfloat16
F32 = jnp.float32
I32 = jnp.int32
FIRST = (((0,), (0,)), ((), ()))
LAST = (((1,), (1,)), ((), ()))
MIB = 1 << 20
PART = 4
UNROLL = 8
AHEAD = 24
BACK = 16
ROWS_OF_PLAN = 8
TILE = 512
LOW = 256


def send_order(devs):
    ys = devs // 8
    every = [(y, x, c) for y in range(ys) for x in range(4) for c in range(2)][1:]
    draw = random.Random(1)
    draw.shuffle(every)
    other = [(-y % ys, -x % 4, c) for y, x, c in every]
    return every, other


class Place:
    def __init__(self, me, devs):
        self.me = me
        self.ys = devs // 8
        self.y = lax.div(me, 8)
        self.x = lax.rem(lax.div(me, 2), 4)
        self.core = lax.rem(me, 2)
        self.mate = me + 1 - 2 * self.core
        self.chip = lax.div(me, 2)
        self.plans = send_order(devs)

    def at(self, offset, sign):
        y, x, c = offset
        y, x = (y, x) if sign > 0 else (self.ys - y, 4 - x)
        return (
            lax.rem(self.y + y, self.ys) * 8
            + lax.rem(self.x + x, 4) * 2
            + lax.rem(self.core + c, 2)
        )

    def target(self, n):
        first, second = self.plans
        return jnp.where(self.core == 0, self.at(first[n], 1), self.at(second[n], 1))

    def source(self, n):
        first, second = self.plans
        sender = lax.rem(self.core + first[n][2], 2)
        return jnp.where(sender == 0, self.at(first[n], -1), self.at(second[n], -1))

    def across(self, n):
        chips = 4 * self.ys
        return lax.rem(self.chip + n, chips) * 2 + self.core


def column_of(row, size):
    return jnp.broadcast_to(row, (size, size)).T


def slot_plan(key, other, count, limit):
    size = key.shape[1]
    down = lax.broadcasted_iota(I32, (size, size), 0)
    along = lax.broadcasted_iota(I32, (size, size), 1)
    live = down < count
    keys = column_of(key, size)
    others = column_of(other, size)

    def total(mask, value=1):
        return jnp.sum(jnp.where(mask, value, 0), axis=0, keepdims=True)

    earlier = (keys == key) & (down < along)
    rank = total(earlier & live)
    odd = rank & 1
    ranks = column_of(rank, size)
    odds = ranks & 1
    heads = live & (odds == 0)
    pair = total(heads & ((keys < key) | earlier)) - odd
    pairs = column_of(pair, size)
    match = live & (pairs == along)
    left = match & (odds == 0)
    right = match & (odds == 1)
    has_right = total(right)
    return [
        total(left, down),
        total(right, down) + (1 - has_right) * size,
        total(left, others),
        total(right, others),
        1 - total(match & (ranks == 0)),
        total(heads & (keys <= along)) * jnp.minimum(total(live & (keys == along)), 1),
    ]


def layer_kernel(
    groups, devs,
    hub_rows, counts, src_hbm, tgt_hbm, lists_hbm, feat_hbm, vals_hbm, ws_hbm, wn_hbm, bias_hbm, cot_hbm,
    output_hbm, grad_hbm, wout, bias_out,
    src_v, tgt_v, output, grad, bias_sum, wide, lists, vals, turned, ws, wn, bias, cot,
    table, runs, own_pre, dpre_ref, dagg, acc,
    halo_out, halo_back, halo_in, hub_row, hub_pair, hub_send, hub_plane,
    pair_out, pair_in, z_out, z_in, row_out, row_in, wsend, wmate, wpair, w_in, wz_in, wfin,
    plan_v, plan_s,
    local, h_send, h_recv, m_sem, a_send, a_recv, z_send, z_recv, c_send, c_recv,
    g_send, g_recv, p_sem, s_send, s_recv, r_send, r_recv,
    w_send, w_recv, y_send, y_recv, f_send, f_recv,
):
    group = lax.axis_index("group")
    me = lax.axis_index("dev")
    here = Place(me, devs)
    core, mate, chip = here.core, here.mate, here.chip
    blocks, block, width = table.shape
    own_blocks = feat_hbm.shape[0]
    rows = own_blocks * block
    hub_start = own_blocks + devs
    capacity = vals_hbm.shape[0]
    share = hub_row.shape[0]
    chips = devs // 2
    messages = devs - 1

    def fetch(src, dst, which):
        copy = pltpu.make_async_copy(src, dst, local.at[which])
        copy.start()
        return copy

    early = [
        fetch(feat_hbm, table.at[pl.ds(0, own_blocks)], 0),
        fetch(lists_hbm, lists, 1),
    ]

    def to_plane(src, dst, send, recv, peer):
        return pltpu.make_async_remote_copy(
            src_ref=src, dst_ref=dst, send_sem=send, recv_sem=recv,
            device_id={"dev": peer}, device_id_type=MESH,
        )

    def to_column(src, dst, send, recv, peer):
        return pltpu.make_async_remote_copy(
            src_ref=src, dst_ref=dst, send_sem=send, recv_sem=recv,
            device_id={"group": peer}, device_id_type=MESH,
        )

    def above(step):
        return lax.rem(group + step, groups)

    barrier = pltpu.get_barrier_semaphore()
    for n in range(messages):
        pl.semaphore_signal(
            barrier, inc=1, device_id={"dev": here.target(n)}, device_id_type=MESH
        )
    for step in range(1, groups):
        pl.semaphore_signal(
            barrier, inc=1, device_id={"group": above(step)}, device_id_type=MESH
        )
    for copy in early:
        copy.wait()
    late = [
        fetch(vals_hbm, vals.at[pl.ds(0, capacity)], 3),
        fetch(ws_hbm, ws, 4),
        fetch(wn_hbm, wn, 5),
        fetch(bias_hbm, bias, 6),
        fetch(cot_hbm, cot, 7),
        fetch(src_hbm, src_v, 2),
        fetch(tgt_hbm, tgt_v, 9),
    ]

    lane = lax.broadcasted_iota(I32, (block, LANES), 1)
    owned = pl.ds(0, own_blocks)

    def onehot(column):
        low = column & (LOW - 1)
        high = lax.shift_right_logical(column, 8).astype(F32).astype(BF16)
        high = jnp.concatenate([high] * (LOW // LANES), axis=1)
        ones = jnp.concatenate(
            [
                jnp.where(low == lane[: column.shape[0]] + LANES * r, 1.0, 0.0)
                for r in range(LOW // LANES)
            ],
            axis=1,
        ).astype(BF16)
        none = jnp.zeros_like(ones)
        return jnp.concatenate(
            [jnp.where(high == float(t), ones, none) for t in range(rows // LOW)], axis=1
        )

    def pick(matrix):
        return jnp.dot(matrix, table[owned].reshape(rows, width), preferred_element_type=F32)

    def fill(low, high):
        parts = [
            onehot(column_of(lists[pl.ds(here.target(n), 1), :], block))
            for n in range(low, high)
        ]
        got = pick(jnp.concatenate(parts, axis=0)).astype(BF16)
        halo_out[pl.ds(low, high - low)] = got.reshape(high - low, block, width)

    def halo_copy(n):
        return to_plane(
            halo_out.at[n], table.at[own_blocks + me], h_send.at[n], h_recv.at[me], here.target(n)
        )

    def from_plane(dst, send, recv, peer):
        return to_plane(dst, dst, send, recv, peer)

    starts = [0, 2] + list(range(2 + PART, messages, PART))
    spans = list(zip(starts, starts[1:] + [messages]))

    def ship(span):
        for n in range(*span):
            halo_copy(n).start()

    hub_mate = to_plane(hub_row, hub_pair.at[core], m_sem.at[0], m_sem.at[1], mate)

    def hub_spread(n):
        return to_plane(
            hub_send, hub_plane.at[chip], a_send.at[n], a_recv.at[chip], here.across(n)
        )

    def hub_block(owner, side):
        return table.at[hub_start + owner * 2 + side]

    half_chips = chips // 2

    def hub_up(step):
        return to_column(
            hub_plane.at[pl.ds(core * half_chips, half_chips)],
            hub_in_table(group, core),
            z_send.at[step], z_recv.at[group], above(step),
        )

    def hub_in_table(owner, side):
        return hub_table.at[pl.ds((owner * 2 + side) * half_chips, half_chips)]

    hub_table = table.at[pl.ds(hub_start, blocks - hub_start)].reshape(
        (blocks - hub_start) * half_chips, 2 * share, width
    )

    fill(*spans[0])
    pl.semaphore_wait(barrier, devs + groups - 2)
    ship(spans[0])
    hub_ids = jnp.full((1, block), rows, I32)
    for k in range(share):
        hub_ids = jnp.where((lane[:1] == k) | (lane[:1] == k + share), hub_rows[k], hub_ids)
    picked = pick(onehot(column_of(hub_ids, block)[: 2 * share]))[:share]
    hub_row[...] = picked
    hub_pair[core] = picked
    hub_mate.start()
    fill(*spans[1])

    hub_mate.wait_recv()
    both = hub_pair[...].reshape(2 * share, width).astype(BF16)
    hub_send[...] = both
    hub_plane[chip] = both
    spreads = core == lax.div(chip, half_chips)

    @pl.when(spreads)
    def _():
        for n in range(1, chips):
            hub_spread(n).start()

    ship(spans[1])

    for span in spans[2:]:
        fill(*span)
        ship(span)

    for n in range(half_chips):
        source = core * half_chips + n

        @pl.when(source != chip)
        def _():
            from_plane(hub_plane.at[source], a_send.at[n], a_recv.at[source], mate).wait_recv()

    for step in range(1, groups):
        hub_up(step).start()
    hub_table[pl.ds((group * 2 + core) * half_chips, half_chips)] = hub_plane[
        pl.ds(core * half_chips, half_chips)
    ]

    def hub_over(owner):
        part = hub_in_table(owner, core)
        return to_plane(part, part, c_send.at[owner], c_recv.at[owner], mate)

    hub_over(group).start()

    for copy in late:
        copy.wait()
    count = counts[0, 0]
    src = src_v[...]
    tgt = tgt_v[...]
    ahead = slot_plan(tgt, src, count, own_blocks)
    back = slot_plan(lax.rem(src + blocks - own_blocks, blocks), tgt, count, blocks)
    for at, row in enumerate(ahead):
        plan_v[pl.ds(at, 1), :] = row
    for at, row in enumerate(back):
        plan_v[pl.ds(ROWS_OF_PLAN + at, 1), :] = row
    plan_copy = fetch(plan_v, plan_s, 8)
    table[own_blocks + me] = jnp.zeros((block, width), BF16)
    vals[capacity] = jnp.zeros((block, block), BF16)
    turned[capacity] = jnp.zeros((block, block), BF16)
    runs[0] = jnp.zeros((block, width), F32)
    wide[pl.ds(2 * width, 16), :] = jnp.ones((16, rows), BF16)

    def turn(step, _):
        for u in range(UNROLL):
            k = step * UNROLL + u
            turned[k] = vals[k].T
        return _

    lax.fori_loop(0, capacity // UNROLL, turn, 0)

    def span_of(t):
        return pl.ds(pl.multiple_of(t * 2 * block, 2 * block), 2 * block)

    def own_part(t, _):
        own = table[pl.ds(t * 2, 2)].reshape(2 * block, width)
        own_pre[span_of(t), :] = (
            jnp.dot(own, ws[...], preferred_element_type=F32) + bias[...]
        )
        wide[pl.ds(0, width), span_of(t)] = own.T
        return _

    lax.fori_loop(0, own_blocks // 2, own_part, 0)
    plan_copy.wait()

    def pass_on(step):
        owner = lax.rem(group + groups - step, groups)
        part = hub_in_table(owner, core)
        to_column(part, part, z_send.at[step], z_recv.at[owner], owner).wait_recv()
        hub_over(owner).start()

    for step in range(1, groups):
        pass_on(step)

    for step in range(groups):
        owner = lax.rem(group + groups - step, groups)
        got = hub_in_table(owner, 1 - core)
        hub_over(owner).wait_send()
        to_plane(got, got, c_send.at[owner], c_recv.at[owner], mate).wait_recv()
    for n in range(messages):
        source = here.source(n)
        from_plane(
            table.at[own_blocks + source], h_send.at[n], h_recv.at[source], source
        ).wait_recv()

    def run_totals(low, high, unroll, start, row, weights, tiles):
        def body(step, total):
            for u in range(unroll):
                p = step * unroll + u
                left = jnp.concatenate(
                    [weights[plan_s[row, p]], weights[plan_s[row + 1, p]]], axis=1
                )
                right = jnp.concatenate(
                    [tiles[plan_s[row + 2, p]], tiles[plan_s[row + 3, p]]], axis=0
                )
                total = total * plan_s[row + 4, p].astype(F32) + jnp.dot(
                    left, right, preferred_element_type=F32
                )
                runs[p + 1] = total
            return total

        return lax.fori_loop(low, high, body, start)

    nothing = jnp.zeros((block, width), F32)
    run_totals(0, pl.cdiv(capacity + own_blocks, 2 * AHEAD), AHEAD, nothing, 0, vals, table)

    def dense_part(t):
        at = span_of(t)
        near = jnp.concatenate(
            [runs[plan_s[5, t * 2]], runs[plan_s[5, t * 2 + 1]]], axis=0
        ).astype(BF16)
        wide[pl.ds(width, width), at] = near.T
        pre = own_pre[at, :] + jnp.dot(near, wn[...], preferred_element_type=F32)
        sigmoid = 0.5 * jnp.tanh(0.5 * pre) + 0.5
        result = pre * sigmoid
        output[at, :] = result.astype(BF16)
        slope = sigmoid + result * (1.0 - sigmoid)
        dpre = (cot[at, :].astype(F32) * slope).astype(BF16)
        dpre_ref[at, :] = dpre
        dagg[pl.ds(t * 2, 2)] = (
            lax.dot_general(dpre, wn[...], LAST, preferred_element_type=F32)
            .astype(BF16)
            .reshape(2, block, width)
        )

    def dense(step, _):
        for u in range(4):
            dense_part(step * 4 + u)
        return _

    lax.fori_loop(0, own_blocks // 8, dense, 0)
    output_copy = fetch(output, output_hbm, 10)

    def backward(low, high, start):
        return run_totals(low, high, BACK, start, ROWS_OF_PLAN, turned, dagg)

    halo_steps = pl.cdiv(capacity + devs, 2 * BACK)
    reached = backward(0, halo_steps, nothing)

    def dtable(key):
        return runs[plan_s[ROWS_OF_PLAN + 5, key]]

    hub_key, own_key = devs, blocks - own_blocks

    def back_copy(n):
        return to_plane(halo_back.at[n], halo_in.at[me], g_send.at[n], g_recv.at[me], here.target(n))

    for n in range(messages):
        halo_back[n] = dtable(here.target(n)).astype(BF16)
        back_copy(n).start()
    backward(halo_steps, pl.cdiv(capacity + blocks, 2 * BACK), reached)
    for k in range(groups):
        pair_out[k] = dtable(hub_key + 2 * k + 1 - core).astype(BF16)
    pair = to_plane(pair_out, pair_in, p_sem.at[0], p_sem.at[1], mate)
    pair.start()

    sums = jnp.dot(wide[...], dpre_ref[...], preferred_element_type=F32)
    part_rows = wsend.shape[2]
    wsend[:, :, :, pl.ds(0, width)] = (
        sums[: 2 * width].astype(BF16).reshape(2, chips, part_rows, width)
    )
    line = lax.broadcasted_iota(I32, (part_rows, LANES), 0)
    gbias = sums[2 * width : 2 * width + 1]
    gbias = jnp.where(line == 0, gbias[:, :LANES], jnp.where(line == 1, gbias[:, LANES:], 0.0))
    wsend[:, :, :, pl.ds(width, LANES)] = jnp.broadcast_to(
        gbias.astype(BF16)[None, None], (2, chips, part_rows, LANES)
    )
    w_mate = to_plane(wsend.at[1 - core], wmate, m_sem.at[2], m_sem.at[3], mate)
    w_mate.start()
    def begin(t, _):
        at = span_of(t)
        own = jnp.concatenate(
            [dtable(own_key + t * 2), dtable(own_key + t * 2 + 1)], axis=0
        )
        acc[at, :] = own + lax.dot_general(
            dpre_ref[at, :], ws[...], LAST, preferred_element_type=F32
        )
        return _

    lax.fori_loop(0, own_blocks // 2, begin, 0)

    pair.wait_recv()
    for k in range(groups):
        z_out[k] = (dtable(hub_key + 2 * k + core) + pair_in[k].astype(F32)).astype(BF16)

    def s_copy(step):
        return to_column(
            z_out.at[above(step)], z_in.at[group], s_send.at[step], s_recv.at[group], above(step)
        )

    for step in range(1, groups):
        s_copy(step).start()
    z_in[group] = z_out[group]

    w_mate.wait_recv()
    wpair[...] = (wsend[core].astype(F32) + wmate[...].astype(F32)).astype(BF16)

    def w_copy(n):
        target = here.across(n)
        return to_plane(
            wpair.at[lax.div(target, 2)], w_in.at[chip], w_send.at[n], w_recv.at[chip], target
        )

    for n in range(1, chips):
        w_copy(n).start()
    w_in[chip] = wpair[chip]

    for n in range(messages):
        halo_copy(n).wait_send()

    for n in range(1, chips):
        source = here.across(n)
        at = lax.div(source, 2)
        from_plane(w_in.at[at], w_send.at[n], w_recv.at[at], source).wait_recv()
    wz_in[group] = jnp.sum(w_in[...].astype(F32), axis=0).astype(BF16)

    def y_copy(step):
        return to_column(
            wz_in.at[group], wz_in.at[group], y_send.at[step], y_recv.at[group], above(step)
        )

    for step in range(1, groups):
        y_copy(step).start()


    for step in range(1, groups):
        peer = above(step)
        to_column(
            wz_in.at[peer], wz_in.at[peer], y_send.at[step], y_recv.at[peer], peer
        ).wait_recv()
    total = jnp.sum(wz_in[...].astype(F32), axis=0)
    wfin[core, chip] = total[:, :width].astype(BF16)
    bias_sum[...] = total[:8, width:]
    bias_copy = fetch(bias_sum, bias_out, 11)

    def f_copy(n):
        part = wfin.at[core, chip]
        return to_plane(part, part, f_send.at[n], f_recv.at[chip], here.across(n))

    for n in range(1, chips):
        f_copy(n).start()

    def result_copy(t):
        at = pl.ds(t * TILE, TILE)
        return pltpu.make_async_copy(grad.at[at], grad_hbm.at[at], local.at[13 + t])

    def scatter(span, more_ids=(), more=(), last=False):
        ids, got = list(more_ids), list(more)
        for n in range(*span):
            source = here.source(n)
            from_plane(halo_in.at[source], g_send.at[n], g_recv.at[source], source).wait_recv()
            ids.append(lists[pl.ds(source, 1), :])
            got.append(halo_in[source])
        ids = jnp.concatenate(ids, axis=1)
        got = jnp.concatenate(got, axis=0)
        low = ids & (TILE - 1)
        node = lax.broadcasted_iota(I32, (TILE, ids.shape[1]), 0)
        ones = jnp.where(node == low, 1.0, 0.0).astype(BF16)
        for t in range(rows // TILE):
            here_too = jnp.where(ids - low == t * TILE, 1.0, 0.0).astype(BF16)
            at = pl.ds(t * TILE, TILE)
            added = acc[at, :] + jnp.dot(ones * here_too, got, preferred_element_type=F32)
            if last:
                grad[at, :] = added.astype(BF16)
                result_copy(t).start()
            else:
                acc[at, :] = added

    edges = [0, 8, 16, 24, 28, messages]
    wider = list(zip(edges[:-1], edges[1:]))
    for step in range(1, groups):
        peer = above(step)
        to_column(
            z_out.at[peer], z_in.at[peer], s_send.at[step], s_recv.at[peer], peer
        ).wait_recv()
    row_out[...] = jnp.sum(z_in[...].astype(F32), axis=0).reshape(row_out.shape)

    def row_copy(k):
        return to_plane(
            row_out.at[k], row_in.at[chip], r_send.at[k], r_recv.at[chip], core * chips + k
        )

    for k in range(chips):
        @pl.when(core * chips + k != me)
        def _():
            row_copy(k).start()

        @pl.when(core * chips + k == me)
        def _():
            row_in[chip] = row_out[k]

    for span in wider[:2]:
        scatter(span)
    for n in range(1, chips):
        source = here.across(n)
        at = lax.div(source, 2)
        from_plane(wfin.at[core, at], f_send.at[n], f_recv.at[at], source).wait_recv()
    f_mate = to_plane(wfin.at[core], wfin.at[core], m_sem.at[4], m_sem.at[5], mate)
    f_mate.start()
    for span in wider[2:-1]:
        scatter(span)

    side = lax.div(me, chips)
    for k in range(chips):
        sender = k * 2 + side

        @pl.when(sender != me)
        def _():
            to_plane(row_out.at[k], row_in.at[k], r_send.at[k], r_recv.at[k], sender).wait_recv()

    hub_sum = jnp.sum(row_in[...], axis=0)
    top = hub_sum.astype(BF16).astype(F32)
    spare = jnp.zeros((block - 2 * share, width), F32)
    both = jnp.concatenate([top, hub_sum - top, spare], axis=0).astype(BF16)

    hub_mate.wait_send()
    pair.wait_send()

    @pl.when(spreads)
    def _():
        for n in range(1, chips):
            hub_spread(n).wait_send()

    for step in range(1, groups):
        hub_up(step).wait_send()
        y_copy(step).wait_send()
        s_copy(step).wait_send()
    for n in range(1, chips):
        w_copy(n).wait_send()
        f_copy(n).wait_send()
    w_mate.wait_send()
    f_mate.wait_send()
    for k in range(chips):
        @pl.when(core * chips + k != me)
        def _():
            row_copy(k).wait_send()

    other = wfin.at[1 - core]
    from_plane(other, m_sem.at[4], m_sem.at[5], mate).wait_recv()
    wout_copy = fetch(wfin, wout, 12)
    for n in range(wider[-2][0]):
        back_copy(n).wait_send()

    scatter(wider[-1], [hub_ids], [both], last=True)
    for n in range(wider[-2][0], messages):
        back_copy(n).wait_send()
    for copy in (output_copy, bias_copy, wout_copy):
        copy.wait()
    for t in range(rows // TILE):
        result_copy(t).wait()


def layer_call(hub_rows, count, src, tgt, lists, features, values, ws, wn, bias, cot, groups, devs, share):
    own_blocks, block, width = features.shape
    rows = own_blocks * block
    capacity = values.shape[0]
    hubs = groups * devs * share
    blocks = own_blocks + devs + hubs // block
    chips = devs // 2
    part_rows = width // chips
    most = max(
        AHEAD * pl.cdiv(capacity + own_blocks, 2 * AHEAD), BACK * pl.cdiv(capacity + blocks, 2 * BACK)
    )
    dma = pltpu.SemaphoreType.DMA
    vm = pltpu.VMEM
    anywhere = pl.BlockSpec(memory_space=pl.ANY)
    smem = pl.BlockSpec(memory_space=pltpu.SMEM)
    return pl.pallas_call(
        functools.partial(layer_kernel, groups, devs),
        out_shape=(
            jax.ShapeDtypeStruct((rows, width), BF16),
            jax.ShapeDtypeStruct((rows, width), BF16),
            jax.ShapeDtypeStruct((2, chips, part_rows, width), BF16),
            jax.ShapeDtypeStruct((8, LANES), F32),
        ),
        in_specs=[smem] * 2 + [anywhere] * 9,
        out_specs=[anywhere] * 4,
        scratch_shapes=[
            vm(src.shape, I32), vm(tgt.shape, I32), vm((rows, width), BF16), vm((rows, width), BF16),
            vm((8, LANES), F32), vm((2 * width + 16, rows), BF16), vm(lists.shape, I32),
            vm((capacity + 1, block, block), BF16), vm((capacity + 1, block, block), BF16),
            vm((width, width), BF16), vm((width, width), BF16), vm((1, width), F32),
            vm((rows, width), BF16),
            vm((blocks, block, width), BF16), vm((most + 1, block, width), F32),
            vm((rows, width), F32), vm((rows, width), BF16),
            vm((own_blocks, block, width), BF16), vm((rows, width), F32),
            vm((devs, block, width), BF16), vm((devs, block, width), BF16), vm((devs, block, width), BF16),
            vm((share, width), F32), vm((2, share, width), F32),
            vm((2 * share, width), BF16), vm((chips, 2 * share, width), BF16),
            vm((groups, block, width), BF16), vm((groups, block, width), BF16),
            vm((groups, block, width), BF16), vm((groups, block, width), BF16),
            vm((chips, share, width), F32), vm((chips, share, width), F32),
            vm((2, chips, part_rows, width + LANES), BF16), vm((chips, part_rows, width + LANES), BF16),
            vm((chips, part_rows, width + LANES), BF16), vm((chips, part_rows, width + LANES), BF16),
            vm((groups, part_rows, width + LANES), BF16), vm((2, chips, part_rows, width), BF16),
            vm((2 * ROWS_OF_PLAN, LANES), I32), pltpu.SMEM((2 * ROWS_OF_PLAN, LANES), I32),
            dma((13 + rows // TILE,)), dma((devs,)), dma((devs,)), dma((6,)), dma((chips,)), dma((chips,)),
            dma((groups,)), dma((groups,)), dma((groups,)), dma((groups,)),
            dma((devs,)), dma((devs,)), dma((2,)), dma((groups,)), dma((groups,)),
            dma((chips,)), dma((chips,)),
            dma((chips,)), dma((chips,)), dma((groups,)), dma((groups,)), dma((chips,)), dma((chips,)),
        ],
        compiler_params=pltpu.CompilerParams(
            collective_id=0, has_side_effects=True, vmem_limit_bytes=56 * MIB
        ),
        name="layer",
    )(hub_rows, count, src, tgt, lists, features, values, ws, wn, bias, cot)


def finish_kernel(
    scale, output_in, grad_in, weights_in, bias_in,
    output, grad, grad_self, grad_neigh, grad_bias,
    weights, sums, self_v, neigh_v, bias_v, staged, sems,
):
    def move(src, dst, which):
        copy = pltpu.make_async_copy(src, dst, sems.at[which])
        copy.start()
        return copy

    first = [move(weights_in, weights, 0), move(bias_in, sums, 1)]
    rows = staged.shape[2]
    whole = [(output_in, output), (grad_in, grad)]
    pieces = [(which, part) for part in range(staged.shape[1]) for which in range(2)]

    def place(part):
        return pl.ds(part * rows, rows)

    inward = [
        move(whole[which][0].at[place(part)], staged.at[which, part], 5 + n)
        for n, (which, part) in enumerate(pieces)
    ]
    for copy in first:
        copy.wait()
    self_v[...] = weights[0].reshape(self_v.shape).astype(F32) * scale
    moved = [move(self_v, grad_self, 2)]
    neigh_v[...] = weights[1].reshape(neigh_v.shape).astype(F32) * scale
    moved.append(move(neigh_v, grad_neigh, 3))
    bias_v[...] = jnp.concatenate([sums[pl.ds(0, 1), :], sums[pl.ds(1, 1), :]], axis=1) * scale
    moved.append(move(bias_v, grad_bias, 4))
    for n, (which, part) in enumerate(pieces):
        inward[n].wait()
        moved.append(move(staged.at[which, part], whole[which][1].at[place(part)], 5 + n))
    for copy in moved:
        copy.wait()


def finish_call(scale, output, grad, weights, bias):
    rows, width = output.shape
    vm = pltpu.VMEM
    anywhere = pl.BlockSpec(memory_space=pl.ANY)
    square = jax.ShapeDtypeStruct((width, width), F32)
    line = jax.ShapeDtypeStruct((1, width), F32)
    return pl.pallas_call(
        functools.partial(finish_kernel, scale),
        out_shape=(
            jax.ShapeDtypeStruct(output.shape, BF16), jax.ShapeDtypeStruct(grad.shape, BF16),
            square, square, line,
        ),
        in_specs=[anywhere] * 4,
        out_specs=[anywhere] * 5,
        scratch_shapes=[
            vm(weights.shape, BF16), vm(bias.shape, F32),
            vm((width, width), F32), vm((width, width), F32), vm((1, width), F32),
            vm((2, rows // TILE, TILE, width), BF16),
            pltpu.SemaphoreType.DMA((5 + 2 * (rows // TILE),)),
        ],
        compiler_params=pltpu.CompilerParams(vmem_limit_bytes=63 * MIB),
        name="finish",
    )(output, grad, weights, bias)


def shards(groups, devs, features, weight_self, weight_neigh, bias, cotangent, hub_rows,
           halo_send, block_src, block_tgt, block_count, block_vals):
    rows, width = features.shape
    scale = 1.0 / math.sqrt(rows * groups * devs)
    block = block_vals.shape[-1]
    results = layer_call(
        hub_rows, block_count, block_src[0], block_tgt[0],
        halo_send[0, 0], features.reshape(-1, block, width), block_vals[0, 0],
        weight_self, weight_neigh, bias[None], cotangent, groups, devs, hub_rows.shape[0],
    )
    output, grad, grad_self, grad_neigh, grad_bias = finish_call(scale, *results)
    return output, grad, grad_self, grad_neigh, grad_bias.reshape(width)


def solution(mesh):
    groups, devs = mesh.shape["group"], mesh.shape["dev"]
    return jax.shard_map(
        functools.partial(shards, groups, devs),
        mesh=mesh,
        in_specs=(
            P(("group", "dev"), None),
            P(),
            P(),
            P(),
            P(("group", "dev"), None),
            P(("group", "dev")),
            P("group", "dev", None, None),
            P("group", "dev", None),
            P("group", "dev", None),
            P("group", "dev"),
            P("group", "dev", None, None, None),
        ),
        out_specs=(P(("group", "dev"), None), P(("group", "dev"), None), P(), P(), P()),
        check_vma=False,
    )
```
